32 devices in a mesh: dp: 4 (over z), seq: 4 (over y, x), mp: 2 (over core).
Axes of the slice: x: 2, y: 2, z: 4, core: 2. Of those that a mesh axis runs over, the one named last changes fastest.
Arguments:
- inputs: bfloat16 [8, 4096, 768], P('dp', 'seq'), may hold values from -8 to 8
- cotangent: bfloat16 [8, 4096, 768], P('dp', 'seq'), may hold values from -8 to 8
- padding: int32 [8, 4096], P('dp'), may hold values from 0 to 1, as said below
- documents: int32 [8, 4096], P('dp'), may hold values from 0 to 8, as said below
- w_query: bfloat16 [768, 768], P(None, 'mp'), may hold values from -0.75 to 0.75
- w_key: bfloat16 [768, 768], P(None, 'mp'), may hold values from -0.75 to 0.75
- w_value: bfloat16 [768, 768], P(None, 'mp'), may hold values from -0.4375 to 0.4375
- w_out: bfloat16 [768, 768], P('mp'), may hold values from -0.21875 to 0.21875
- w_up: bfloat16 [768, 3072], P(None, 'mp'), may hold values from -0.21875 to 0.21875
- w_down: bfloat16 [3072, 768], P('mp'), may hold values from -0.109375 to 0.109375
- conv_taps: float32 [12, 33], P('mp'), may hold values from -2.5 to 2.5
- gain_attn: float32 [768], replicated, may hold values from 0.5 to 1.5
- shift_attn: float32 [768], replicated, may hold values from -1.25 to 1.25
- gain_ffn: float32 [768], replicated, may hold values from 0.5 to 1.5
- shift_ffn: float32 [768], replicated, may hold values from -1.25 to 1.25
Outputs:
- outputs: bfloat16 [8, 4096, 768], P('dp', 'seq')
- grad_inputs: bfloat16 [8, 4096, 768], P('dp', 'seq', 'mp')
- grad_query: float32 [768, 768], P(('dp', 'seq'), 'mp')
- grad_key: float32 [768, 768], P(('dp', 'seq'), 'mp')
- grad_value: float32 [768, 768], P(('dp', 'seq'), 'mp')
- grad_out: float32 [768, 768], P('mp', ('dp', 'seq'))
- grad_up: float32 [768, 3072], P(('dp', 'seq'), 'mp')
- grad_down: float32 [3072, 768], P('mp', ('dp', 'seq'))
- grad_taps: float32 [12, 33], P('mp')
- grad_gain_attn: float32 [768], replicated
- grad_shift_attn: float32 [768], replicated
- grad_gain_ffn: float32 [768], replicated
- grad_shift_ffn: float32 [768], replicated
- row_rms: float32 [8, 3], P('dp')
The draws below stay inside these ranges and needn't reach their ends.
Inputs may be any that keep to these rules, and one draw needn't show every extreme that they name: `padding`: each row is 1 on a leading run of at least 3072 positions and 0 after it. `documents`: never falls along a row; position 0 of every row is in document 0; positions 512 to 3583 of a row lie in one document.
All inputs are finite; a program needn't handle non-finite values.
Results may differ from the reference program's by a relative error of at most 0.035.
Values may be sent and summed in bfloat16 or wider, within the bound.
A program may use at most 192 MiB of HBM per device.

```python
from functools import partial
import jax
import jax.numpy as jnp
from jax import lax

D = 768
H = 12
F = 3072
M = 64
KW = 33
ITERS = 6
LEN = 4096
ROWS = 8
SEQ_TOK = 1024


def draw_padding(key, part):
    key = jax.random.fold_in(key, 11)
    pad_len = jax.random.randint(key, (ROWS, 1), 0, LEN // 4 + 1)
    places = jnp.arange(LEN, dtype=jnp.int32)[None, :]
    return (places < LEN - pad_len).astype(jnp.int32)


def draw_documents(key, part):
    key = jax.random.fold_in(key, 23)
    key_a, key_b, key_c, key_d = jax.random.split(key, 4)
    first = jax.random.randint(key_a, (ROWS, 1), 1, SEQ_TOK // 2 + 1)
    last = jax.random.randint(key_b, (ROWS, 1), LEN - SEQ_TOK // 2, LEN)
    early = jax.random.randint(key_c, (ROWS, 3), 1, SEQ_TOK // 2)
    late = jax.random.randint(key_d, (ROWS, 3), LEN - SEQ_TOK // 2, LEN)
    bounds = jnp.concatenate([first, early, last, late], axis=1)
    places = jnp.arange(LEN, dtype=jnp.int32)[None, :, None]
    return jnp.sum((places >= bounds[:, None, :]).astype(jnp.int32), axis=2).astype(jnp.int32)


def raised(entries, key, source, target, blocks, factor):
    def block_of(dim):
        return (jnp.arange(entries.shape[dim]) // (entries.shape[dim] // blocks)).reshape((-1,) + (1,) * (entries.ndim - 1 - dim))

    first = jax.random.permutation(key, blocks)[block_of(target)]
    second = (block_of(target) + blocks // 2) % blocks
    return jnp.where((block_of(source) == first) | (block_of(source) == second), factor * entries, entries)


def steps_of(own_key, extent, cuts, low, largest):
    def one(axis_at, parts):
        draws = jax.random.uniform(jax.random.fold_in(jax.random.fold_in(own_key, 6), axis_at), (parts,), jnp.float32, low / len(cuts), largest / len(cuts))
        return jnp.repeat(jnp.exp(draws), extent[axis_at] // parts).reshape((-1,) + (1,) * (len(extent) - axis_at - 1))

    level = one(*cuts[0])
    for cut in cuts[1:]:
        level = level * one(*cut)
    return level


def scatter_about(key, dims, deviation, most, cuts=(), kind=jnp.bfloat16):
    array = jax.random.normal(key, dims, jnp.float32) * deviation
    if len(cuts) > 0:
        array = steps_of(key, dims, cuts, -0.22, 0.18) * array
    return jnp.clip(array, min=-most, max=most).astype(kind)


def heavy_noise(key, extent, scale, most, cuts, heavy, kind=jnp.bfloat16):
    array = scale * jax.random.normal(key, extent, jnp.float32)
    if cuts:
        array = array * steps_of(key, extent, cuts, -0.22, 0.18)
    return jnp.clip(raised(array, jax.random.fold_in(key, 3), *heavy), -most, most).astype(kind)


def setup_inputs(seed: int = 0) -> dict:
    key_of = jax.random.split(jax.random.key(seed), 16)
    inputs = heavy_noise(key_of[0], (ROWS, LEN, D), 1.0, 8.0, ((0, 4), (1, 4)), (0, 2, 4, 2.0))
    cotangent = heavy_noise(key_of[1], (ROWS, LEN, D), 1.0, 8.0, ((0, 4), (1, 4)), (1, 2, 4, 2.0))
    padding = draw_padding(jax.random.fold_in(key_of[15], 71), 0)
    documents = draw_documents(jax.random.fold_in(key_of[15], 71), 0)
    w_query = scatter_about(key_of[4], (D, D), (D // 12) ** -0.5, 0.75, ((1, 2),))
    w_key = scatter_about(key_of[5], (D, D), (D // 12) ** -0.5, 0.75, ((1, 2),))
    w_value = scatter_about(key_of[6], (D, D), (D // 4) ** -0.5, 0.4375, ((1, 2),))
    w_out = scatter_about(key_of[7], (D, D), D ** -0.5, 0.21875, ((0, 2),))
    w_up = scatter_about(key_of[8], (D, F), D ** -0.5, 0.21875, ((1, 2),))
    w_down = scatter_about(key_of[9], (F, D), F ** -0.5, 0.109375, ((0, 2),))
    conv_taps = scatter_about(key_of[10], (H, KW), (2.4 / KW ** 0.5), 2.5, ((0, 2),), jnp.float32)
    gain_attn = jnp.clip(1.0 + 0.1 * jax.random.normal(key_of[11], (D,), jnp.float32), 0.5, 1.5)
    shift_attn = scatter_about(key_of[12], (D,), 0.2, 1.25, (), jnp.float32)
    gain_ffn = jnp.clip(1.0 + 0.1 * jax.random.normal(key_of[13], (D,), jnp.float32), 0.5, 1.5)
    shift_ffn = scatter_about(key_of[14], (D,), 0.2, 1.25, (), jnp.float32)
    return dict(inputs=inputs, cotangent=cotangent, padding=padding, documents=documents, w_query=w_query, w_key=w_key, w_value=w_value, w_out=w_out, w_up=w_up, w_down=w_down, conv_taps=conv_taps, gain_attn=gain_attn, shift_attn=shift_attn, gain_ffn=gain_ffn, shift_ffn=shift_ffn)


highest = lax.Precision.HIGHEST

@jax.custom_vjp
def low(v):
    return lax.optimization_barrier(v.astype(jnp.bfloat16)).astype(jnp.float32)

@jax.custom_vjp
def low_back(v):
    return v

def low_keep(v):
    return (low(v), None)

def low_pass(kept, grad):
    return (grad,)

def back_keep(v):
    return (v, None)

def back_low(kept, grad):
    return (low(grad),)
low.defvjp(low_keep, low_pass)
low_back.defvjp(back_keep, back_low)

def pseudo_inverse(kernel):
    size = kernel.shape[-1]
    ident = jnp.eye(size, dtype=kernel.dtype)
    scale = 1.0 / lax.optimization_barrier(jnp.max(lax.optimization_barrier(jnp.sum(kernel, axis=-2)), axis=-1))
    approx = jnp.swapaxes(kernel, -1, -2) * scale[..., None, None]
    for section in range(ITERS):
        product = jnp.matmul(kernel, approx, precision=highest)
        inner = 7.0 * ident - product
        inner = 15.0 * ident - jnp.matmul(product, inner, precision=highest)
        inner = 13.0 * ident - jnp.matmul(product, inner, precision=highest)
        approx = 0.25 * jnp.matmul(approx, inner, precision=highest)
    return approx

def norm_layer(hidden, gain, shift):
    centre = hidden - lax.optimization_barrier(jnp.mean(hidden, axis=-1, keepdims=True))
    spread = lax.optimization_barrier(jnp.mean(centre * centre, axis=-1, keepdims=True))
    return centre * lax.rsqrt(spread + 1e-05) * gain + shift

def layer_row(keep, documents, inputs, w_query, w_key, w_value, w_out, w_up, w_down, conv_taps, gain_attn, shift_attn, gain_ffn, shift_ffn):
    seq_len, model_width = inputs.shape
    head_count, tap_count = conv_taps.shape
    head_dim = model_width // head_count
    half_taps = tap_count // 2
    seg_len = seq_len // M
    queries = low(low_back(jnp.dot(inputs, w_query, precision=highest)))
    key_rows = low(low_back(jnp.dot(inputs, w_key, precision=highest)))
    value_rows = low(low_back(jnp.dot(inputs, w_value, precision=highest))) * keep[:, None]
    counts = lax.optimization_barrier(jnp.sum(keep.reshape(M, seg_len), axis=1))
    denom = jnp.maximum(counts, 1.0)[:, None]
    query_marks = low(lax.optimization_barrier(jnp.sum((queries * keep[:, None]).reshape(M, seg_len, model_width), axis=1)) / denom)
    key_marks = low(lax.optimization_barrier(jnp.sum((key_rows * keep[:, None]).reshape(M, seg_len, model_width), axis=1)) / denom)
    q_heads = queries.reshape(seq_len, head_count, head_dim)
    k_heads = key_rows.reshape(seq_len, head_count, head_dim)
    v_heads = value_rows.reshape(seq_len, head_count, head_dim)
    q_marks = query_marks.reshape(M, head_count, head_dim)
    k_marks = key_marks.reshape(M, head_count, head_dim)
    score_one = low_back(jnp.einsum('the,mhe->thm', q_heads, k_marks, precision=highest) * 0.125)
    kernel_one = low(jax.nn.softmax(score_one, axis=-1))
    score_two = jnp.einsum('ahe,bhe->hab', q_marks, k_marks, precision=highest) * 0.125
    kernel_two = jax.nn.softmax(score_two, axis=-1)
    inverse = pseudo_inverse(kernel_two)
    score_three = low_back(jnp.einsum('mhe,the->hmt', q_marks, k_heads, precision=highest) * 0.125)
    masked = score_three - (1.0 - keep)[None, None, :] * 1000000000.0
    top = lax.optimization_barrier(jnp.max(masked, axis=-1))
    exp_terms = jnp.exp(masked - top[..., None])
    totals = lax.optimization_barrier(jnp.sum(exp_terms, axis=-1))
    mixed = low_back(jnp.einsum('hmt,the->hme', low(exp_terms), v_heads, precision=highest))
    landmark_values = mixed / totals[..., None]
    context_mix = low(jnp.einsum('hab,hbe->hae', inverse, landmark_values, precision=highest))
    attended = jnp.einsum('thm,hme->the', kernel_one, context_mix, precision=highest).reshape(seq_len, model_width)
    padded_values = jnp.pad(value_rows, ((half_taps, half_taps), (0, 0)))
    padded_docs = jnp.pad(documents, (half_taps, half_taps), constant_values=-1)
    tap_weights = jnp.repeat(conv_taps, head_dim, axis=0)
    conv_sum = jnp.zeros_like(value_rows)
    for offset in range(tap_count):
        same_doc = (padded_docs[offset:offset + seq_len] == documents).astype(jnp.float32)
        conv_sum = conv_sum + tap_weights[:, offset][None, :] * padded_values[offset:offset + seq_len] * same_doc[:, None]
    context = low(low_back(attended + conv_sum))
    branch_attn = low_back(jnp.dot(context, w_out, precision=highest))
    normed = norm_layer(inputs + branch_attn, gain_attn, shift_attn)
    up_rows = low_back(jnp.dot(low(normed), w_up, precision=highest))
    activated = low(jax.nn.gelu(up_rows, approximate=False))
    branch_ffn = low_back(jnp.dot(activated, w_down, precision=highest))
    result = norm_layer(normed + branch_ffn, gain_ffn, shift_ffn)
    squares = jnp.stack([jnp.sum(keep[:, None] * inputs * inputs), jnp.sum(keep[:, None] * branch_attn * branch_attn), jnp.sum(keep[:, None] * branch_ffn * branch_ffn)])
    return (result, squares)

def reference(inputs, cotangent, padding, documents, w_query, w_key, w_value, w_out, w_up, w_down, conv_taps, gain_attn, shift_attn, gain_ffn, shift_ffn):
    weights = tuple((item.astype(jnp.float32) for item in (w_query, w_key, w_value, w_out, w_up, w_down, conv_taps, gain_attn, shift_attn, gain_ffn, shift_ffn)))
    start_sums = tuple((jnp.zeros(item.shape, jnp.float32) for item in weights))

    def one_row(grad_sums, row_data):
        x_row, cot_row, pad_row, doc_row = row_data
        keep = pad_row.astype(jnp.float32)
        row_layer = partial(layer_row, keep, doc_row)
        result, pullback, squares = jax.vjp(row_layer, x_row.astype(jnp.float32), *weights, has_aux=True)
        pulled = pullback(cot_row.astype(jnp.float32))
        new_sums = tuple((total + part for total, part in zip(grad_sums, pulled[1:])))
        rms = jnp.sqrt(squares / (jnp.sum(keep) * x_row.shape[1]) + 1e-06)
        return (new_sums, (result.astype(jnp.bfloat16), pulled[0].astype(jnp.bfloat16), rms))
    grad_sums, (outputs, grad_inputs, row_rms) = lax.scan(one_row, start_sums, (inputs, cotangent, padding, documents))
    return (outputs, grad_inputs, grad_sums[0], grad_sums[1], grad_sums[2], grad_sums[3], grad_sums[4], grad_sums[5], grad_sums[6], grad_sums[7], grad_sums[8], grad_sums[9], grad_sums[10], row_rms)
```

```python
import functools

import jax
import jax.numpy as jnp
from jax import lax
from jax.experimental import pallas as pl
from jax.experimental.pallas import tpu as pltpu
from jax.sharding import PartitionSpec as P

M = 64
ITERS = 6
LEN = 4096
QUAD = 256
MESH = pl.DeviceIdType.MESH
F32 = jnp.float32
BF = jnp.bfloat16
EPS = 1e-05


def nn(a, b):
    return lax.dot_general(a, b, (((1,), (0,)), ((), ())), preferred_element_type=F32)


def nt(a, b):
    return lax.dot_general(a, b, (((1,), (1,)), ((), ())), preferred_element_type=F32)


def tn(a, b):
    return lax.dot_general(a, b, (((0,), (0,)), ((), ())), preferred_element_type=F32)


def split(a):
    high = a.astype(BF)
    return high, (a - high.astype(F32)).astype(BF)


def three(dot, a, b):
    ah, al = split(a)
    bh, bl = split(b)
    return dot(ah, bh) + (dot(ah, bl) + dot(al, bh))


def iota(shape, dim):
    return lax.broadcasted_iota(jnp.int32, shape, dim)


def block_mask():
    return iota((QUAD, QUAD), 0) // M == iota((QUAD, QUAD), 1) // M


def spread_blocks(x, mask):
    return jnp.where(mask, jnp.concatenate([x] * (QUAD // M), axis=0), jnp.zeros((), x.dtype))


def gather_blocks(y):
    lane = iota((M, QUAD), 1) // M
    out = jnp.zeros((M, QUAD), y.dtype)
    for h in range(QUAD // M):
        out = out + jnp.where(lane == h, y[h * M : (h + 1) * M], 0.0)
    return out


def params(limit=56, **kw):
    return pltpu.CompilerParams(vmem_limit_bytes=limit * 1024 * 1024, **kw)


def whole(shape):
    nd = len(shape)
    return pl.BlockSpec(shape, lambda *a: (0,) * nd)


def sds(shape, dtype):
    return jax.ShapeDtypeStruct(shape, dtype)


def valid_count(pad_ref, idx_ref):
    row = pad_ref[pl.ds(idx_ref[0], 1), :].astype(F32)
    return jnp.sum(row, axis=1, keepdims=True).astype(jnp.int32)


def project_kernel(
    idx, x_ref, pad_ref, q0, q1, k0, k1, v0, v1, q_ref, k_ref, v_ref, pack_ref, sums, *, tok
):
    step = pl.program_id(0)
    rows = x_ref.shape[1]
    half = q0.shape[1]
    x = x_ref[0]
    keep_n = valid_count(pad_ref, idx) - idx[1] * tok - step * rows
    keep = (iota((rows, 1), 0) < keep_n).astype(F32)
    marks = rows // M
    count = jnp.maximum(jnp.sum(keep.reshape(marks, M, 1), axis=1), 1.0)

    def one(w0, w1, out, place):
        for part, w in ((0, w0), (1, w1)):
            val = nn(x, w[...]).astype(BF)
            cols = pl.ds(part * half, half)
            if place is None:
                val = (val.astype(F32) * keep).astype(BF)
            out[:, cols] = val
            if place is not None:
                wide = (val.astype(F32) * keep).reshape(marks, M, half)
                sums[pl.ds(pl.multiple_of(place * (tok // M) + step * marks, marks), marks), cols] = (
                    jnp.sum(wide, axis=1) / count
                )

    one(q0, q1, q_ref, 0)
    one(k0, k1, k_ref, 1)
    one(v0, v1, v_ref, None)
    lm = tok // M

    @pl.when(step == 0)
    def _():
        pack_ref[2 * lm : 2 * lm + 16, :] = v_ref[0:16, :]

    @pl.when(step == pl.num_programs(0) - 1)
    def _():
        pack_ref[0 : 2 * lm, :] = sums[...].astype(BF)
        pack_ref[2 * lm + 16 : 2 * lm + 32, :] = v_ref[rows - 16 : rows, :]


def project(idx, inputs, padding, weights, tok):
    d = inputs.shape[2]
    half = weights[0].shape[1]
    rows = 512
    lm = tok // M
    cost = pl.CostEstimate(flops=6 * tok * d * d, bytes_accessed=12 * tok * d, transcendentals=0)
    return pl.pallas_call(
        functools.partial(project_kernel, tok=tok),
        grid_spec=pltpu.PrefetchScalarGridSpec(
            num_scalar_prefetch=1,
            grid=(tok // rows,),
            in_specs=[
                pl.BlockSpec((1, rows, d), lambda i, s: (s[0], i, 0)),
                whole(padding.shape),
            ]
            + [whole((d, half))] * 6,
            out_specs=[pl.BlockSpec((rows, d), lambda i, s: (i, 0))] * 3
            + [whole((2 * lm + 32, d))],
            scratch_shapes=[pltpu.VMEM((2 * lm, d), F32)],
        ),
        out_shape=[sds((tok, d), BF)] * 3 + [sds((2 * lm + 32, d), BF)],
        compiler_params=params(),
        cost_estimate=cost,
        name="project",
    )(idx, inputs, padding, *weights)


def enter(n):
    me = lax.axis_index("seq")
    barrier = pltpu.get_barrier_semaphore()
    for p in range(1, n):
        pl.semaphore_signal(
            barrier, inc=1, device_id={"seq": lax.rem(me + p, n)}, device_id_type=MESH
        )
    pl.semaphore_wait(barrier, n - 1)
    return me


def gather_kernel(*refs, n, count, edges):
    ins = refs[:count]
    outs = refs[count : 2 * count]
    at = 2 * count
    if edges:
        edge_in, edge_out = refs[at], refs[at + 1]
        at += 2
    send, recv, local = refs[at : at + 3]
    me = enter(n)
    copies = []
    slot = 0
    for src, dst in zip(ins, outs):
        for p in range(1, n):
            copies.append(
                pltpu.make_async_remote_copy(
                    src_ref=src,
                    dst_ref=dst.at[me],
                    send_sem=send.at[slot],
                    recv_sem=recv.at[slot],
                    device_id={"seq": lax.rem(me + p, n)},
                    device_id_type=MESH,
                )
            )
            slot += 1
    if edges:
        for side, p in ((0, 1), (1, n - 1)):
            first = 16 if side == 0 else 0
            copies.append(
                pltpu.make_async_remote_copy(
                    src_ref=edge_in.at[pl.ds(first, 16)],
                    dst_ref=edge_out.at[pl.ds(side * 16, 16)],
                    send_sem=send.at[slot],
                    recv_sem=recv.at[slot],
                    device_id={"seq": lax.rem(me + p, n)},
                    device_id_type=MESH,
                )
            )
            slot += 1
    for c in copies:
        c.start()
    locals_ = [
        pltpu.make_async_copy(src, dst.at[me], local.at[i])
        for i, (src, dst) in enumerate(zip(ins, outs))
    ]
    for c in locals_:
        c.start()
    for c in locals_:
        c.wait()
    for c in copies:
        c.wait()


def gather_seq(n, arrays, edge, cid):
    count = len(arrays)
    total = count * (n - 1) + (2 if edge is not None else 0)
    outs = [sds((n,) + a.shape, a.dtype) for a in arrays]
    args = list(arrays)
    if edge is not None:
        outs.append(sds(edge.shape, edge.dtype))
        args.append(edge)

    def body(*refs):
        ins = refs[: len(args)]
        rest = refs[len(args) :]
        o = rest[: len(outs)]
        sems = rest[len(outs) :]
        if edge is not None:
            order = ins[:count] + o[:count] + (ins[count], o[count]) + sems
        else:
            order = ins + o + sems
        gather_kernel(*order, n=n, count=count, edges=edge is not None)

    return pl.pallas_call(
        body,
        in_specs=[pl.BlockSpec(memory_space=pl.ANY)] * len(args),
        out_specs=[pl.BlockSpec(memory_space=pl.ANY)] * len(outs),
        out_shape=outs,
        scratch_shapes=[
            pltpu.SemaphoreType.DMA((total,)),
            pltpu.SemaphoreType.DMA((total,)),
            pltpu.SemaphoreType.DMA((count,)),
        ],
        compiler_params=params(8, collective_id=cid, has_side_effects=True),
        name="gather%d" % cid,
    )(*args)


def scatter_seq(n, array, cid):
    def body(src, dst, send, recv, local):
        me = enter(n)
        copies = []
        for p in range(1, n):
            to = lax.rem(me + p, n)
            copies.append(
                pltpu.make_async_remote_copy(
                    src_ref=src.at[to],
                    dst_ref=dst.at[me],
                    send_sem=send.at[p],
                    recv_sem=recv.at[p],
                    device_id={"seq": to},
                    device_id_type=MESH,
                )
            )
        for c in copies:
            c.start()
        own = pltpu.make_async_copy(src.at[me], dst.at[me], local)
        own.start()
        own.wait()
        for c in copies:
            c.wait()

    return pl.pallas_call(
        body,
        in_specs=[pl.BlockSpec(memory_space=pl.ANY)],
        out_specs=pl.BlockSpec(memory_space=pl.ANY),
        out_shape=sds(array.shape, array.dtype),
        scratch_shapes=[
            pltpu.SemaphoreType.DMA((n,)),
            pltpu.SemaphoreType.DMA((n,)),
            pltpu.SemaphoreType.DMA,
        ],
        compiler_params=params(8, collective_id=cid, has_side_effects=True),
        name="scatter%d" % cid,
    )(array)


def score_kernel(idx, q_ref, k_ref, v_ref, marks_ref, pad_ref, k1_ref, e_ref, mix_ref, stat_ref, *, tok):
    quad = pl.program_id(0)
    n = marks_ref.shape[0]
    lm = tok // M
    mask = block_mask()
    qm = jnp.concatenate([marks_ref[i, 0:lm, :] for i in range(n)], axis=0)
    km = jnp.concatenate([marks_ref[i, lm : 2 * lm, :] for i in range(n)], axis=0)
    s1 = nt(spread_blocks(km, mask), q_ref[...]) * 0.125
    s1 = s1.reshape(QUAD // M, M, tok)
    e1 = jnp.exp(s1 - jnp.max(s1, axis=1, keepdims=True))
    k1 = e1 / jnp.sum(e1, axis=1, keepdims=True)
    k1_ref[...] = k1.reshape(QUAD, tok).astype(BF)
    keep_n = valid_count(pad_ref, idx) - idx[1] * tok
    minus = jnp.where(iota((1, tok), 1) < keep_n, 0.0, 1000000000.0)
    s3 = nt(spread_blocks(qm, mask), k_ref[...]) * 0.125 - minus
    top = jnp.max(s3, axis=1, keepdims=True)
    e3 = jnp.exp(s3 - top)
    total = jnp.sum(e3, axis=1, keepdims=True)
    e3 = e3.astype(BF)
    e_ref[...] = e3
    mix_ref[...] = gather_blocks(nn(e3, v_ref[...])).astype(BF)
    lane = iota((M, 128), 1)
    stat = jnp.where(quad == 0, jnp.zeros((M, 128), F32), stat_ref[...])
    for h in range(QUAD // M):
        stat = jnp.where(lane == quad * (QUAD // M) + h, top[h * M : (h + 1) * M], stat)
        stat = jnp.where(lane == 64 + quad * (QUAD // M) + h, total[h * M : (h + 1) * M], stat)
    stat_ref[...] = stat


def scores(idx, q, k, v, marks, padding):
    tok, d = q.shape
    n = marks.shape[0]
    lane = lambda i, s: (0, i)
    cost = pl.CostEstimate(
        flops=6 * tok * d * QUAD, bytes_accessed=10 * tok * d, transcendentals=2 * tok * d
    )
    return pl.pallas_call(
        functools.partial(score_kernel, tok=tok),
        grid_spec=pltpu.PrefetchScalarGridSpec(
            num_scalar_prefetch=1,
            grid=(d // QUAD,),
            in_specs=[pl.BlockSpec((tok, QUAD), lane)] * 3
            + [pl.BlockSpec((n, marks.shape[1], QUAD), lambda i, s: (0, 0, i)), whole(padding.shape)],
            out_specs=[pl.BlockSpec((QUAD, tok), lambda i, s: (i, 0))] * 2
            + [pl.BlockSpec((M, QUAD), lane), whole((M, 128))],
        ),
        out_shape=[sds((d, tok), BF), sds((d, tok), BF), sds((M, d), BF), sds((M, 128), F32)],
        compiler_params=params(),
        cost_estimate=cost,
        name="scores",
    )(idx, q, k, v, marks, padding)


def pinv_kernel(idx, marks_ref, k2_ref, inv_ref, save_ref, *, lm):
    n = marks_ref.shape[0]
    d = marks_ref.shape[2]
    quads = d // QUAD
    mask = block_mask()
    ident = (iota((QUAD, QUAD), 0) == iota((QUAD, QUAD), 1)).astype(F32)
    qm = jnp.concatenate([marks_ref[i, 0:lm, :] for i in range(n)], axis=0)
    km = jnp.concatenate([marks_ref[i, lm : 2 * lm, :] for i in range(n)], axis=0)
    kernel, z = [], []
    for c in range(quads):
        cols = slice(c * QUAD, (c + 1) * QUAD)
        s2 = nt(spread_blocks(qm[:, cols], mask), spread_blocks(km[:, cols], mask)) * 0.125
        s2 = jnp.where(mask, s2, -1e30)
        e2 = jnp.exp(s2 - jnp.max(s2, axis=1, keepdims=True))
        e2 = e2 / jnp.sum(e2, axis=1, keepdims=True)
        kernel.append(e2)
        sums = jnp.sum(e2, axis=0, keepdims=True)
        lane = iota((1, QUAD), 1) // M
        scale = jnp.zeros((1, QUAD), F32)
        for h in range(QUAD // M):
            best = jnp.max(jnp.where(lane == h, sums, 0.0), axis=1, keepdims=True)
            scale = jnp.where(lane == h, 1.0 / best, scale)
        z.append(e2.T * scale)
        k2_ref[:, cols] = gather_blocks(e2)
    sel = jnp.minimum(idx[1], quads - 1)

    def keep(it, kind, vals):
        if kind is None:
            return
        for c in range(quads):

            @pl.when(sel == c)
            def _():
                save_ref[it, kind] = vals[c].astype(BF)

    ksp = [split(a) for a in kernel]

    def mul(a, b):
        return nn(a[0], b[0]) + (nn(a[0], b[1]) + nn(a[1], b[0]))

    for it in range(ITERS):
        zs = [split(a) for a in z]
        p = [mul(a, b) for a, b in zip(ksp, zs)]
        ps = [split(a) for a in p]
        i2 = [15.0 * ident - mul(a, split(7.0 * ident - b)) for a, b in zip(ps, p)]
        i3 = [13.0 * ident - mul(a, split(b)) for a, b in zip(ps, i2)]
        keep(it, 0, z)
        keep(it, 1, p)
        keep(it, 2, i2)
        keep(it, 3, i3)
        z = [0.25 * mul(a, split(b)) for a, b in zip(zs, i3)]
    for c in range(quads):
        inv_ref[:, c * QUAD : (c + 1) * QUAD] = gather_blocks(z[c])


def pinv(idx, marks, lm):
    d = marks.shape[2]
    shape = (ITERS, 4, QUAD, QUAD)
    cost = pl.CostEstimate(
        flops=24 * 3 * 3 * 2 * QUAD**3, bytes_accessed=4 * 10**6, transcendentals=0
    )
    return pl.pallas_call(
        functools.partial(pinv_kernel, lm=lm),
        grid_spec=pltpu.PrefetchScalarGridSpec(
            num_scalar_prefetch=1,
            grid=(1,),
            in_specs=[whole(marks.shape)],
            out_specs=[whole((M, d)), whole((M, d)), whole(shape)],
        ),
        out_shape=[sds((M, d), F32), sds((M, d), F32), sds(shape, BF)],
        compiler_params=params(),
        cost_estimate=cost,
        name="pinv",
    )(idx, marks)


def per_head(stat, base, c):
    lane = iota((M, QUAD), 1) // M
    out = jnp.zeros((M, QUAD), F32)
    for h in range(QUAD // M):
        at = base + c * (QUAD // M) + h
        out = jnp.where(lane == h, stat[:, at : at + 1], out)
    return out


def combine_kernel(idx, mix_ref, stat_ref, inv_ref, cm_ref, lv_ref, gst_ref):
    n = mix_ref.shape[0]
    d = mix_ref.shape[2]
    lane = iota((M, 128), 1)
    top = stat_ref[0]
    for i in range(1, n):
        top = jnp.maximum(top, stat_ref[i])
    top = jnp.where(lane < 64, top, 0.0)
    total = jnp.zeros((M, 128), F32)
    scales = []
    for i in range(n):
        st = stat_ref[i]
        sc = jnp.where(lane < 64, jnp.exp(st - top), 0.0)
        scales.append(sc)
        total = total + sc * pltpu.roll(st, 64, 1)
    own = jnp.zeros((M, 128), F32)
    for i in range(n):
        own = jnp.where(idx[1] == i, scales[i], own)
    gst_ref[...] = jnp.where(lane < 64, own, pltpu.roll(total, 64, 1))
    mask = block_mask()
    for c in range(d // QUAD):
        cols = slice(c * QUAD, (c + 1) * QUAD)
        mixed = jnp.zeros((M, QUAD), F32)
        for i in range(n):
            mixed = mixed + per_head(scales[i], 0, c) * mix_ref[i, :, cols].astype(F32)
        lv = mixed / per_head(total, 0, c)
        lv_ref[:, cols] = lv
        cm = three(nn, spread_blocks(inv_ref[:, cols], mask), spread_blocks(lv, mask))
        cm_ref[:, cols] = gather_blocks(cm).astype(BF)


def combine(idx, mix, stat, inv):
    d = mix.shape[2]
    return pl.pallas_call(
        combine_kernel,
        grid_spec=pltpu.PrefetchScalarGridSpec(
            num_scalar_prefetch=1,
            grid=(1,),
            in_specs=[whole(mix.shape), whole(stat.shape), whole(inv.shape)],
            out_specs=[whole((M, d)), whole((M, d)), whole((M, 128))],
        ),
        out_shape=[sds((M, d), BF), sds((M, d), F32), sds((M, 128), F32)],
        compiler_params=params(),
        name="combine",
    )(idx, mix, stat, inv)


def doc_bounds(doc_ref, idx):
    row = doc_ref[pl.ds(idx[0], 1), :]
    return [
        jnp.sum((row < j).astype(F32), axis=1, keepdims=True).astype(jnp.int32)
        for j in range(1, 9)
    ]


def docs_at(place, bounds, length):
    doc = jnp.zeros(place.shape, jnp.int32)
    for b in bounds:
        doc = doc + (place >= b).astype(jnp.int32)
    return jnp.where((place >= 0) & (place < length), doc, -1)


def fill_bands(taps_ref, band_ref, half, flip):
    heads, width = taps_ref.shape[0], 2 * half + 1
    rows, span = band_ref.shape[1], band_ref.shape[2]
    gap = iota((rows, span), 1) - iota((rows, span), 0) - 64
    if flip:
        gap = -gap
    for h in range(heads):
        acc = jnp.zeros((rows, span), F32)
        line = taps_ref[h : h + 1, :]
        for o in range(width):
            acc = jnp.where(gap == o - half, line[:, o : o + 1], acc)
        band_ref[h] = acc.astype(BF)


def banded(band_ref, window, same, col0):
    lane = iota((band_ref.shape[1], 128), 1)
    first = nn(band_ref[col0] * same, window)
    second = nn(band_ref[col0 + 1] * same, window)
    return jnp.where(lane < 64, first, second)


def fill_halo(ext, body, edge_ref, tok):
    ext[0:48, :] = jnp.zeros((48, ext.shape[1]), BF)
    ext[48:64, :] = edge_ref[0:16, :]
    ext[64 : 64 + tok, :] = body[...]
    ext[64 + tok : 80 + tok, :] = edge_ref[16:32, :]
    ext[80 + tok :, :] = jnp.zeros((48, ext.shape[1]), BF)


def erf_parts(u):
    a = jnp.abs(u) * 0.7071067811865476
    e = jnp.exp(-0.5 * u * u)
    t = 1.0 / (1.0 + 0.3275911 * a)
    poly = t * (
        0.254829592
        + t * (-0.284496736 + t * (1.421413741 + t * (-1.453152027 + t * 1.061405429)))
    )
    tail = 0.5 * poly * e
    cdf = jnp.where(u < 0.0, tail, 1.0 - tail)
    return cdf, e * 0.3989422804014327


def norm_stats(h):
    mean = jnp.mean(h, axis=-1, keepdims=True)
    centre = h - mean
    rstd = lax.rsqrt(jnp.mean(centre * centre, axis=-1, keepdims=True) + EPS)
    return centre * rstd, rstd


def norm_back(g, hat, rstd):
    return rstd * (
        g
        - jnp.mean(g, axis=-1, keepdims=True)
        - hat * jnp.mean(g * hat, axis=-1, keepdims=True)
    )


def forward_kernel(
    idx,
    x_ref,
    cot_ref,
    pad_ref,
    doc_ref,
    v_ref,
    edge_ref,
    k1_ref,
    cm_ref,
    taps_ref,
    wo0,
    wo1,
    wu0,
    wu1,
    wd0,
    wd1,
    ga_ref,
    sa_ref,
    gf_ref,
    sf_ref,
    out_ref,
    ctx_ref,
    h1_ref,
    nl_ref,
    act0,
    act1,
    gp0,
    gp1,
    gh2_ref,
    acc_ref,
    ext,
    band,
    *,
    tok,
):
    step = pl.program_id(0)
    rows, d = ctx_ref.shape
    half = wo0.shape[0]
    taps = taps_ref.shape[1]

    @pl.when(step == 0)
    def _():
        fill_halo(ext, v_ref, edge_ref, tok)
        fill_bands(taps_ref, band, taps // 2, False)
        acc_ref[...] = jnp.zeros_like(acc_ref)

    bounds = doc_bounds(doc_ref, idx)
    mask = block_mask()
    start = idx[1] * tok + step * rows
    parts = []
    for sub in range(rows // 128):
        place = start + sub * 128
        same = (
            docs_at(place + iota((128, 1), 0), bounds, LEN)
            == docs_at(place - 64 + iota((1, 256), 1), bounds, LEN)
        ).astype(BF)
        base = pl.multiple_of(step * rows + sub * 128, 128)
        cols = []
        for pair in range(d // 128):
            window = ext[pl.ds(base, 256), pair * 128 : (pair + 1) * 128]
            cols.append(banded(band, window, same, 2 * pair))
        parts.append(jnp.concatenate(cols, axis=1))
    conv = jnp.concatenate(parts, axis=0)
    for c in range(d // QUAD):
        cols = slice(c * QUAD, (c + 1) * QUAD)
        att = tn(k1_ref[cols, :], spread_blocks(cm_ref[:, cols], mask))
        ctx_ref[:, cols] = (att + conv[:, cols]).astype(BF)
    branch = nn(ctx_ref[:, :half], wo0[...]) + nn(ctx_ref[:, half:], wo1[...])
    xf = x_ref[0].astype(F32)
    h1 = xf + branch
    h1_ref[...] = h1
    hat1, _ = norm_stats(h1)
    normed = hat1 * ga_ref[...] + sa_ref[...]
    nl = normed.astype(BF)
    nl_ref[...] = nl
    ffn = jnp.zeros((rows, d), F32)
    chunk = 512
    for wu, wd, act, gp in ((wu0, wd0, act0, gp0), (wu1, wd1, act1, gp1)):
        for at in range(0, wu.shape[1], chunk):
            cols = slice(at, at + chunk)
            u = nn(nl, wu[:, cols])
            cdf, pdf = erf_parts(u)
            a = (u * cdf).astype(BF)
            act[:, cols] = a
            gp[:, cols] = (cdf + u * pdf).astype(BF)
            ffn = ffn + nn(a, wd[cols, :])
    hat2, rstd2 = norm_stats(normed + ffn)
    out_ref[...] = (hat2 * gf_ref[...] + sf_ref[...]).astype(BF)
    cot = cot_ref[0].astype(F32)
    gh2_ref[...] = norm_back(cot * gf_ref[...], hat2, rstd2)
    keep_n = valid_count(pad_ref, idx) - start
    keep = (iota((rows, 1), 0) < keep_n).astype(F32)
    acc_ref[0:1, :] += jnp.sum(cot * hat2, axis=0, keepdims=True)
    acc_ref[1:2, :] += jnp.sum(cot, axis=0, keepdims=True)
    acc_ref[2:3, :] += jnp.sum(xf * xf * keep, axis=0, keepdims=True)
    acc_ref[3:4, :] += jnp.sum(branch * branch * keep, axis=0, keepdims=True)
    acc_ref[4:5, :] += jnp.sum(ffn * ffn * keep, axis=0, keepdims=True)


def forward(idx, inputs, cot, padding, documents, v, edge, k1, cm, taps, wo, wu, wd, vecs):
    tok, d = v.shape
    rows = 256
    f2 = wu[0].shape[1]
    blk = lambda i, s: (i, 0)
    row = pl.BlockSpec((1, rows, d), lambda i, s: (s[0], i, 0))
    cost = pl.CostEstimate(
        flops=8 * tok * d * f2, bytes_accessed=60 * tok * d, transcendentals=4 * tok * f2
    )
    return pl.pallas_call(
        functools.partial(forward_kernel, tok=tok),
        grid_spec=pltpu.PrefetchScalarGridSpec(
            num_scalar_prefetch=1,
            grid=(tok // rows,),
            in_specs=[
                row,
                row,
                whole(padding.shape),
                whole(documents.shape),
                whole(v.shape),
                whole(edge.shape),
                pl.BlockSpec((d, rows), lambda i, s: (0, i)),
                whole(cm.shape),
                whole(taps.shape),
            ]
            + [whole(w.shape) for w in (*wo, *wu, *wd, *vecs)],
            out_specs=[pl.BlockSpec((rows, d), blk)] * 4
            + [pl.BlockSpec((rows, f2), blk)] * 4
            + [pl.BlockSpec((rows, d), blk), whole((8, d))],
            scratch_shapes=[
                pltpu.VMEM((tok + 128, d), BF),
                pltpu.VMEM((taps.shape[0], 128, 256), BF),
            ],
        ),
        out_shape=[sds((tok, d), BF), sds((tok, d), BF), sds((tok, d), F32), sds((tok, d), BF)]
        + [sds((tok, f2), BF)] * 4
        + [sds((tok, d), F32), sds((8, d), F32)],
        compiler_params=params(60),
        cost_estimate=cost,
        name="forward",
    )(idx, inputs, cot, padding, documents, v, edge, k1, cm, taps, *wo, *wu, *wd, *vecs)


def backward_kernel(
    idx, gh2_ref, h1_ref, gp0, gp1, wo0, wo1, wu0, wu1, wd0, wd1, ga_ref,
    du0, du1, gh1_ref, gc_ref, acc_ref,
):
    step = pl.program_id(0)
    half = wo0.shape[0]

    @pl.when(step == 0)
    def _():
        acc_ref[...] = jnp.zeros_like(acc_ref)

    gh2 = gh2_ref[...]
    low = gh2.astype(BF)
    gn = gh2
    chunk = 512
    for wu, wd, gp, du in ((wu0, wd0, gp0, du0), (wu1, wd1, gp1, du1)):
        for at in range(0, wu.shape[1], chunk):
            cols = slice(at, at + chunk)
            g = (nt(low, wd[cols, :]) * gp[:, cols].astype(F32)).astype(BF)
            du[:, cols] = g
            gn = gn + nt(g, wu[:, cols])
    hat1, rstd1 = norm_stats(h1_ref[...])
    acc_ref[0:1, :] += jnp.sum(gn * hat1, axis=0, keepdims=True)
    acc_ref[1:2, :] += jnp.sum(gn, axis=0, keepdims=True)
    gh1 = norm_back(gn * ga_ref[...], hat1, rstd1).astype(BF)
    gh1_ref[...] = gh1
    gc_ref[:, :half] = nt(gh1, wo0[...]).astype(BF)
    gc_ref[:, half:] = nt(gh1, wo1[...]).astype(BF)


def backward(idx, gh2, h1, gp, wo, wu, wd, ga):
    tok, d = h1.shape
    rows = 256
    f2 = wu[0].shape[1]
    blk = lambda i, s: (i, 0)
    cost = pl.CostEstimate(flops=8 * tok * d * f2, bytes_accessed=40 * tok * d, transcendentals=0)
    return pl.pallas_call(
        backward_kernel,
        grid_spec=pltpu.PrefetchScalarGridSpec(
            num_scalar_prefetch=1,
            grid=(tok // rows,),
            in_specs=[pl.BlockSpec((rows, d), blk)] * 2
            + [pl.BlockSpec((rows, f2), blk)] * 2
            + [whole(w.shape) for w in (*wo, *wu, *wd, ga)],
            out_specs=[pl.BlockSpec((rows, f2), blk)] * 2
            + [pl.BlockSpec((rows, d), blk)] * 2
            + [whole((8, d))],
        ),
        out_shape=[sds((tok, f2), BF)] * 2 + [sds((tok, d), BF)] * 2 + [sds((8, d), F32)],
        compiler_params=params(60),
        cost_estimate=cost,
        name="backward",
    )(idx, gh2, h1, *gp, *wo, *wu, *wd, ga)


def weight_kernel(idx, *refs, nl, nr, blocks, shape):
    lhs = refs[:nl]
    rhs = refs[nl : nl + nl * nr]
    outs = refs[nl + nl * nr : nl + nl * nr + nr]
    held = refs[-1]
    step = pl.program_id(0)
    z, sq, chunk = shape

    @pl.when(step == 0)
    def _():
        for i in range(nl):
            a = lhs[i][...] if len(lhs[i].shape) == 2 else lhs[i][0]
            tokens = a.shape[0]
            t = a.astype(BF).T
            if z == 0:
                held[:, i * tokens : (i + 1) * tokens] = t
            else:
                lhs_t = refs[-2]
                lhs_t[...] = t
                for b0 in range(2):
                    for b1 in range(2):
                        for zp in range(z):
                            place = ((b0 * 2 + b1) * z + zp) * chunk
                            src = (idx[2] ^ zp) * sq + (idx[1] ^ (b1 * 2 + b0))
                            held[place : place + chunk, i * tokens : (i + 1) * tokens] = lhs_t[
                                pl.ds(pl.multiple_of(src * chunk, chunk), chunk), :
                            ]

    tokens = held.shape[1] // nl
    for r in range(nr):
        acc = None
        for i in range(nl):
            part = nn(held[:, i * tokens : (i + 1) * tokens], rhs[i * nr + r][...])
            acc = part if acc is None else acc + part
        outs[r][...] = acc.astype(BF)


def weight_grads(idx, lhs, rhs, width, shape):
    nl, nr = len(lhs), len(rhs[0])
    tok, d = rhs[0][0].shape[0], lhs[0][0].shape[-1]
    cols = rhs[0][0].shape[1]
    blocks = cols // width
    in_specs, args = [], []
    for a, row in lhs:
        if a.ndim == 3:
            if row == 0:
                in_specs.append(pl.BlockSpec((1, tok, d), lambda j, s: (s[0], 0, 0)))
            else:
                in_specs.append(pl.BlockSpec((1, tok, d), lambda j, s: (1 - s[0], 0, 0)))
        else:
            in_specs.append(whole(a.shape))
        args.append(a)
    for group in rhs:
        for b in group:
            in_specs.append(pl.BlockSpec((tok, width), lambda j, s: (0, j)))
            args.append(b)
    cost = pl.CostEstimate(
        flops=2 * tok * d * cols * nl * nr, bytes_accessed=8 * tok * cols, transcendentals=0
    )
    return pl.pallas_call(
        functools.partial(weight_kernel, nl=nl, nr=nr, blocks=blocks, shape=shape),
        grid_spec=pltpu.PrefetchScalarGridSpec(
            num_scalar_prefetch=1,
            grid=(blocks,),
            in_specs=in_specs,
            out_specs=[pl.BlockSpec((d, width), lambda j, s: (0, j))] * nr,
            scratch_shapes=[pltpu.VMEM((d, tok), BF), pltpu.VMEM((d, tok * nl), BF)],
        ),
        out_shape=[sds((d, cols), BF)] * nr,
        compiler_params=params(60),
        cost_estimate=cost,
        name="weights",
    )(idx, *args)


def halving(seq_n, bit):
    return [(i, i ^ bit) for i in range(seq_n)]


def reduce_fast(full):
    seq_n, dp_n = lax.axis_size("seq"), lax.axis_size("dp")
    d, n = full.shape
    q = d // 4
    na = n // 2
    a, b = full[:, :na], full[:, na:]
    send_a, keep_a = a[2 * q :], a[: 2 * q]
    send_b = jnp.concatenate([b[q : 2 * q], b[3 * q :]], axis=0)
    keep_b = jnp.concatenate([b[:q], b[2 * q : 3 * q]], axis=0)
    got_a = lax.ppermute(send_a, "seq", halving(seq_n, 1))
    got_b = lax.ppermute(send_b, "seq", halving(seq_n, 2))
    add = lambda u, v: (u.astype(F32) + v.astype(F32)).astype(BF)
    a, b = add(keep_a, got_a), add(keep_b, got_b)
    got_a = lax.ppermute(a[q:], "seq", halving(seq_n, 2))
    got_b = lax.ppermute(b[q:], "seq", halving(seq_n, 1))
    c = jnp.concatenate([add(a[:q], got_a), add(b[:q], got_b)], axis=1)
    ch = q // dp_n
    out = c[:ch].astype(F32)
    for p in range(1, dp_n):
        out = out + lax.ppermute(c[p * ch : (p + 1) * ch], "dp", halving(dp_n, p)).astype(F32)
    return out


def reduce_any(full):
    part = lax.psum_scatter(full.astype(F32), "dp", scatter_dimension=0, tiled=True)
    return lax.psum_scatter(part, "seq", scatter_dimension=0, tiled=True)


def first_kernel(q_ref, k1_ref, gc_ref, cm_ref, marks_ref, gq_ref, mix_ref, km_ref, *, tok):
    n = marks_ref.shape[0]
    lm = tok // M
    mask = block_mask()
    km = spread_blocks(
        jnp.concatenate([marks_ref[i, lm : 2 * lm, :] for i in range(n)], axis=0), mask
    )
    gc = gc_ref[...]
    k1 = k1_ref[...]
    mix_ref[...] = gather_blocks(nn(k1, gc)).astype(BF)
    g = nt(spread_blocks(cm_ref[...], mask), gc).reshape(QUAD // M, M, tok)
    kf = k1.astype(F32).reshape(QUAD // M, M, tok)
    inner = jnp.sum(g * kf, axis=1, keepdims=True)
    g1 = (kf * (g - inner)).reshape(QUAD, tok).astype(BF)
    gq_ref[...] = (tn(g1, km) * 0.125).astype(BF)
    km_ref[...] = gather_blocks(nn(g1, q_ref[...])) * 0.125


def first_back(q, k1, gc, cm, marks):
    tok, d = q.shape
    n = marks.shape[0]
    lane = lambda i: (0, i)
    cost = pl.CostEstimate(flops=8 * tok * d * QUAD, bytes_accessed=8 * tok * d, transcendentals=0)
    return pl.pallas_call(
        functools.partial(first_kernel, tok=tok),
        grid=(d // QUAD,),
        in_specs=[
            pl.BlockSpec((tok, QUAD), lane),
            pl.BlockSpec((QUAD, tok), lambda i: (i, 0)),
            pl.BlockSpec((tok, QUAD), lane),
            pl.BlockSpec((M, QUAD), lane),
            pl.BlockSpec((n, marks.shape[1], QUAD), lambda i: (0, 0, i)),
        ],
        out_specs=[
            pl.BlockSpec((tok, QUAD), lane),
            pl.BlockSpec((M, QUAD), lane),
            pl.BlockSpec((M, QUAD), lane),
        ],
        out_shape=[sds((tok, d), BF), sds((M, d), BF), sds((M, d), F32)],
        compiler_params=params(),
        cost_estimate=cost,
        name="first_back",
    )(q, k1, gc, cm, marks)


def middle_kernel(idx, gmix_ref, lv_ref, inv_ref, gst_ref, gm_ref, gt_ref):
    n = gmix_ref.shape[0]
    d = lv_ref.shape[1]
    mask = block_mask()
    lane = iota((M, 128), 1)
    head = iota((M, QUAD), 1) // M
    stat = gst_ref[...]
    gt = jnp.zeros((M, 128), F32)
    for c in range(d // QUAD):
        cols = slice(c * QUAD, (c + 1) * QUAD)
        gmix = jnp.zeros((M, QUAD), F32)
        for i in range(n):
            gmix = gmix + gmix_ref[i, :, cols].astype(F32)
        glv = gather_blocks(
            three(tn, spread_blocks(inv_ref[:, cols], mask), spread_blocks(gmix, mask))
        )
        scale = per_head(stat, 0, c)
        total = per_head(stat, 64, c)
        gm_ref[:, cols] = ((glv / total).astype(BF).astype(F32) * scale).astype(BF)
        prod = glv * lv_ref[:, cols]
        for h in range(QUAD // M):
            at = c * (QUAD // M) + h
            s = jnp.sum(jnp.where(head == h, prod, 0.0), axis=1, keepdims=True)
            gt = jnp.where(lane == at, -s / stat[:, 64 + at : 65 + at] * stat[:, at : at + 1], gt)
    gt_ref[...] = gt


def middle(idx, gmix, lv, inv, gst):
    d = lv.shape[1]
    return pl.pallas_call(
        middle_kernel,
        grid_spec=pltpu.PrefetchScalarGridSpec(
            num_scalar_prefetch=1,
            grid=(1,),
            in_specs=[whole(gmix.shape), whole(lv.shape), whole(inv.shape), whole(gst.shape)],
            out_specs=[whole((M, d)), whole((M, 128))],
        ),
        out_shape=[sds((M, d), BF), sds((M, 128), F32)],
        compiler_params=params(),
        name="middle",
    )(idx, gmix, lv, inv, gst)


def pinv_back_kernel(idx, gmix_ref, lv_ref, k2_ref, save_ref, marks_ref, out_ref, *, lm):
    n = gmix_ref.shape[0]
    mask = block_mask()
    ident = (iota((QUAD, QUAD), 0) == iota((QUAD, QUAD), 1)).astype(F32)
    gmix = jnp.zeros((M, QUAD), F32)
    for i in range(n):
        gmix = gmix + gmix_ref[i].astype(F32)
    dz = three(nt, spread_blocks(gmix, mask), spread_blocks(lv_ref[...], mask))
    kernel = spread_blocks(k2_ref[...], mask)
    klow = kernel.astype(BF)
    dk = jnp.zeros((QUAD, QUAD), F32)
    ibf = ident.astype(BF)
    for it in range(ITERS - 1, -1, -1):
        z, p, i2, i3 = (save_ref[it, kind] for kind in range(4))
        i1 = 7.0 * ibf - p
        dlow = dz.astype(BF)
        d3 = (0.25 * tn(z, dlow)).astype(BF)
        dp = nt(d3, i2)
        d2 = (-tn(p, d3)).astype(BF)
        dp = dp + nt(d2, i1)
        d1 = -tn(p, d2)
        dp = (-dp - d1).astype(BF)
        dz = 0.25 * nt(dlow, i3) + tn(klow, dp)
        dk = dk + nt(dp, z)
    sums = jnp.sum(kernel, axis=0, keepdims=True)
    lane = iota((1, QUAD), 1) // M
    dzt = jnp.where(mask, dz, 0.0).T
    dsum = jnp.sum(dzt * kernel, axis=0, keepdims=True)
    scale = jnp.zeros((1, QUAD), F32)
    extra = jnp.zeros((1, QUAD), F32)
    for h in range(QUAD // M):
        mine = lane == h
        best = jnp.max(jnp.where(mine, sums, 0.0), axis=1, keepdims=True)
        dscale = jnp.sum(jnp.where(mine, dsum, 0.0), axis=1, keepdims=True)
        is_best = (mine & (sums == best)).astype(F32)
        share = is_best / jnp.sum(is_best, axis=1, keepdims=True)
        scale = jnp.where(mine, 1.0 / best, scale)
        extra = jnp.where(mine, -dscale / (best * best) * share, extra)
    dk = dk + dzt * scale + extra
    inner = jnp.sum(jnp.where(mask, dk * kernel, 0.0), axis=1, keepdims=True)
    g2 = kernel * (dk - inner)
    qm = jnp.concatenate([marks_ref[i, 0:lm, :] for i in range(n)], axis=0)
    km = jnp.concatenate([marks_ref[i, lm : 2 * lm, :] for i in range(n)], axis=0)
    g2h, g2l = split(g2)
    kb, qb = spread_blocks(km, mask), spread_blocks(qm, mask)
    use = (idx[1] < idx[3]).astype(F32) * 0.125
    out_ref[0] = gather_blocks(nn(g2h, kb) + nn(g2l, kb)) * use
    out_ref[1] = gather_blocks(tn(g2h, qb) + tn(g2l, qb)) * use


def pinv_back(idx, gmix, lv, k2, save, marks, lm):
    d = lv.shape[1]
    n = marks.shape[0]
    last = d // QUAD - 1
    col = lambda i, s: (0, jnp.minimum(s[1], last))
    col3 = lambda i, s: (0, 0, jnp.minimum(s[1], last))
    cost = pl.CostEstimate(flops=48 * 2 * QUAD**3, bytes_accessed=4 * 10**6, transcendentals=0)
    return pl.pallas_call(
        functools.partial(pinv_back_kernel, lm=lm),
        grid_spec=pltpu.PrefetchScalarGridSpec(
            num_scalar_prefetch=1,
            grid=(1,),
            in_specs=[
                pl.BlockSpec((n, M, QUAD), col3),
                pl.BlockSpec((M, QUAD), col),
                pl.BlockSpec((M, QUAD), col),
                whole(save.shape),
                pl.BlockSpec((n, marks.shape[1], QUAD), col3),
            ],
            out_specs=whole((2, M, QUAD)),
        ),
        out_shape=sds((2, M, QUAD), F32),
        compiler_params=params(),
        cost_estimate=cost,
        name="pinv_back",
    )(idx, gmix, lv, k2, save, marks)


def second_kernel(
    idx, k_ref, v_ref, vedge_ref, gc_ref, gedge_ref, e_ref, gm_ref, gt_ref, marks_ref, doc_ref,
    pad_ref, taps_ref, gk_ref, gv_ref, qm_ref, gtap_ref, vext, gext, band, *, tok,
):
    quad = pl.program_id(0)
    n = marks_ref.shape[0]
    lm = tok // M
    heads = QUAD // M
    half = taps_ref.shape[2] // 2
    mask = block_mask()
    qm = spread_blocks(
        jnp.concatenate([marks_ref[i, 0:lm, :] for i in range(n)], axis=0), mask
    )
    gm = spread_blocks(gm_ref[...], mask)
    lane = iota((M, 128), 1)
    cols = []
    for h in range(heads):
        pick = jnp.where(lane == quad * heads + h, gt_ref[...], 0.0)
        cols.append(jnp.sum(pick, axis=1, keepdims=True))
    gt = jnp.concatenate(cols, axis=0)
    e = e_ref[...]
    g3 = (e.astype(F32) * (nt(gm, v_ref[...]) + gt)).astype(BF)
    qm_ref[...] = gather_blocks(nn(g3, k_ref[...])) * 0.125
    gk_ref[...] = (tn(g3, qm) * 0.125).astype(BF)
    gv = tn(e, gm)
    fill_halo(vext, v_ref, vedge_ref, tok)
    fill_halo(gext, gc_ref, gedge_ref, tok)
    fill_bands(taps_ref.at[0], band, half, True)
    bounds = doc_bounds(doc_ref, idx)
    start = idx[1] * tok
    keep_n = valid_count(pad_ref, idx) - start
    col64 = iota((128, 128), 1)
    pairs = [jnp.zeros((128, 256), F32) for _ in range(heads)]
    for sub in range(tok // 128):
        place = start + sub * 128
        same = (
            docs_at(place + iota((128, 1), 0), bounds, LEN)
            == docs_at(place - 64 + iota((1, 256), 1), bounds, LEN)
        )
        low = same.astype(BF)
        keep = iota((128, 1), 0) < keep_n - sub * 128
        at = slice(sub * 128, sub * 128 + 128)
        for pair in range(heads // 2):
            lanes = slice(pair * 128, pair * 128 + 128)
            back = banded(band, gext[sub * 128 : sub * 128 + 256, lanes], low, 2 * pair)
            gv_ref[at, lanes] = jnp.where(keep, gv[at, lanes] + back, 0.0).astype(BF)
            g = gc_ref[at, lanes]
            win = vext[sub * 128 : sub * 128 + 256, lanes]
            for h in range(2):
                own = jnp.where((col64 < 64) == (h == 0), g, jnp.zeros((), BF))
                pairs[2 * pair + h] += jnp.where(same, nt(own, win), 0.0)
    gap = iota((128, 256), 1) - iota((128, 256), 0) - 64 + half
    out = jnp.zeros((8, 128), F32)
    line, lane8 = iota((8, 128), 0), iota((8, 128), 1)
    for h in range(heads):
        for o in range(2 * half + 1):
            val = jnp.sum(jnp.where(gap == o, pairs[h], 0.0))
            out = jnp.where((line == h) & (lane8 == o), val, out)
    gtap_ref[0] = out


def second_back(idx, k, v, vedge, gc, gedge, e, gm, gt, marks, documents, padding, taps):
    tok, d = k.shape
    n = marks.shape[0]
    heads = QUAD // M
    lane = lambda i, s: (0, i)
    taps3 = taps.reshape(d // QUAD, heads, taps.shape[1])
    cost = pl.CostEstimate(flops=16 * tok * d * QUAD, bytes_accessed=12 * tok * d, transcendentals=0)
    return pl.pallas_call(
        functools.partial(second_kernel, tok=tok),
        grid_spec=pltpu.PrefetchScalarGridSpec(
            num_scalar_prefetch=1,
            grid=(d // QUAD,),
            in_specs=[
                pl.BlockSpec((tok, QUAD), lane),
                pl.BlockSpec((tok, QUAD), lane),
                pl.BlockSpec((32, QUAD), lane),
                pl.BlockSpec((tok, QUAD), lane),
                pl.BlockSpec((32, QUAD), lane),
                pl.BlockSpec((QUAD, tok), lambda i, s: (i, 0)),
                pl.BlockSpec((M, QUAD), lane),
                whole(gt.shape),
                pl.BlockSpec((n, marks.shape[1], QUAD), lambda i, s: (0, 0, i)),
                whole(documents.shape),
                whole(padding.shape),
                pl.BlockSpec((1, heads, taps.shape[1]), lambda i, s: (i, 0, 0)),
            ],
            out_specs=[
                pl.BlockSpec((tok, QUAD), lane),
                pl.BlockSpec((tok, QUAD), lane),
                pl.BlockSpec((M, QUAD), lane),
                pl.BlockSpec((1, 8, 128), lambda i, s: (i, 0, 0)),
            ],
            scratch_shapes=[
                pltpu.VMEM((tok + 128, QUAD), BF),
                pltpu.VMEM((tok + 128, QUAD), BF),
                pltpu.VMEM((heads, 128, 256), BF),
            ],
        ),
        out_shape=[
            sds((tok, d), BF),
            sds((tok, d), BF),
            sds((M, d), F32),
            sds((d // QUAD, 8, 128), F32),
        ],
        compiler_params=params(),
        cost_estimate=cost,
        name="second_back",
    )(idx, k, v, vedge, gc, gedge, e, gm, gt, marks, documents, padding, taps3)


def spread_kernel(idx, gq_ref, gk_ref, got_ref, pad_ref, dq0, dq1, dk0, dk1, *, tok):
    n = got_ref.shape[0]
    lm = tok // M
    d = gq_ref.shape[1]
    half = d // 2
    got = got_ref[0].astype(F32)
    for i in range(1, n):
        got = got + got_ref[i].astype(F32)
    keep_n = valid_count(pad_ref, idx) - idx[1] * tok
    keep = (iota((tok, 1), 0) < keep_n).astype(F32).reshape(lm, M, 1)
    share = keep / jnp.maximum(jnp.sum(keep, axis=1, keepdims=True), 1.0)
    for at, src, outs in ((0, gq_ref, (dq0, dq1)), (lm, gk_ref, (dk0, dk1))):
        mark = got[at : at + lm].reshape(lm, 1, d)
        val = src[...].astype(F32).reshape(lm, M, d) + mark * share
        val = val.reshape(tok, d).astype(BF)
        outs[0][...] = val[:, :half]
        outs[1][...] = val[:, half:]


def spread(idx, gq, gk, got, padding):
    tok, d = gq.shape
    return pl.pallas_call(
        functools.partial(spread_kernel, tok=tok),
        grid_spec=pltpu.PrefetchScalarGridSpec(
            num_scalar_prefetch=1,
            grid=(1,),
            in_specs=[whole(gq.shape), whole(gk.shape), whole(got.shape), whole(padding.shape)],
            out_specs=[whole((tok, d // 2))] * 4,
        ),
        out_shape=[sds((tok, d // 2), BF)] * 4,
        compiler_params=params(),
        name="spread",
    )(idx, gq, gk, got, padding)


def inputs_kernel(idx, gh1_ref, dq0, dq1, dk0, dk1, dv_ref, q0, q1, k0, k1, v0, v1, out_ref):
    half = dq0.shape[1]
    acc = gh1_ref[...].astype(F32)
    acc = acc + nt(dq0[...], q0[...]) + nt(dq1[...], q1[...])
    acc = acc + nt(dk0[...], k0[...]) + nt(dk1[...], k1[...])
    acc = acc + nt(dv_ref[:, :half], v0[...]) + nt(dv_ref[:, half:], v1[...])
    out_ref[0] = acc.astype(BF)


def inputs_grad(idx, gh1, dq, dk, dv, wq, wk, wv):
    tok, d = gh1.shape
    half = d // 2
    rows = 512
    tokb = lambda j, i, s: (i, 0)
    wspec = pl.BlockSpec((half, half), lambda j, i, s: (s[0] ^ j, 0))
    cost = pl.CostEstimate(flops=6 * tok * d * d, bytes_accessed=12 * tok * d, transcendentals=0)
    return pl.pallas_call(
        inputs_kernel,
        grid_spec=pltpu.PrefetchScalarGridSpec(
            num_scalar_prefetch=1,
            grid=(2, tok // rows),
            in_specs=[pl.BlockSpec((rows, half), lambda j, i, s: (i, s[0] ^ j))]
            + [pl.BlockSpec((rows, half), tokb)] * 4
            + [pl.BlockSpec((rows, d), tokb)]
            + [wspec] * 6,
            out_specs=pl.BlockSpec((1, rows, half), lambda j, i, s: (j, i, 0)),
        ),
        out_shape=sds((2, tok, half), BF),
        compiler_params=params(),
        cost_estimate=cost,
        name="inputs_grad",
    )(idx, gh1, *dq, *dk, dv, *wq, *wk, *wv)


def shards(
    inputs,
    cotangent,
    padding,
    documents,
    w_query,
    w_key,
    w_value,
    w_out,
    w_up,
    w_down,
    conv_taps,
    gain_attn,
    shift_attn,
    gain_ffn,
    shift_ffn,
):
    row_count, tok, d = inputs.shape
    seq_n, dp_n = lax.axis_size("seq"), lax.axis_size("dp")
    mp, seq, dp = lax.axis_index("mp"), lax.axis_index("seq"), lax.axis_index("dp")
    lm = tok // M
    chunk = d // (seq_n * dp_n)
    fast = seq_n == 4 and dp_n == 4 and chunk % 16 == 0
    shape = (dp_n if fast else 0, seq_n, chunk)
    idx = jnp.stack(
        [mp, seq, dp, jnp.full((), min(d // QUAD, seq_n), jnp.int32)]
    ).astype(jnp.int32)

    def swap(a):
        return lax.ppermute(a, "mp", [(0, 1), (1, 0)])

    wq, wk, wv = ((w, swap(w)) for w in (w_query, w_key, w_value))
    wo, wu, wd = ((w, swap(w)) for w in (w_out, w_up, w_down))
    taps = jnp.concatenate([conv_taps, swap(conv_taps)], axis=0)
    q, k, v, pack = project(idx, inputs, padding, (*wq, *wk, *wv), tok)
    marks, vedge = gather_seq(seq_n, [pack[: 2 * lm]], pack[2 * lm :], 1)
    k1, e, mix, stat = scores(idx, q, k, v, marks, padding)
    k2, inv, save = pinv(idx, marks, lm)
    mixes, stats = gather_seq(seq_n, [mix, stat], None, 2)
    cm, lv, gst = combine(idx, mixes, stats, inv)
    vecs = [a.reshape(1, d) for a in (gain_attn, shift_attn, gain_ffn, shift_ffn)]
    out_own, ctx, h1, nl, act0, act1, gp0, gp1, gh2, acc_f = forward(
        idx, inputs, cotangent, padding, documents, v, vedge, k1, cm, taps, wo, wu, wd, vecs
    )
    out_other = swap(out_own)
    g_down = weight_grads(idx, [(gh2, 0)], [[act0, act1]], 256, shape)
    down_other = swap(g_down[1])
    du0, du1, gh1, gc, acc_b = backward(idx, gh2, h1, (gp0, gp1), wo, wu, wd, vecs[0])
    g_up = weight_grads(idx, [(nl, 0)], [[du0, du1]], 256, shape)
    up_other = swap(g_up[1])
    half = d // 2
    g_out = weight_grads(idx, [(gh1, 0)], [[ctx[:, :half], ctx[:, half:]]], 128, shape)
    out_w_other = swap(g_out[1])
    gq, gmix, gkm = first_back(q, k1, gc, cm, marks)
    gedge_own = jnp.concatenate([gc[:16], gc[tok - 16 :]], axis=0)
    gmixes, gedge = gather_seq(seq_n, [gmix], gedge_own, 3)
    gm, gt = middle(idx, gmixes, lv, inv, gst)
    two = pinv_back(idx, gmixes, lv, k2, save, marks, lm)
    gk, gv, gqm, gtap = second_back(
        idx, k, v, vedge, gc, gedge, e, gm, gt, marks, documents, padding, taps
    )
    at = jnp.minimum(seq, d // QUAD - 1) * QUAD
    gqm = gqm + lax.dynamic_update_slice(jnp.zeros((M, d), F32), two[0], (0, at))
    gkm = gkm + lax.dynamic_update_slice(jnp.zeros((M, d), F32), two[1], (0, at))
    both = jnp.concatenate(
        [gqm.reshape(seq_n, lm, d), gkm.reshape(seq_n, lm, d)], axis=1
    ).astype(BF)
    got = scatter_seq(seq_n, both, 4)
    dq0, dq1, dk0, dk1 = spread(idx, gq, gk, got, padding)
    dq1_got, dk1_got, dv1_got = swap(dq1), swap(dk1), swap(gv[:, half:])
    g_qkv = weight_grads(
        idx,
        [(inputs, 0), (inputs, 1)],
        [[dq0, dk0, gv[:, :half]], [dq1_got, dk1_got, dv1_got]],
        128,
        shape,
    )
    gin = inputs_grad(idx, gh1, (dq0, dq1), (dk0, dk1), gv, wq, wk, wv)
    gin_other = swap(gin[1])

    reduce = reduce_fast if fast else reduce_any

    def add(a, b):
        return (a.astype(F32) + b.astype(F32)).astype(BF)

    sum_down = reduce(add(g_down[0], down_other))
    sum_up = reduce(add(g_up[0], up_other))
    sum_out = reduce(add(g_out[0], out_w_other))
    sum_qkv = reduce(jnp.concatenate(g_qkv, axis=1))

    def rows_of(own, other):
        return jnp.where(mp == 0, jnp.stack([own, other]), jnp.stack([other, own]))

    heads = conv_taps.shape[0]
    tap_all = gtap[:, : QUAD // M, : conv_taps.shape[1]].reshape(2, heads, -1)
    tap_all = jnp.where(mp == 0, tap_all, tap_all[::-1])
    squares = jnp.sum(acc_f[2:5], axis=1)
    place = jnp.arange(dp_n * row_count, dtype=jnp.int32) == dp * row_count + mp
    squares = jnp.where(place[:, None], squares[None, :], 0.0)
    tap_all, norms, squares = lax.psum(
        (tap_all, jnp.concatenate([acc_b[:2], acc_f[:2]], axis=0), squares), ("dp", "seq", "mp")
    )
    tap_total = lax.dynamic_index_in_dim(tap_all, mp, 0, keepdims=False)
    own_squares = lax.dynamic_slice_in_dim(squares, dp * row_count, row_count, 0)
    row_valid = jnp.sum(padding.astype(F32), axis=1)
    row_rms = jnp.sqrt(own_squares / (row_valid[:, None] * d) + 1e-06)
    return (
        rows_of(out_own, out_other),
        rows_of(gin[0], gin_other),
        sum_qkv[:, :half],
        sum_qkv[:, half : 2 * half],
        sum_qkv[:, 2 * half :],
        sum_out.T,
        sum_up,
        sum_down.T,
        tap_total,
        norms[0],
        norms[1],
        norms[2],
        norms[3],
        row_rms,
    )


def solution(mesh):
    return jax.shard_map(
        shards,
        mesh=mesh,
        in_specs=(
            P("dp", "seq", None),
            P("dp", "seq", None),
            P("dp", None),
            P("dp", None),
            P(None, "mp"),
            P(None, "mp"),
            P(None, "mp"),
            P("mp", None),
            P(None, "mp"),
            P("mp", None),
            P("mp", None),
            P(),
            P(),
            P(),
            P(),
        ),
        out_specs=(
            P("dp", "seq", None),
            P("dp", "seq", "mp"),
            P(("dp", "seq"), "mp"),
            P(("dp", "seq"), "mp"),
            P(("dp", "seq"), "mp"),
            P("mp", ("dp", "seq")),
            P(("dp", "seq"), "mp"),
            P("mp", ("dp", "seq")),
            P("mp", None),
            P(),
            P(),
            P(),
            P(),
            P("dp", None),
        ),
        check_vma=False,
    )
```

```python
import functools

import jax
import jax.numpy as jnp
from jax import lax
from jax.experimental import pallas as pl
from jax.experimental.pallas import tpu as pltpu
from jax.sharding import PartitionSpec as P

M = 64
ITERS = 6
LEN = 4096
QUAD = 256
MESH = pl.DeviceIdType.MESH
F32 = jnp.float32
BF = jnp.bfloat16
EPS = 1e-05


def nn(a, b):
    return lax.dot_general(a, b, (((1,), (0,)), ((), ())), preferred_element_type=F32)


def nt(a, b):
    return lax.dot_general(a, b, (((1,), (1,)), ((), ())), preferred_element_type=F32)


def tn(a, b):
    return lax.dot_general(a, b, (((0,), (0,)), ((), ())), preferred_element_type=F32)


def split(a):
    high = a.astype(BF)
    return high, (a - high.astype(F32)).astype(BF)


def three(dot, a, b):
    ah, al = split(a)
    bh, bl = split(b)
    return dot(ah, bh) + (dot(ah, bl) + dot(al, bh))


def iota(shape, dim):
    return lax.broadcasted_iota(jnp.int32, shape, dim)


def block_mask():
    return iota((QUAD, QUAD), 0) // M == iota((QUAD, QUAD), 1) // M


def spread_blocks(x, mask):
    return jnp.where(mask, jnp.concatenate([x] * (QUAD // M), axis=0), jnp.zeros((), x.dtype))


def gather_blocks(y):
    lane = iota((M, QUAD), 1) // M
    out = jnp.zeros((M, QUAD), y.dtype)
    for h in range(QUAD // M):
        out = out + jnp.where(lane == h, y[h * M : (h + 1) * M], 0.0)
    return out


def params(limit=56, **kw):
    return pltpu.CompilerParams(vmem_limit_bytes=limit * 1024 * 1024, **kw)


def whole(shape):
    nd = len(shape)
    return pl.BlockSpec(shape, lambda *a: (0,) * nd)


def sds(shape, dtype):
    return jax.ShapeDtypeStruct(shape, dtype)


ANY = pl.BlockSpec(memory_space=pl.ANY)


def call(kernel, idx, args, in_specs, out_specs, out_shape, grid, name, scratch=(), flops=0, moved=0, exps=0, deps=(), limit=56):
    nd = len(deps)

    def body(idx_ref, *refs):
        kernel(idx_ref, *refs[nd:])

    return pl.pallas_call(
        body,
        grid_spec=pltpu.PrefetchScalarGridSpec(
            num_scalar_prefetch=1,
            grid=grid,
            in_specs=[ANY] * nd + list(in_specs),
            out_specs=out_specs,
            scratch_shapes=list(scratch),
        ),
        out_shape=out_shape,
        compiler_params=params(limit),
        cost_estimate=pl.CostEstimate(flops=flops, bytes_accessed=moved, transcendentals=exps),
        name=name,
    )(idx, *deps, *args)


def store_chunks(out_ref, t, idx, shape):
    z, sq, chunk = shape
    if z == 0:
        out_ref[...] = t
        return
    for zr in range(z):
        for sr in range(sq):
            b = idx[1] ^ sr
            place = ((b & 1) * 2 + (b >> 1)) * z + (idx[2] ^ zr)
            src = (zr * sq + sr) * chunk
            out_ref[pl.ds(pl.multiple_of(place * chunk, chunk), chunk), :] = t[src : src + chunk]


def valid_count(pad_ref, idx_ref):
    row = pad_ref[pl.ds(idx_ref[0], 1), :].astype(F32)
    return jnp.sum(row, axis=1, keepdims=True).astype(jnp.int32)


def enter(n):
    me = lax.axis_index("seq")
    barrier = pltpu.get_barrier_semaphore()
    for p in range(1, n):
        pl.semaphore_signal(
            barrier, inc=1, device_id={"seq": lax.rem(me + p, n)}, device_id_type=MESH
        )
    pl.semaphore_wait(barrier, n - 1)
    return me


def gather_kernel(*refs, n, count, edges):
    ins = refs[:count]
    outs = refs[count : 2 * count]
    at = 2 * count
    if edges:
        edge_in, edge_out = refs[at], refs[at + 1]
        at += 2
    send, recv, local = refs[at : at + 3]
    me = enter(n)
    copies = []
    slot = 0
    for src, dst in zip(ins, outs):
        for p in range(1, n):
            copies.append(
                pltpu.make_async_remote_copy(
                    src_ref=src,
                    dst_ref=dst.at[me],
                    send_sem=send.at[slot],
                    recv_sem=recv.at[slot],
                    device_id={"seq": lax.rem(me + p, n)},
                    device_id_type=MESH,
                )
            )
            slot += 1
    if edges:
        for side, p in ((0, 1), (1, n - 1)):
            first = 16 if side == 0 else 0
            copies.append(
                pltpu.make_async_remote_copy(
                    src_ref=edge_in.at[pl.ds(first, 16)],
                    dst_ref=edge_out.at[pl.ds(side * 16, 16)],
                    send_sem=send.at[slot],
                    recv_sem=recv.at[slot],
                    device_id={"seq": lax.rem(me + p, n)},
                    device_id_type=MESH,
                )
            )
            slot += 1
    for c in copies:
        c.start()
    locals_ = [
        pltpu.make_async_copy(src, dst.at[me], local.at[i])
        for i, (src, dst) in enumerate(zip(ins, outs))
    ]
    for c in locals_:
        c.start()
    for c in locals_:
        c.wait()
    for c in copies:
        c.wait()


def gather_seq(n, arrays, edge, cid, deps=()):
    count = len(arrays)
    total = count * (n - 1) + (2 if edge is not None else 0)
    outs = [sds((n,) + a.shape, a.dtype) for a in arrays]
    args = list(arrays)
    if edge is not None:
        outs.append(sds(edge.shape, edge.dtype))
        args.append(edge)

    nd = len(deps)

    def body(*refs):
        ins = refs[nd : nd + len(args)]
        rest = refs[nd + len(args) :]
        o = rest[: len(outs)]
        sems = rest[len(outs) :]
        if edge is not None:
            order = ins[:count] + o[:count] + (ins[count], o[count]) + sems
        else:
            order = ins + o + sems
        gather_kernel(*order, n=n, count=count, edges=edge is not None)

    return pl.pallas_call(
        body,
        in_specs=[pl.BlockSpec(memory_space=pl.ANY)] * (nd + len(args)),
        out_specs=[pl.BlockSpec(memory_space=pl.ANY)] * len(outs),
        out_shape=outs,
        scratch_shapes=[
            pltpu.SemaphoreType.DMA((total,)),
            pltpu.SemaphoreType.DMA((total,)),
            pltpu.SemaphoreType.DMA((count,)),
        ],
        compiler_params=params(8, collective_id=cid, has_side_effects=True),
        name="gather%d" % cid,
    )(*deps, *args)


def scatter_seq(n, array, small, cid, deps=()):
    nd = len(deps)

    def body(*refs):
        src, src2, dst, dst2, send, recv, local = refs[nd:]
        me = enter(n)
        copies = []
        for p in range(1, n):
            to = lax.rem(me + p, n)
            for at, a, b in ((0, src.at[to], dst.at[me]), (n, src2, dst2.at[me])):
                copies.append(
                    pltpu.make_async_remote_copy(
                        src_ref=a,
                        dst_ref=b,
                        send_sem=send.at[at + p],
                        recv_sem=recv.at[at + p],
                        device_id={"seq": to},
                        device_id_type=MESH,
                    )
                )
        for c in copies:
            c.start()
        owns = [
            pltpu.make_async_copy(src.at[me], dst.at[me], local.at[0]),
            pltpu.make_async_copy(src2, dst2.at[me], local.at[1]),
        ]
        for c in owns:
            c.start()
        for c in owns:
            c.wait()
        for c in copies:
            c.wait()

    return pl.pallas_call(
        body,
        in_specs=[ANY] * (2 + nd),
        out_specs=[ANY] * 2,
        out_shape=[sds(array.shape, array.dtype), sds((n,) + small.shape, small.dtype)],
        scratch_shapes=[
            pltpu.SemaphoreType.DMA((2 * n,)),
            pltpu.SemaphoreType.DMA((2 * n,)),
            pltpu.SemaphoreType.DMA((2,)),
        ],
        compiler_params=params(8, collective_id=cid, has_side_effects=True),
        name="scatter%d" % cid,
    )(*deps, array, small)


def per_head(stat, base, c):
    lane = iota((M, QUAD), 1) // M
    out = jnp.zeros((M, QUAD), F32)
    for h in range(QUAD // M):
        at = base + c * (QUAD // M) + h
        out = jnp.where(lane == h, stat[:, at : at + 1], out)
    return out


def places():
    return [lax.axis_index(a) for a in ("mp", "seq", "dp")]


def greet(seq_n, dp_n=1):
    barrier = pltpu.get_barrier_semaphore()
    for axis, size in (("seq", seq_n), ("dp", dp_n)):
        me = lax.axis_index(axis)
        for p in range(1, size):
            pl.semaphore_signal(
                barrier, inc=1, device_id={axis: lax.rem(me + p, size)}, device_id_type=MESH
            )
    return lambda: pl.semaphore_wait(barrier, seq_n + dp_n - 2)


def remote(src, dst, send, recv, axis, to):
    return pltpu.make_async_remote_copy(
        src_ref=src,
        dst_ref=dst,
        send_sem=send,
        recv_sem=recv,
        device_id={axis: to},
        device_id_type=MESH,
    )


def score_quad(c, q_ref, k_ref, v_ref, qm, km, minus, k1_ref, e_ref, mix_ref, stat):
    cols = slice(c * QUAD, (c + 1) * QUAD)
    tok = q_ref.shape[0]
    mask = block_mask()
    s1 = nt(spread_blocks(km[:, cols], mask), q_ref[:, cols]) * 0.125
    s1 = s1.reshape(QUAD // M, M, tok)
    e1 = jnp.exp(s1 - jnp.max(s1, axis=1, keepdims=True))
    k1 = e1 * (1.0 / jnp.sum(e1, axis=1, keepdims=True))
    k1_ref[cols, :] = k1.reshape(QUAD, tok).astype(BF)
    s3 = nt(spread_blocks(qm[:, cols], mask), k_ref[:, cols]) * 0.125 - minus
    top = jnp.max(s3, axis=1, keepdims=True)
    e3 = jnp.exp(s3 - top)
    total = jnp.sum(e3, axis=1, keepdims=True)
    e3 = e3.astype(BF)
    e_ref[cols, :] = e3
    mix_ref[:, cols] = gather_blocks(nn(e3, v_ref[:, cols])).astype(BF)
    lane = iota((M, 128), 1)
    for h in range(QUAD // M):
        at = c * (QUAD // M) + h
        stat = jnp.where(lane == at, top[h * M : (h + 1) * M], stat)
        stat = jnp.where(lane == 64 + at, total[h * M : (h + 1) * M], stat)
    return stat


def pseudo_inverse(qm, km, k2_ref, inv_ref, save_ref, sel):
    d = qm.shape[1]
    quads = d // QUAD
    mask = block_mask()
    ident = (iota((QUAD, QUAD), 0) == iota((QUAD, QUAD), 1)).astype(F32)
    kernel, z = [], []
    for c in range(quads):
        cols = slice(c * QUAD, (c + 1) * QUAD)
        s2 = nt(spread_blocks(qm[:, cols], mask), spread_blocks(km[:, cols], mask)) * 0.125
        s2 = jnp.where(mask, s2, -1e30)
        e2 = jnp.exp(s2 - jnp.max(s2, axis=1, keepdims=True))
        e2 = e2 / jnp.sum(e2, axis=1, keepdims=True)
        kernel.append(e2)
        sums = jnp.sum(e2, axis=0, keepdims=True)
        lane = iota((1, QUAD), 1) // M
        scale = jnp.zeros((1, QUAD), F32)
        for h in range(QUAD // M):
            best = jnp.max(jnp.where(lane == h, sums, 0.0), axis=1, keepdims=True)
            scale = jnp.where(lane == h, 1.0 / best, scale)
        z.append(e2.T * scale)
        k2_ref[:, cols] = gather_blocks(e2)

    def keep(it, kind, vals):
        for c in range(quads):

            @pl.when(sel == c)
            def _():
                save_ref[it, kind] = vals[c].astype(BF)

    ksp = [split(a) for a in kernel]

    def mul(a, b):
        return nn(a[0], b[0]) + (nn(a[0], b[1]) + nn(a[1], b[0]))

    for it in range(ITERS):
        zs = [split(a) for a in z]
        p = [mul(a, b) for a, b in zip(ksp, zs)]
        ps = [split(a) for a in p]
        i2 = [15.0 * ident - mul(a, split(7.0 * ident - b)) for a, b in zip(ps, p)]
        i3 = [13.0 * ident - mul(a, split(b)) for a, b in zip(ps, i2)]
        keep(it, 0, z)
        keep(it, 1, p)
        keep(it, 2, i2)
        keep(it, 3, i3)
        z = [0.25 * mul(a, split(b)) for a, b in zip(zs, i3)]
    for c in range(quads):
        inv_ref[:, c * QUAD : (c + 1) * QUAD] = gather_blocks(z[c])


def combine(mix_ref, stat_ref, inv_ref, me, cm_ref, lv_ref, gst_ref):
    n, _, d = mix_ref.shape
    lane = iota((M, 128), 1)
    top = stat_ref[0]
    for i in range(1, n):
        top = jnp.maximum(top, stat_ref[i])
    top = jnp.where(lane < 64, top, 0.0)
    total = jnp.zeros((M, 128), F32)
    scales = []
    for i in range(n):
        st = stat_ref[i]
        sc = jnp.where(lane < 64, jnp.exp(st - top), 0.0)
        scales.append(sc)
        total = total + sc * pltpu.roll(st, 64, 1)
    own = jnp.where(lane < 64, jnp.exp(stat_ref[me] - top), 0.0)
    gst_ref[...] = jnp.where(lane < 64, own, pltpu.roll(total, 64, 1))
    mask = block_mask()
    for c in range(d // QUAD):
        cols = slice(c * QUAD, (c + 1) * QUAD)
        mixed = jnp.zeros((M, QUAD), F32)
        for i in range(n):
            mixed = mixed + per_head(scales[i], 0, c) * mix_ref[i, :, cols].astype(F32)
        lv = mixed / per_head(total, 0, c)
        lv_ref[:, cols] = lv
        cm = three(nn, spread_blocks(inv_ref[:, cols], mask), spread_blocks(lv, mask))
        cm_ref[:, cols] = gather_blocks(cm).astype(BF)


def attend_kernel(
    inputs_any, pad_ref, wq0, wq1, wk0, wk1, wv0, wv1,
    q_any, k_any, v_any, xt_any, k1_any, e_any, save_any,
    marks, edge, cm_ref, lv_ref, gst_ref, inv_ref, k2_ref,
    x, q, k, v, xt, k1, e, save, pack, mix, stat, mixes, stats,
    ship, send, recv, *, n, shape,
):
    idx = places()
    me = idx[1]
    tok, d = x.shape
    half = d // 2
    lm = tok // M
    ready = greet(n)
    load = pltpu.make_async_copy(inputs_any.at[idx[0]], x, ship.at[0])
    load.start()
    moved = []

    def out(src, dst):
        c = pltpu.make_async_copy(src, dst, ship.at[1 + len(moved)])
        c.start()
        moved.append(c)

    peers = [lax.rem(me + p, n) for p in range(1, n)]
    sent = []

    def tell(src, dst, to):
        c = remote(src, dst, send.at[len(sent)], recv.at[len(sent)], "seq", to)
        c.start()
        sent.append(c)
        return c

    valid = pad_ref[pl.ds(idx[0], 1), :].astype(F32)
    keep_n = jnp.sum(valid, axis=1, keepdims=True).astype(jnp.int32) - me * tok
    keep = (iota((tok, 1), 0) < keep_n).astype(F32)
    count = jnp.maximum(jnp.sum(keep.reshape(lm, M, 1), axis=1), 1.0)
    load.wait()
    for at, w, dst in ((0, (wq0, wq1), q), (lm, (wk0, wk1), k)):
        for i in range(2):
            cols = slice(i * half, (i + 1) * half)
            val = nn(x[...], w[i][...]).astype(BF)
            dst[:, cols] = val
            wide = (val.astype(F32) * keep).reshape(lm, M, half)
            pack[at : at + lm, cols] = (jnp.sum(wide, axis=1) / count).astype(BF)
    ready()
    first = [tell(pack, marks.at[me], to) for to in peers]
    marks[me] = pack[...]
    for i, w in enumerate((wv0, wv1)):
        v[:, i * half : (i + 1) * half] = (nn(x[...], w[...]) * keep).astype(BF)
    edges = [
        tell(v.at[pl.ds(tok - 16, 16)], edge.at[pl.ds(0, 16)], peers[0]),
        tell(v.at[pl.ds(0, 16)], edge.at[pl.ds(16, 16)], peers[n - 2]),
    ]
    store_chunks(xt, x[...].T, idx, shape)
    for src, dst in ((q, q_any), (k, k_any), (v, v_any), (xt, xt_any)):
        out(src, dst)
    for c in first:
        c.wait()
    qm = jnp.concatenate([marks[i, 0:lm, :] for i in range(n)], axis=0)
    km = jnp.concatenate([marks[i, lm : 2 * lm, :] for i in range(n)], axis=0)
    minus = jnp.where(iota((1, tok), 1) < keep_n, 0.0, 1000000000.0)
    st = jnp.zeros((M, 128), F32)
    for c in range(d // QUAD):
        st = score_quad(c, q, k, v, qm, km, minus, k1, e, mix, st)
    stat[...] = st
    second = [tell(a, b.at[me], to) for a, b in ((mix, mixes), (stat, stats)) for to in peers]
    mixes[me] = mix[...]
    stats[me] = stat[...]
    out(k1, k1_any)
    out(e, e_any)
    pseudo_inverse(qm, km, k2_ref, inv_ref, save, jnp.minimum(me, d // QUAD - 1))
    out(save, save_any)
    for c in second:
        c.wait()
    combine(mixes, stats, inv_ref, me, cm_ref, lv_ref, gst_ref)
    for c in edges + moved:
        c.wait()


def attend(n, inputs, padding, weights, shape):
    _, tok, d = inputs.shape
    lm = tok // M
    flat, turned = sds((tok, d), BF), sds((d, tok), BF)
    save = sds((ITERS, 4, QUAD, QUAD), BF)
    big = [flat, flat, flat, turned, turned, turned, save]
    small = [
        sds((n, 2 * lm, d), BF),
        sds((32, d), BF),
        sds((M, d), BF),
        sds((M, d), F32),
        sds((M, 128), F32),
        sds((M, d), F32),
        sds((M, d), F32),
    ]
    vm = pl.BlockSpec(memory_space=pltpu.VMEM)
    count = 3 * (n - 1) + 2
    return pl.pallas_call(
        functools.partial(attend_kernel, n=n, shape=shape),
        in_specs=[ANY] + [vm] * 7,
        out_specs=[ANY] * len(big) + [vm] * len(small),
        out_shape=big + small,
        scratch_shapes=[pltpu.VMEM(a.shape, a.dtype) for a in [flat] + big]
        + [
            pltpu.VMEM((2 * lm, d), BF),
            pltpu.VMEM((M, d), BF),
            pltpu.VMEM((M, 128), F32),
            pltpu.VMEM((n, M, d), BF),
            pltpu.VMEM((n, M, 128), F32),
            pltpu.SemaphoreType.DMA((8,)),
            pltpu.SemaphoreType.DMA((count,)),
            pltpu.SemaphoreType.DMA((count,)),
        ],
        compiler_params=params(56, collective_id=1, has_side_effects=True),
        cost_estimate=pl.CostEstimate(
            flops=6 * tok * d * d + 72 * 3 * 2 * QUAD**3,
            bytes_accessed=30 * tok * d,
            transcendentals=2 * tok * d,
        ),
        name="attend",
    )(inputs, padding, *weights)


def doc_bounds(doc_ref, idx):
    row = doc_ref[pl.ds(idx[0], 1), :]
    return [
        jnp.sum((row < j).astype(F32), axis=1, keepdims=True).astype(jnp.int32)
        for j in range(1, 9)
    ]


def docs_at(place, bounds, length):
    doc = jnp.zeros(place.shape, jnp.int32)
    for b in bounds:
        doc = doc + (place >= b).astype(jnp.int32)
    return jnp.where((place >= 0) & (place < length), doc, -1)


def tap_lines(taps):
    heads, width = taps.shape
    at = 64 - width // 2
    pad = ((0, 0), (at, 256 - at - width))
    return jnp.stack([jnp.pad(taps, pad), jnp.pad(taps[:, ::-1], pad)])


def fill_bands(line_ref, band_ref):
    for h in range(band_ref.shape[0]):
        wide = jnp.broadcast_to(line_ref[h : h + 1, :], band_ref.shape[1:])
        band_ref[h] = pltpu.roll(wide, 0, 1, stride=1, stride_axis=0).astype(BF)


def banded(band_ref, window, same, col0):
    lane = iota((band_ref.shape[1], 128), 1)
    first = nn(band_ref[col0] * same, window)
    second = nn(band_ref[col0 + 1] * same, window)
    return jnp.where(lane < 64, first, second)


def fill_halo(ext, body, edge_ref, tok):
    ext[0:48, :] = jnp.zeros((48, ext.shape[1]), BF)
    ext[48:64, :] = edge_ref[0:16, :]
    ext[64 : 64 + tok, :] = body[...]
    ext[64 + tok : 80 + tok, :] = edge_ref[16:32, :]
    ext[80 + tok :, :] = jnp.zeros((48, ext.shape[1]), BF)


def erf_parts(u):
    a = jnp.abs(u) * 0.7071067811865476
    e = jnp.exp(-0.5 * u * u)
    t = 1.0 / (1.0 + 0.3275911 * a)
    poly = t * (
        0.254829592
        + t * (-0.284496736 + t * (1.421413741 + t * (-1.453152027 + t * 1.061405429)))
    )
    tail = 0.5 * poly * e
    cdf = jnp.where(u < 0.0, tail, 1.0 - tail)
    return cdf, e * 0.3989422804014327


def norm_stats(h):
    mean = jnp.mean(h, axis=-1, keepdims=True)
    centre = h - mean
    rstd = lax.rsqrt(jnp.mean(centre * centre, axis=-1, keepdims=True) + EPS)
    return centre * rstd, rstd


def norm_back(g, hat, rstd):
    return rstd * (
        g
        - jnp.mean(g, axis=-1, keepdims=True)
        - hat * jnp.mean(g * hat, axis=-1, keepdims=True)
    )


def core_kernel(
    idx,
    x_ref,
    cot_ref,
    pad_ref,
    doc_ref,
    v_ref,
    edge_ref,
    k1_ref,
    cm_ref,
    line_ref,
    wo0_any,
    wo1_any,
    wu0_any,
    wu1_any,
    wd0_any,
    wd1_any,
    vec_ref,
    out_ref,
    ctx0,
    ctx1,
    nlt_ref,
    act0,
    act1,
    gh2t_ref,
    du0,
    du1,
    gh1_ref,
    gh1t_ref,
    gc_ref,
    acc_ref,
    ext,
    band,
    wo,
    wu,
    wd,
    gp,
    sems,
    *,
    tok,
    shape,
):
    step = pl.program_id(0)
    rows, d = gh1_ref.shape
    half = d // 2
    ga, sa, gf, sf = (vec_ref[i : i + 1, :] for i in range(4))
    loads = [
        pltpu.make_async_copy(src, dst.at[i], sems.at[n])
        for n, (src, dst, i) in enumerate(
            [
                (wo0_any, wo, 0),
                (wo1_any, wo, 1),
                (wu0_any, wu, 0),
                (wu1_any, wu, 1),
                (wd0_any, wd, 0),
                (wd1_any, wd, 1),
            ]
        )
    ]

    def arrived(*which):
        @pl.when(step == 0)
        def _():
            for i in which:
                loads[i].wait()

    @pl.when(step == 0)
    def _():
        for c in loads:
            c.start()
        fill_halo(ext, v_ref, edge_ref, tok)
        fill_bands(line_ref.at[0], band)
        acc_ref[...] = jnp.zeros_like(acc_ref)

    bounds = doc_bounds(doc_ref, idx)
    mask = block_mask()
    start = idx[1] * tok + step * rows
    parts = []
    for sub in range(rows // 128):
        place = start + sub * 128
        same = (
            docs_at(place + iota((128, 1), 0), bounds, LEN)
            == docs_at(place - 64 + iota((1, 256), 1), bounds, LEN)
        ).astype(BF)
        base = pl.multiple_of(step * rows + sub * 128, 128)
        cols = []
        for pair in range(d // 128):
            window = ext[pl.ds(base, 256), pair * 128 : (pair + 1) * 128]
            cols.append(banded(band, window, same, 2 * pair))
        parts.append(jnp.concatenate(cols, axis=1))
    conv = jnp.concatenate(parts, axis=0)
    ctxs = []
    for c in range(d // QUAD):
        cols = slice(c * QUAD, (c + 1) * QUAD)
        att = tn(k1_ref[cols, :], spread_blocks(cm_ref[:, cols], mask))
        ctxs.append((att + conv[:, cols]).astype(BF))
    ctx = jnp.concatenate(ctxs, axis=1)
    ctx0[...] = ctx[:, :half]
    ctx1[...] = ctx[:, half:]
    arrived(0, 1)
    branch = nn(ctx[:, :half], wo[0]) + nn(ctx[:, half:], wo[1])
    xf = x_ref[0].astype(F32)
    hat1, rstd1 = norm_stats(xf + branch)
    normed = hat1 * ga + sa
    nl = normed.astype(BF)
    store_chunks(nlt_ref, nl.T, idx, shape)
    arrived(2, 3)
    chunk = 512
    hidden = wu.shape[2]
    for i, act in ((0, act0), (1, act1)):
        for at in range(0, hidden, chunk):
            cols = slice(at, at + chunk)
            u = nn(nl, wu[i, :, cols])
            cdf, pdf = erf_parts(u)
            act[:, cols] = (u * cdf).astype(BF)
            gp[i, :, cols] = (cdf + u * pdf).astype(BF)
    arrived(4, 5)
    ffn = nn(act0[...], wd[0]) + nn(act1[...], wd[1])
    hat2, rstd2 = norm_stats(normed + ffn)
    out_ref[...] = (hat2 * gf + sf).astype(BF)
    cot = cot_ref[0].astype(F32)
    gh2 = norm_back(cot * gf, hat2, rstd2)
    low = gh2.astype(BF)
    store_chunks(gh2t_ref, low.T, idx, shape)
    for i, du in ((0, du0), (1, du1)):
        for at in range(0, hidden, chunk):
            cols = slice(at, at + chunk)
            du[:, cols] = (nt(low, wd[i, cols, :]) * gp[i, :, cols].astype(F32)).astype(BF)
    gn = gh2 + nt(du0[...], wu[0]) + nt(du1[...], wu[1])
    gh1 = norm_back(gn * ga, hat1, rstd1).astype(BF)
    gh1_ref[...] = gh1
    store_chunks(gh1t_ref, gh1.T, idx, shape)
    gc_ref[:, :half] = nt(gh1, wo[0]).astype(BF)
    gc_ref[:, half:] = nt(gh1, wo[1]).astype(BF)
    keep_n = valid_count(pad_ref, idx) - start
    keep = (iota((rows, 1), 0) < keep_n).astype(F32)
    acc_ref[0:1, :] += jnp.sum(gn * hat1, axis=0, keepdims=True)
    acc_ref[1:2, :] += jnp.sum(gn, axis=0, keepdims=True)
    acc_ref[2:3, :] += jnp.sum(cot * hat2, axis=0, keepdims=True)
    acc_ref[3:4, :] += jnp.sum(cot, axis=0, keepdims=True)
    acc_ref[4:5, :] += jnp.sum(xf * xf * keep, axis=0, keepdims=True)
    acc_ref[5:6, :] += jnp.sum(branch * branch * keep, axis=0, keepdims=True)
    acc_ref[6:7, :] += jnp.sum(ffn * ffn * keep, axis=0, keepdims=True)


def core(idx, inputs, cot, padding, documents, v, edge, k1, cm, lines, wo, wu, wd, vecs, shape):
    tok, d = v.shape
    rows = 256
    f2 = wu[0].shape[1]
    heads = lines.shape[1]
    blk = lambda i, s: (i, 0)
    row = pl.BlockSpec((1, rows, d), lambda i, s: (s[0], i, 0))
    flat = pl.BlockSpec((rows, d), blk)
    part = pl.BlockSpec((rows, d // 2), blk)
    turned = pl.BlockSpec((d, rows), lambda i, s: (0, i))
    wide = pl.BlockSpec((rows, f2), blk)
    full, t = sds((tok, d), BF), sds((d, tok), BF)
    return call(
        functools.partial(core_kernel, tok=tok, shape=shape),
        idx,
        [inputs, cot, padding, documents, v, edge, k1, cm, lines, *wo, *wu, *wd, vecs],
        [row, row]
        + [whole(a.shape) for a in (padding, documents, v, edge)]
        + [turned]
        + [whole(a.shape) for a in (cm, lines)]
        + [ANY] * 6
        + [whole(vecs.shape)],
        [flat, part, part, turned, wide, wide, turned, wide, wide, flat, turned, flat, whole((8, d))],
        [full]
        + [sds((tok, d // 2), BF)] * 2
        + [t]
        + [sds((tok, f2), BF)] * 2
        + [t]
        + [sds((tok, f2), BF)] * 2
        + [full, t, full, sds((8, d), F32)],
        (tok // rows,),
        "core",
        scratch=[
            pltpu.VMEM((tok + 128, d), BF),
            pltpu.VMEM((heads, 128, 256), BF),
            pltpu.VMEM((2, d // 2, d), BF),
            pltpu.VMEM((2, d, f2), BF),
            pltpu.VMEM((2, f2, d), BF),
            pltpu.VMEM((2, rows, f2), BF),
            pltpu.SemaphoreType.DMA((6,)),
        ],
        flops=16 * tok * d * f2,
        moved=60 * tok * d,
        exps=4 * tok * f2,
        limit=60,
    )


def weight_kernel(idx, *refs, pairs, blocks, split):
    ins = refs[: 4 * pairs]
    send_a, keep_a, send_b, keep_b = refs[4 * pairs :]
    step = pl.program_id(0)
    d = ins[0].shape[0]
    q = d // 4

    def product(which):
        lhs, rhs = ins[: 2 * pairs], ins[2 * pairs :]
        at = 2 * which if pairs == 2 else 0
        return (nn(lhs[at][...], rhs[at][...]) + nn(lhs[at + 1][...], rhs[at + 1][...])).astype(BF)

    @pl.when(step < blocks)
    def _():
        acc = product(0)
        keep_a[...] = acc[: 2 * q]
        send_a[...] = acc[2 * q :]

    @pl.when(step >= blocks)
    def _():
        acc = product(1)
        keep_b[:q] = acc[:q]
        send_b[:q] = acc[q : 2 * q]
        keep_b[q:] = acc[2 * q : 3 * q]
        send_b[q:] = acc[3 * q :]


def weight_grads(idx, lhs, rhs, width, deps=()):
    pairs = len(lhs)
    d, tok = lhs[0][0].shape
    cols = rhs[0][0].shape[1] // (1 if pairs == 2 else 2)
    blocks = cols // width
    args = [a for pair in lhs for a in pair] + [a for pair in rhs for a in pair]
    specs = [whole((d, tok))] * (2 * pairs)
    if pairs == 1:
        specs += [pl.BlockSpec((tok, width), lambda j, s: (0, j))] * 2
    else:
        specs += [pl.BlockSpec((tok, width), lambda j, s: (0, jnp.minimum(j, blocks - 1)))] * 2
        specs += [pl.BlockSpec((tok, width), lambda j, s: (0, jnp.maximum(j - blocks, 0)))] * 2
    first = pl.BlockSpec((d // 2, width), lambda j, s: (0, jnp.minimum(j, blocks - 1)))
    second = pl.BlockSpec((d // 2, width), lambda j, s: (0, jnp.maximum(j - blocks, 0)))
    if pairs == 1:
        kernel = functools.partial(weight_kernel, pairs=1, blocks=blocks, split=False)
    else:
        kernel = functools.partial(weight_kernel, pairs=2, blocks=blocks, split=True)
    return call(
        kernel,
        idx,
        args,
        specs,
        [first, first, second, second],
        [sds((d // 2, cols), BF)] * 4,
        (2 * blocks,),
        "weights",
        flops=8 * tok * d * cols,
        moved=8 * tok * cols,
        deps=deps,
    )


def halving(size, bit):
    return [(i, i ^ bit) for i in range(size)]


def first_add_kernel(idx, ka, ra, kb, rb, sa, ma, sb, mb):
    q = sa.shape[0]
    for keep, got, send, mine in ((ka, ra, sa, ma), (kb, rb, sb, mb)):
        mine[...] = (keep[:q].astype(F32) + got[:q].astype(F32)).astype(BF)
        send[...] = (keep[q:].astype(F32) + got[q:].astype(F32)).astype(BF)


def first_add(idx, arrays, deps=()):
    rows, n = arrays[0].shape
    out = sds((rows // 2, n), BF)
    return call(
        first_add_kernel,
        idx,
        arrays,
        [whole((rows, n))] * 4,
        [whole((rows // 2, n))] * 4,
        [out] * 4,
        (1,),
        "first_add",
        moved=12 * rows * n,
        deps=deps,
    )


def second_add_kernel(idx, ka, ra, kb, rb, *outs):
    n = ka.shape[1]
    ch = outs[0].shape[0]
    for at, keep, got in ((0, ka, ra), (n, kb, rb)):
        for p, out in enumerate(outs):
            r = slice(p * ch, (p + 1) * ch)
            out[:, at : at + n] = (keep[r].astype(F32) + got[r].astype(F32)).astype(BF)


def second_add(idx, arrays, parts, deps=()):
    rows, n = arrays[0].shape
    shape = (rows // parts, 2 * n)
    return call(
        second_add_kernel,
        idx,
        arrays,
        [whole((rows, n))] * 4,
        [whole(shape)] * parts,
        [sds(shape, BF)] * parts,
        (1,),
        "second_add",
        moved=12 * rows * n,
        deps=deps,
    )


class Reducer:
    def __init__(self, idx, parts, fast):
        self.idx, self.fast = idx, fast
        self.seq, self.dp = lax.axis_size("seq"), lax.axis_size("dp")
        self.parts = parts
        if fast:
            self.got = (self.send(parts[0], 1), self.send(parts[2], 2))

    def send(self, a, bit, axis="seq"):
        return lax.ppermute(a, axis, halving(lax.axis_size(axis), bit))

    def step1(self, deps=()):
        if not self.fast:
            return ()
        _, ka, _, kb = self.parts
        sa, ma, sb, mb = first_add(self.idx, [ka, self.got[0], kb, self.got[1]], deps)
        self.mine = (ma, mb)
        self.got = (self.send(sa, 2), self.send(sb, 1))
        return (ma,)

    def step2(self, deps=()):
        if not self.fast:
            return ()
        c = second_add(self.idx, [self.mine[0], self.got[0], self.mine[1], self.got[1]], self.dp, deps)
        self.own = c[0]
        self.got = [self.send(c[p], p, "dp") for p in range(1, self.dp)]
        return (c[0],)

    def finish(self):
        if self.fast:
            out = self.own.astype(F32)
            for g in self.got:
                out = out + g.astype(F32)
            return out
        sa, ka, sb, kb = self.parts
        q = ka.shape[0] // 2
        b = jnp.concatenate([kb[:q], sb[:q], kb[q:], sb[q:]], axis=0)
        full = jnp.concatenate([jnp.concatenate([ka, sa], axis=0), b], axis=1).astype(F32)
        part = lax.psum_scatter(full, "dp", scatter_dimension=0, tiled=True)
        return lax.psum_scatter(part, "seq", scatter_dimension=0, tiled=True)


def first_kernel(idx, q_ref, k1_ref, gc_ref, cm_ref, marks_ref, gq_ref, mix_ref, km_ref, *, tok):
    n = marks_ref.shape[0]
    lm = tok // M
    mask = block_mask()
    km = spread_blocks(
        jnp.concatenate([marks_ref[i, lm : 2 * lm, :] for i in range(n)], axis=0), mask
    )
    gc = gc_ref[...]
    k1 = k1_ref[...]
    mix_ref[...] = gather_blocks(nn(k1, gc)).astype(BF)
    g = nt(spread_blocks(cm_ref[...], mask), gc).reshape(QUAD // M, M, tok)
    kf = k1.astype(F32).reshape(QUAD // M, M, tok)
    inner = jnp.sum(g * kf, axis=1, keepdims=True)
    g1 = (kf * (g - inner)).reshape(QUAD, tok).astype(BF)
    gq_ref[...] = (tn(g1, km) * 0.125).astype(BF)
    km_ref[...] = gather_blocks(nn(g1, q_ref[...])) * 0.125


def first_back(idx, q, k1, gc, cm, marks, deps=()):
    tok, d = q.shape
    n = marks.shape[0]
    lane = lambda i, s: (0, i)
    flat, mark = pl.BlockSpec((tok, QUAD), lane), pl.BlockSpec((M, QUAD), lane)
    return call(
        functools.partial(first_kernel, tok=tok),
        idx,
        [q, k1, gc, cm, marks],
        [
            flat,
            pl.BlockSpec((QUAD, tok), lambda i, s: (i, 0)),
            flat,
            mark,
            pl.BlockSpec((n, marks.shape[1], QUAD), lambda i, s: (0, 0, i)),
        ],
        [flat, mark, mark],
        [sds((tok, d), BF), sds((M, d), BF), sds((M, d), F32)],
        (d // QUAD,),
        "first_back",
        flops=8 * tok * d * QUAD,
        moved=8 * tok * d,
        deps=deps,
    )


def middle_kernel(idx, gmix_ref, lv_ref, inv_ref, gst_ref, gm_ref, gt_ref):
    n = gmix_ref.shape[0]
    d = lv_ref.shape[1]
    mask = block_mask()
    lane = iota((M, 128), 1)
    head = iota((M, QUAD), 1) // M
    stat = gst_ref[...]
    gt = jnp.zeros((M, 128), F32)
    for c in range(d // QUAD):
        cols = slice(c * QUAD, (c + 1) * QUAD)
        gmix = jnp.zeros((M, QUAD), F32)
        for i in range(n):
            gmix = gmix + gmix_ref[i, :, cols].astype(F32)
        glv = gather_blocks(
            three(tn, spread_blocks(inv_ref[:, cols], mask), spread_blocks(gmix, mask))
        )
        scale = per_head(stat, 0, c)
        total = per_head(stat, 64, c)
        gm_ref[:, cols] = ((glv / total).astype(BF).astype(F32) * scale).astype(BF)
        prod = glv * lv_ref[:, cols]
        for h in range(QUAD // M):
            at = c * (QUAD // M) + h
            s = jnp.sum(jnp.where(head == h, prod, 0.0), axis=1, keepdims=True)
            gt = jnp.where(lane == at, -s / stat[:, 64 + at : 65 + at] * stat[:, at : at + 1], gt)
    gt_ref[...] = gt


def middle(idx, gmix, lv, inv, gst):
    d = lv.shape[1]
    return pl.pallas_call(
        middle_kernel,
        grid_spec=pltpu.PrefetchScalarGridSpec(
            num_scalar_prefetch=1,
            grid=(1,),
            in_specs=[whole(gmix.shape), whole(lv.shape), whole(inv.shape), whole(gst.shape)],
            out_specs=[whole((M, d)), whole((M, 128))],
        ),
        out_shape=[sds((M, d), BF), sds((M, 128), F32)],
        compiler_params=params(),
        name="middle",
    )(idx, gmix, lv, inv, gst)


def pinv_back_kernel(idx, gmix_ref, lv_ref, k2_ref, save_ref, marks_ref, out_ref, *, lm):
    n = gmix_ref.shape[0]
    mask = block_mask()
    ident = (iota((QUAD, QUAD), 0) == iota((QUAD, QUAD), 1)).astype(F32)
    gmix = jnp.zeros((M, QUAD), F32)
    for i in range(n):
        gmix = gmix + gmix_ref[i].astype(F32)
    dz = three(nt, spread_blocks(gmix, mask), spread_blocks(lv_ref[...], mask))
    kernel = spread_blocks(k2_ref[...], mask)
    klow = kernel.astype(BF)
    dk = jnp.zeros((QUAD, QUAD), F32)
    ibf = ident.astype(BF)
    for it in range(ITERS - 1, -1, -1):
        z, p, i2, i3 = (save_ref[it, kind] for kind in range(4))
        i1 = 7.0 * ibf - p
        dlow = dz.astype(BF)
        d3 = (0.25 * tn(z, dlow)).astype(BF)
        dp = nt(d3, i2)
        d2 = (-tn(p, d3)).astype(BF)
        dp = dp + nt(d2, i1)
        d1 = -tn(p, d2)
        dp = (-dp - d1).astype(BF)
        dz = 0.25 * nt(dlow, i3) + tn(klow, dp)
        dk = dk + nt(dp, z)
    sums = jnp.sum(kernel, axis=0, keepdims=True)
    lane = iota((1, QUAD), 1) // M
    dzt = jnp.where(mask, dz, 0.0).T
    dsum = jnp.sum(dzt * kernel, axis=0, keepdims=True)
    scale = jnp.zeros((1, QUAD), F32)
    extra = jnp.zeros((1, QUAD), F32)
    for h in range(QUAD // M):
        mine = lane == h
        best = jnp.max(jnp.where(mine, sums, 0.0), axis=1, keepdims=True)
        dscale = jnp.sum(jnp.where(mine, dsum, 0.0), axis=1, keepdims=True)
        is_best = (mine & (sums == best)).astype(F32)
        share = is_best / jnp.sum(is_best, axis=1, keepdims=True)
        scale = jnp.where(mine, 1.0 / best, scale)
        extra = jnp.where(mine, -dscale / (best * best) * share, extra)
    dk = dk + dzt * scale + extra
    inner = jnp.sum(jnp.where(mask, dk * kernel, 0.0), axis=1, keepdims=True)
    g2 = kernel * (dk - inner)
    qm = jnp.concatenate([marks_ref[i, 0:lm, :] for i in range(n)], axis=0)
    km = jnp.concatenate([marks_ref[i, lm : 2 * lm, :] for i in range(n)], axis=0)
    g2h, g2l = split(g2)
    kb, qb = spread_blocks(km, mask), spread_blocks(qm, mask)
    use = (idx[1] < idx[3]).astype(F32) * 0.125
    out_ref[0] = gather_blocks(nn(g2h, kb) + nn(g2l, kb)) * use
    out_ref[1] = gather_blocks(tn(g2h, qb) + tn(g2l, qb)) * use


def pinv_back(idx, gmix, lv, k2, save, marks, lm, deps=()):
    n, _, d = gmix.shape
    last = d // QUAD - 1
    col = lambda i, s: (0, jnp.minimum(s[1], last))
    col3 = lambda i, s: (0, 0, jnp.minimum(s[1], last))
    return call(
        functools.partial(pinv_back_kernel, lm=lm),
        idx,
        [gmix, lv, k2, save, marks],
        [
            pl.BlockSpec((n, M, QUAD), col3),
            pl.BlockSpec((M, QUAD), col),
            pl.BlockSpec((M, QUAD), col),
            whole(save.shape),
            pl.BlockSpec((n, marks.shape[1], QUAD), col3),
        ],
        whole((2, M, QUAD)),
        sds((2, M, QUAD), F32),
        (1,),
        "pinv_back",
        flops=48 * 2 * QUAD**3,
        moved=4 * 10**6,
        deps=deps,
    )


def second_kernel(
    idx, k_ref, v_ref, vedge_ref, gc_ref, gedge_ref, e_ref, gm_ref, gt_ref, marks_ref, doc_ref,
    pad_ref, taps_ref, gk_ref, gv_ref, qm_ref, gtap_ref, vext, gext, band, *, tok, half,
):
    quad = pl.program_id(0)
    n = marks_ref.shape[0]
    lm = tok // M
    heads = QUAD // M
    mask = block_mask()
    qm = spread_blocks(
        jnp.concatenate([marks_ref[i, 0:lm, :] for i in range(n)], axis=0), mask
    )
    gm = spread_blocks(gm_ref[...], mask)
    lane = iota((M, 128), 1)
    cols = []
    for h in range(heads):
        pick = jnp.where(lane == quad * heads + h, gt_ref[...], 0.0)
        cols.append(jnp.sum(pick, axis=1, keepdims=True))
    gt = jnp.concatenate(cols, axis=0)
    e = e_ref[...]
    g3 = (e.astype(F32) * (nt(gm, v_ref[...]) + gt)).astype(BF)
    qm_ref[...] = gather_blocks(nn(g3, k_ref[...])) * 0.125
    gk_ref[...] = (tn(g3, qm) * 0.125).astype(BF)
    gv = tn(e, gm)
    fill_halo(vext, v_ref, vedge_ref, tok)
    fill_halo(gext, gc_ref, gedge_ref, tok)
    fill_bands(taps_ref.at[0, 0], band)
    bounds = doc_bounds(doc_ref, idx)
    start = idx[1] * tok
    keep_n = valid_count(pad_ref, idx) - start
    col64 = iota((128, 128), 1)
    pairs = [jnp.zeros((128, 256), F32) for _ in range(heads)]
    for sub in range(tok // 128):
        place = start + sub * 128
        same = (
            docs_at(place + iota((128, 1), 0), bounds, LEN)
            == docs_at(place - 64 + iota((1, 256), 1), bounds, LEN)
        )
        low = same.astype(BF)
        keep = iota((128, 1), 0) < keep_n - sub * 128
        at = slice(sub * 128, sub * 128 + 128)
        for pair in range(heads // 2):
            lanes = slice(pair * 128, pair * 128 + 128)
            back = banded(band, gext[sub * 128 : sub * 128 + 256, lanes], low, 2 * pair)
            gv_ref[at, lanes] = jnp.where(keep, gv[at, lanes] + back, 0.0).astype(BF)
            g = gc_ref[at, lanes]
            win = vext[sub * 128 : sub * 128 + 256, lanes]
            for h in range(2):
                own = jnp.where((col64 < 64) == (h == 0), g, jnp.zeros((), BF))
                pairs[2 * pair + h] += jnp.where(same, nt(own, win), 0.0)
    gap = iota((128, 256), 1) - iota((128, 256), 0) - 64 + half
    out = jnp.zeros((8, 128), F32)
    line, lane8 = iota((8, 128), 0), iota((8, 128), 1)
    for h in range(heads):
        for o in range(2 * half + 1):
            val = jnp.sum(jnp.where(gap == o, pairs[h], 0.0))
            out = jnp.where((line == h) & (lane8 == o), val, out)
    gtap_ref[0] = out


def second_back(idx, k, v, vedge, gc, gedge, e, gm, gt, marks, documents, padding, lines, half, deps=()):
    tok, d = k.shape
    n = marks.shape[0]
    heads = QUAD // M
    lane = lambda i, s: (0, i)
    flat, edge = pl.BlockSpec((tok, QUAD), lane), pl.BlockSpec((32, QUAD), lane)
    taps3 = lines[1].reshape(d // QUAD, 1, heads, lines.shape[2])
    gk, gv, gqm, gtap = call(
        functools.partial(second_kernel, tok=tok, half=half),
        idx,
        [k, v, vedge, gc, gedge, e, gm, gt, marks, documents, padding, taps3],
        [
            flat,
            flat,
            edge,
            flat,
            edge,
            pl.BlockSpec((QUAD, tok), lambda i, s: (i, 0)),
            pl.BlockSpec((M, QUAD), lane),
            whole(gt.shape),
            pl.BlockSpec((n, marks.shape[1], QUAD), lambda i, s: (0, 0, i)),
            whole(documents.shape),
            whole(padding.shape),
            pl.BlockSpec((1, 1, heads, lines.shape[2]), lambda i, s: (i, 0, 0, 0)),
        ],
        [
            flat,
            flat,
            pl.BlockSpec((M, QUAD), lane),
            pl.BlockSpec((1, 8, 128), lambda i, s: (i, 0, 0)),
        ],
        [
            sds((tok, d), BF),
            sds((tok, d), BF),
            sds((M, d), F32),
            sds((d // QUAD, 8, 128), F32),
        ],
        (d // QUAD,),
        "second_back",
        scratch=[
            pltpu.VMEM((tok + 128, QUAD), BF),
            pltpu.VMEM((tok + 128, QUAD), BF),
            pltpu.VMEM((heads, 128, 256), BF),
        ],
        flops=16 * tok * d * QUAD,
        moved=12 * tok * d,
        deps=deps,
    )
    return gk, gv[:, : d // 2], gv[:, d // 2 :], gqm, gtap


def spread_kernel(idx, gq_ref, gk_ref, got_ref, pad_ref, dq0, dq1, dk0, dk1, *, tok):
    n = got_ref.shape[0]
    lm = tok // M
    half = dq0.shape[1]
    got = got_ref[0].astype(F32)
    for i in range(1, n):
        got = got + got_ref[i].astype(F32)
    keep_n = valid_count(pad_ref, idx) - idx[1] * tok
    for j in range(lm):
        rows = slice(j * M, (j + 1) * M)
        keep = (iota((M, 1), 0) < keep_n - j * M).astype(F32)
        share = keep / jnp.maximum(jnp.sum(keep, axis=0, keepdims=True), 1.0)
        for at, src, outs in ((0, gq_ref, (dq0, dq1)), (lm, gk_ref, (dk0, dk1))):
            val = (src[rows].astype(F32) + got[at + j : at + j + 1] * share).astype(BF)
            outs[0][rows] = val[:, :half]
            outs[1][rows] = val[:, half:]


def spread(idx, gq, gk, got, padding):
    tok, d = gq.shape
    return call(
        functools.partial(spread_kernel, tok=tok),
        idx,
        [gq, gk, got, padding],
        [whole(gq.shape), whole(gk.shape), whole(got.shape), whole(padding.shape)],
        [whole((tok, d // 2))] * 4,
        [sds((tok, d // 2), BF)] * 4,
        (1,),
        "spread",
        moved=8 * tok * d,
    )


def inputs_kernel(
    idx, gh1_ref, dq0, dq1, dk0, dk1, dv0, dv1, q0, q1, k0, k1, v0, v1, out0, out1, cat, res
):
    half = dq0.shape[1]

    @pl.when(pl.program_id(0) == 0)
    def _():
        for i, w in enumerate((q0, q1, k0, k1, v0, v1)):
            cat[:, i * half : (i + 1) * half] = w[...]

    lhs = jnp.concatenate([a[...] for a in (dq0, dq1, dk0, dk1, dv0, dv1)], axis=1)
    res[...] = gh1_ref[...].astype(F32) + nt(lhs, cat[...])
    own = pl.multiple_of(idx[0] * half, half)
    other = pl.multiple_of((1 - idx[0]) * half, half)
    out0[...] = res[:, pl.ds(own, half)].astype(BF)
    out1[...] = res[:, pl.ds(other, half)].astype(BF)


def inputs_grad(idx, gh1, dq, dk, dv, wq, wk, wv, deps=()):
    tok, d = gh1.shape
    half = d // 2
    rows = 256
    blk = lambda i, s: (i, 0)
    part = pl.BlockSpec((rows, half), blk)
    return call(
        inputs_kernel,
        idx,
        [gh1, *dq, *dk, *dv, *wq, *wk, *wv],
        [pl.BlockSpec((rows, d), blk)] + [part] * 6 + [whole((d, half))] * 6,
        [part] * 2,
        [sds((tok, half), BF)] * 2,
        (tok // rows,),
        "inputs_grad",
        scratch=[pltpu.VMEM((d, 3 * d), BF), pltpu.VMEM((rows, d), F32)],
        flops=6 * tok * d * d,
        moved=12 * tok * d,
        deps=deps,
    )


def place_kernel(idx, own_ref, other_ref, out_ref):
    @pl.when(pl.program_id(0) == 0)
    def _():
        out_ref[0] = own_ref[...]

    @pl.when(pl.program_id(0) == 1)
    def _():
        out_ref[0] = other_ref[...]


def place_rows(idx, own, other, name, deps=()):
    tok, d = own.shape
    steps = 2
    rows = tok // steps
    return call(
        place_kernel,
        idx,
        [own, other],
        [
            pl.BlockSpec((rows, d), lambda j, i, s: (jnp.where(j == 0, i, steps - 1), 0)),
            pl.BlockSpec((rows, d), lambda j, i, s: (jnp.where(j == 0, 0, i), 0)),
        ],
        pl.BlockSpec((1, rows, d), lambda j, i, s: (s[0] ^ j, i, 0)),
        sds((2, tok, d), own.dtype),
        (2, steps),
        name,
        moved=8 * tok * d,
        deps=deps,
    )


def shards(
    inputs,
    cotangent,
    padding,
    documents,
    w_query,
    w_key,
    w_value,
    w_out,
    w_up,
    w_down,
    conv_taps,
    gain_attn,
    shift_attn,
    gain_ffn,
    shift_ffn,
):
    row_count, tok, d = inputs.shape
    half = d // 2
    heads = conv_taps.shape[0]
    seq_n, dp_n = lax.axis_size("seq"), lax.axis_size("dp")
    mp, seq, dp = lax.axis_index("mp"), lax.axis_index("seq"), lax.axis_index("dp")
    lm = tok // M
    chunk = d // (seq_n * dp_n)
    fast = seq_n == 4 and dp_n == 4 and chunk % 16 == 0
    shape = (dp_n if fast else 0, seq_n, chunk)
    idx = jnp.stack(
        [mp, seq, dp, jnp.full((), min(d // QUAD, seq_n), jnp.int32)]
    ).astype(jnp.int32)

    def swap(a):
        return lax.ppermute(a, "mp", [(0, 1), (1, 0)])

    def pair(a):
        return (a, swap(a))

    wq, wk, wv = pair(w_query), pair(w_key), pair(w_value)
    wo, wu, wd = pair(w_out), pair(w_up), pair(w_down)
    lines = tap_lines(jnp.concatenate(pair(conv_taps), axis=0))
    vecs = jnp.stack([gain_attn, shift_attn, gain_ffn, shift_ffn])
    q, k, v, xt, k1, e, save, marks, vedge, cm, lv, gst, inv, k2 = attend(
        seq_n, inputs, padding, (*wq, *wk, *wv), shape
    )
    xts = pair(xt)
    out_own, ctx0, ctx1, nlt, act0, act1, gh2t, du0, du1, gh1, gh1t, gc, acc = core(
        idx, inputs, cotangent, padding, documents, v, vedge, k1, cm, lines, wo, wu, wd, vecs, shape
    )
    act_got, gh2ts, du_got, nlts = swap(act1), pair(gh2t), swap(du1), pair(nlt)
    out_got = swap(out_own)
    gh1ts, ctx_got = pair(gh1t), swap(ctx1)
    gq, gmix, gkm = first_back(idx, q, k1, gc, cm, marks)
    down = Reducer(idx, weight_grads(idx, [gh2ts], [(act0, act_got)], 256, (gq,)), fast)
    up = Reducer(
        idx, weight_grads(idx, [nlts], [(du0, du_got)], 256, (down.parts[1],)), fast
    )
    dep = down.step1((up.parts[1],))
    gedge_own = jnp.concatenate([gc[:16], gc[tok - 16 :]], axis=0)
    gmixes, gedge = gather_seq(seq_n, [gmix], gedge_own, 3, dep)
    gm, gt = middle(idx, gmixes, lv, inv, gst)
    dep = down.step2((gm,))
    gk, gv0, gv1, gqm, gtap = second_back(
        idx, k, v, vedge, gc, gedge, e, gm, gt, marks, documents, padding, lines,
        conv_taps.shape[1] // 2, dep
    )
    gv_got = swap(gv1)
    dep = up.step1((gk,))
    two = pinv_back(idx, gmixes, lv, k2, save, marks, lm, dep)
    ov = Reducer(
        idx, weight_grads(idx, [gh1ts, xts], [(ctx0, ctx_got), (gv0, gv_got)], half, (two,)), fast
    )
    at = jnp.minimum(seq, d // QUAD - 1) * QUAD
    gqm = gqm + lax.dynamic_update_slice(jnp.zeros((M, d), F32), two[0], (0, at))
    gkm = gkm + lax.dynamic_update_slice(jnp.zeros((M, d), F32), two[1], (0, at))
    both = jnp.concatenate(
        [gqm.reshape(seq_n, lm, d), gkm.reshape(seq_n, lm, d)], axis=1
    ).astype(BF)
    squares = jnp.sum(acc[4:7], axis=1, keepdims=True)
    small = jnp.concatenate(
        [
            acc[:4].reshape(-1, 128),
            gtap.reshape(-1, 128),
            jnp.broadcast_to(jnp.pad(squares, ((0, 5), (0, 0))), (8, 128)),
        ],
        axis=0,
    )
    dep = up.step2((ov.parts[1],))
    got, smalls = scatter_seq(seq_n, both, small, 4, dep)
    small = jnp.sum(smalls, axis=0)
    dq0, dq1, dk0, dk1 = spread(idx, gq, gk, got, padding)
    dq_got, dk_got = swap(dq1), swap(dk1)
    dep = ov.step1((dq0,))
    qk = Reducer(
        idx, weight_grads(idx, [xts, xts], [(dq0, dq_got), (dk0, dk_got)], half, dep), fast
    )
    gin0, gin1 = inputs_grad(
        idx, gh1, (dq0, dq1), (dk0, dk1), (gv0, gv1), wq, wk, wv, (qk.parts[1],)
    )
    gin_got = swap(gin1)
    dep = ov.step2((gin0,))
    dep = qk.step1(dep)
    qk.step2()
    sum_down, sum_up, sum_ov, sum_qk = down.finish(), up.finish(), ov.finish(), qk.finish()

    small_got = swap(small)
    n = 2 * d // 128
    total = small + small_got
    norms = total[: 2 * n]
    own_taps = small[2 * n : 2 * n + 24].reshape(3, 8, 128)[:, : QUAD // M].reshape(2, heads, 128)
    got_taps = small_got[2 * n : 2 * n + 24].reshape(3, 8, 128)[:, : QUAD // M].reshape(2, heads, 128)
    tap_sum = own_taps[0] + got_taps[1]
    rest = jnp.concatenate([norms, tap_sum], axis=0)
    if fast:
        rest = rest + sum(lax.ppermute(rest, "dp", halving(dp_n, p)) for p in range(1, dp_n))
    else:
        rest = lax.psum(rest, "dp")
    norms = rest[: 2 * n].reshape(4, d)
    tap_total = rest[2 * n :, : conv_taps.shape[1]]
    own_sq, got_sq = small[-8:-5, 0], small_got[-8:-5, 0]
    own_squares = jnp.where(mp == 0, jnp.stack([own_sq, got_sq]), jnp.stack([got_sq, own_sq]))
    row_valid = jnp.sum(padding.astype(F32), axis=1)
    row_rms = jnp.sqrt(own_squares / (row_valid[:, None] * d) + 1e-06)
    return (
        place_rows(idx, out_own, out_got, "outputs", dep),
        place_rows(idx, gin0, gin_got, "grad_inputs"),
        sum_qk[:, :half],
        sum_qk[:, half:],
        sum_ov[:, half:],
        sum_ov[:, :half].T,
        sum_up,
        sum_down.T,
        tap_total,
        norms[0],
        norms[1],
        norms[2],
        norms[3],
        row_rms,
    )


def solution(mesh):
    return jax.shard_map(
        shards,
        mesh=mesh,
        in_specs=(
            P("dp", "seq", None),
            P("dp", "seq", None),
            P("dp", None),
            P("dp", None),
            P(None, "mp"),
            P(None, "mp"),
            P(None, "mp"),
            P("mp", None),
            P(None, "mp"),
            P("mp", None),
            P("mp", None),
            P(),
            P(),
            P(),
            P(),
        ),
        out_specs=(
            P("dp", "seq", None),
            P("dp", "seq", "mp"),
            P(("dp", "seq"), "mp"),
            P(("dp", "seq"), "mp"),
            P(("dp", "seq"), "mp"),
            P("mp", ("dp", "seq")),
            P(("dp", "seq"), "mp"),
            P("mp", ("dp", "seq")),
            P("mp", None),
            P(),
            P(),
            P(),
            P(),
            P("dp", None),
        ),
        check_vma=False,
    )
```

```python
import functools

import jax
import jax.numpy as jnp
from jax import lax
from jax.experimental import pallas as pl
from jax.experimental.pallas import tpu as pltpu
from jax.sharding import PartitionSpec as P

M = 64
ITERS = 6
LEN = 4096
QUAD = 256
MESH = pl.DeviceIdType.MESH
F32 = jnp.float32
BF = jnp.bfloat16
EPS = 1e-05


def nn(a, b):
    return lax.dot_general(a, b, (((1,), (0,)), ((), ())), preferred_element_type=F32)


def nt(a, b):
    return lax.dot_general(a, b, (((1,), (1,)), ((), ())), preferred_element_type=F32)


def tn(a, b):
    return lax.dot_general(a, b, (((0,), (0,)), ((), ())), preferred_element_type=F32)


def split(a):
    high = a.astype(BF)
    return high, (a - high.astype(F32)).astype(BF)


def three(dot, a, b):
    ah, al = split(a)
    bh, bl = split(b)
    return dot(ah, bh) + (dot(ah, bl) + dot(al, bh))


def iota(shape, dim):
    return lax.broadcasted_iota(jnp.int32, shape, dim)


def block_mask():
    return iota((QUAD, QUAD), 0) // M == iota((QUAD, QUAD), 1) // M


def spread_blocks(x, mask):
    return jnp.where(mask, jnp.concatenate([x] * (QUAD // M), axis=0), jnp.zeros((), x.dtype))


def gather_blocks(y):
    lane = iota((M, QUAD), 1) // M
    out = jnp.zeros((M, QUAD), y.dtype)
    for h in range(QUAD // M):
        out = out + jnp.where(lane == h, y[h * M : (h + 1) * M], 0.0)
    return out


def params(limit=56, **kw):
    return pltpu.CompilerParams(vmem_limit_bytes=limit * 1024 * 1024, **kw)


def whole(shape):
    nd = len(shape)
    return pl.BlockSpec(shape, lambda *a: (0,) * nd)


def sds(shape, dtype):
    return jax.ShapeDtypeStruct(shape, dtype)


ANY = pl.BlockSpec(memory_space=pl.ANY)


def call(kernel, idx, args, in_specs, out_specs, out_shape, grid, name, scratch=(), flops=0, moved=0, exps=0, deps=(), limit=56):
    nd = len(deps)

    def body(idx_ref, *refs):
        kernel(idx_ref, *refs[nd:])

    return pl.pallas_call(
        body,
        grid_spec=pltpu.PrefetchScalarGridSpec(
            num_scalar_prefetch=1,
            grid=grid,
            in_specs=[ANY] * nd + list(in_specs),
            out_specs=out_specs,
            scratch_shapes=list(scratch),
        ),
        out_shape=out_shape,
        compiler_params=params(limit),
        cost_estimate=pl.CostEstimate(flops=flops, bytes_accessed=moved, transcendentals=exps),
        name=name,
    )(idx, *deps, *args)


def store_chunks(out_ref, t, idx, shape):
    z, sq, chunk = shape
    if z == 0:
        out_ref[...] = t
        return
    for zr in range(z):
        for sr in range(sq):
            b = idx[1] ^ sr
            place = ((b & 1) * 2 + (b >> 1)) * z + (idx[2] ^ zr)
            src = (zr * sq + sr) * chunk
            out_ref[pl.ds(pl.multiple_of(place * chunk, chunk), chunk), :] = t[src : src + chunk]


def valid_count(pad_ref, idx_ref):
    row = pad_ref[pl.ds(idx_ref[0], 1), :].astype(F32)
    return jnp.sum(row, axis=1, keepdims=True).astype(jnp.int32)


def per_head(stat, base, c):
    lane = iota((M, QUAD), 1) // M
    out = jnp.zeros((M, QUAD), F32)
    for h in range(QUAD // M):
        at = base + c * (QUAD // M) + h
        out = jnp.where(lane == h, stat[:, at : at + 1], out)
    return out


def places():
    return [lax.axis_index(a) for a in ("mp", "seq", "dp")]


def greet(sizes):
    barrier = pltpu.get_barrier_semaphore()
    for axis, size in sizes.items():
        me = lax.axis_index(axis)
        for p in range(1, size):
            pl.semaphore_signal(
                barrier, inc=1, device_id={axis: lax.rem(me + p, size)}, device_id_type=MESH
            )
    return lambda: pl.semaphore_wait(barrier, sum(sizes.values()) - len(sizes))


def remote(src, dst, send, recv, axis, to):
    return pltpu.make_async_remote_copy(
        src_ref=src,
        dst_ref=dst,
        send_sem=send,
        recv_sem=recv,
        device_id={axis: to},
        device_id_type=MESH,
    )


def score_quad(c, q_ref, k_ref, v_ref, qm, km, minus, k1_ref, e_ref, mix_ref, stat):
    cols = slice(c * QUAD, (c + 1) * QUAD)
    tok = q_ref.shape[0]
    mask = block_mask()
    s1 = nt(spread_blocks(km[:, cols], mask), q_ref[:, cols]) * 0.125
    s1 = s1.reshape(QUAD // M, M, tok)
    e1 = jnp.exp(s1 - jnp.max(s1, axis=1, keepdims=True))
    k1 = e1 * (1.0 / jnp.sum(e1, axis=1, keepdims=True))
    k1_ref[cols, :] = k1.reshape(QUAD, tok).astype(BF)
    s3 = nt(spread_blocks(qm[:, cols], mask), k_ref[:, cols]) * 0.125 - minus
    top = jnp.max(s3, axis=1, keepdims=True)
    e3 = jnp.exp(s3 - top)
    total = jnp.sum(e3, axis=1, keepdims=True)
    e3 = e3.astype(BF)
    e_ref[cols, :] = e3
    mix_ref[:, cols] = gather_blocks(nn(e3, v_ref[:, cols])).astype(BF)
    lane = iota((M, 128), 1)
    for h in range(QUAD // M):
        at = c * (QUAD // M) + h
        stat = jnp.where(lane == at, top[h * M : (h + 1) * M], stat)
        stat = jnp.where(lane == 64 + at, total[h * M : (h + 1) * M], stat)
    return stat


def pseudo_inverse(qm, km, k2_ref, inv_ref, save_ref, sel):
    d = qm.shape[1]
    quads = d // QUAD
    mask = block_mask()
    ident = (iota((QUAD, QUAD), 0) == iota((QUAD, QUAD), 1)).astype(F32)
    kernel, z = [], []
    for c in range(quads):
        cols = slice(c * QUAD, (c + 1) * QUAD)
        s2 = nt(spread_blocks(qm[:, cols], mask), spread_blocks(km[:, cols], mask)) * 0.125
        s2 = jnp.where(mask, s2, -1e30)
        e2 = jnp.exp(s2 - jnp.max(s2, axis=1, keepdims=True))
        e2 = e2 / jnp.sum(e2, axis=1, keepdims=True)
        kernel.append(e2)
        sums = jnp.sum(e2, axis=0, keepdims=True)
        lane = iota((1, QUAD), 1) // M
        scale = jnp.zeros((1, QUAD), F32)
        for h in range(QUAD // M):
            best = jnp.max(jnp.where(lane == h, sums, 0.0), axis=1, keepdims=True)
            scale = jnp.where(lane == h, 1.0 / best, scale)
        z.append(e2.T * scale)
        k2_ref[:, cols] = gather_blocks(e2)

    def keep(it, kind, vals):
        for c in range(quads):

            @pl.when(sel == c)
            def _():
                save_ref[it, kind] = vals[c].astype(BF)

    ksp = [split(a) for a in kernel]

    def mul(a, b):
        return nn(a[0], b[0]) + (nn(a[0], b[1]) + nn(a[1], b[0]))

    for it in range(ITERS):
        zs = [split(a) for a in z]
        p = [mul(a, b) for a, b in zip(ksp, zs)]
        ps = [split(a) for a in p]
        i2 = [15.0 * ident - mul(a, split(7.0 * ident - b)) for a, b in zip(ps, p)]
        i3 = [13.0 * ident - mul(a, split(b)) for a, b in zip(ps, i2)]
        keep(it, 0, z)
        keep(it, 1, p)
        keep(it, 2, i2)
        keep(it, 3, i3)
        z = [0.25 * mul(a, split(b)) for a, b in zip(zs, i3)]
    for c in range(quads):
        inv_ref[:, c * QUAD : (c + 1) * QUAD] = gather_blocks(z[c])


def combine(mix_ref, stat_ref, inv_ref, me, cm_ref, lv_ref, gst_ref):
    n, _, d = mix_ref.shape
    lane = iota((M, 128), 1)
    top = stat_ref[0]
    for i in range(1, n):
        top = jnp.maximum(top, stat_ref[i])
    top = jnp.where(lane < 64, top, 0.0)
    total = jnp.zeros((M, 128), F32)
    scales = []
    for i in range(n):
        st = stat_ref[i]
        sc = jnp.where(lane < 64, jnp.exp(st - top), 0.0)
        scales.append(sc)
        total = total + sc * pltpu.roll(st, 64, 1)
    own = jnp.where(lane < 64, jnp.exp(stat_ref[me] - top), 0.0)
    gst_ref[...] = jnp.where(lane < 64, own, pltpu.roll(total, 64, 1))
    mask = block_mask()
    for c in range(d // QUAD):
        cols = slice(c * QUAD, (c + 1) * QUAD)
        mixed = jnp.zeros((M, QUAD), F32)
        for i in range(n):
            mixed = mixed + per_head(scales[i], 0, c) * mix_ref[i, :, cols].astype(F32)
        lv = mixed / per_head(total, 0, c)
        lv_ref[:, cols] = lv
        cm = three(nn, spread_blocks(inv_ref[:, cols], mask), spread_blocks(lv, mask))
        cm_ref[:, cols] = gather_blocks(cm).astype(BF)


def attend_kernel(
    inputs_any, pad_ref, wq0, wq1, wk0, wk1, wv0, wv1,
    q_any, k_any, v_any, xt_any, k1_any, e_any, save_any,
    marks, edge, cm_ref, lv_ref, gst_ref, inv_ref, k2_ref,
    x, q, k, v, xt, k1, e, save, pack, mix, stat, mixes, stats,
    ship, send, recv, *, n, shape,
):
    idx = places()
    me = idx[1]
    tok, d = x.shape
    half = d // 2
    lm = tok // M
    ready = greet({"seq": n})
    load = pltpu.make_async_copy(inputs_any.at[idx[0]], x, ship.at[0])
    load.start()
    moved = []

    def out(src, dst):
        c = pltpu.make_async_copy(src, dst, ship.at[1 + len(moved)])
        c.start()
        moved.append(c)

    peers = [lax.rem(me + p, n) for p in range(1, n)]
    sent = []

    def tell(src, dst, to):
        c = remote(src, dst, send.at[len(sent)], recv.at[len(sent)], "seq", to)
        c.start()
        sent.append(c)
        return c

    valid = pad_ref[pl.ds(idx[0], 1), :].astype(F32)
    keep_n = jnp.sum(valid, axis=1, keepdims=True).astype(jnp.int32) - me * tok
    keep = (iota((tok, 1), 0) < keep_n).astype(F32)
    count = jnp.maximum(jnp.sum(keep.reshape(lm, M, 1), axis=1), 1.0)
    load.wait()
    for at, w, dst in ((0, (wq0, wq1), q), (lm, (wk0, wk1), k)):
        for i in range(2):
            cols = slice(i * half, (i + 1) * half)
            val = nn(x[...], w[i][...]).astype(BF)
            dst[:, cols] = val
            wide = (val.astype(F32) * keep).reshape(lm, M, half)
            pack[at : at + lm, cols] = (jnp.sum(wide, axis=1) / count).astype(BF)
    ready()
    first = [tell(pack, marks.at[me], to) for to in peers]
    marks[me] = pack[...]
    for i, w in enumerate((wv0, wv1)):
        v[:, i * half : (i + 1) * half] = (nn(x[...], w[...]) * keep).astype(BF)
    edges = [
        tell(v.at[pl.ds(tok - 16, 16)], edge.at[pl.ds(0, 16)], peers[0]),
        tell(v.at[pl.ds(0, 16)], edge.at[pl.ds(16, 16)], peers[n - 2]),
    ]
    store_chunks(xt, x[...].T, idx, shape)
    for src, dst in ((q, q_any), (k, k_any), (v, v_any), (xt, xt_any)):
        out(src, dst)
    for c in first:
        c.wait()
    qm = jnp.concatenate([marks[i, 0:lm, :] for i in range(n)], axis=0)
    km = jnp.concatenate([marks[i, lm : 2 * lm, :] for i in range(n)], axis=0)
    minus = jnp.where(iota((1, tok), 1) < keep_n, 0.0, 1000000000.0)
    st = jnp.zeros((M, 128), F32)
    for c in range(d // QUAD):
        st = score_quad(c, q, k, v, qm, km, minus, k1, e, mix, st)
    stat[...] = st
    second = [tell(a, b.at[me], to) for a, b in ((mix, mixes), (stat, stats)) for to in peers]
    mixes[me] = mix[...]
    stats[me] = stat[...]
    out(k1, k1_any)
    out(e, e_any)
    pseudo_inverse(qm, km, k2_ref, inv_ref, save, jnp.minimum(me, d // QUAD - 1))
    out(save, save_any)
    for c in second:
        c.wait()
    combine(mixes, stats, inv_ref, me, cm_ref, lv_ref, gst_ref)
    for c in edges + moved:
        c.wait()


def attend(n, inputs, padding, weights, shape):
    _, tok, d = inputs.shape
    lm = tok // M
    flat, turned = sds((tok, d), BF), sds((d, tok), BF)
    save = sds((ITERS, 4, QUAD, QUAD), BF)
    big = [flat, flat, flat, turned, turned, turned, save]
    small = [
        sds((n, 2 * lm, d), BF),
        sds((32, d), BF),
        sds((M, d), BF),
        sds((M, d), F32),
        sds((M, 128), F32),
        sds((M, d), F32),
        sds((M, d), F32),
    ]
    vm = pl.BlockSpec(memory_space=pltpu.VMEM)
    count = 3 * (n - 1) + 2
    return pl.pallas_call(
        functools.partial(attend_kernel, n=n, shape=shape),
        in_specs=[ANY] + [vm] * 7,
        out_specs=[ANY] * len(big) + [vm] * len(small),
        out_shape=big + small,
        scratch_shapes=[pltpu.VMEM(a.shape, a.dtype) for a in [flat] + big]
        + [
            pltpu.VMEM((2 * lm, d), BF),
            pltpu.VMEM((M, d), BF),
            pltpu.VMEM((M, 128), F32),
            pltpu.VMEM((n, M, d), BF),
            pltpu.VMEM((n, M, 128), F32),
            pltpu.SemaphoreType.DMA((8,)),
            pltpu.SemaphoreType.DMA((count,)),
            pltpu.SemaphoreType.DMA((count,)),
        ],
        compiler_params=params(56, collective_id=1, has_side_effects=True),
        cost_estimate=pl.CostEstimate(
            flops=6 * tok * d * d + 72 * 3 * 2 * QUAD**3,
            bytes_accessed=30 * tok * d,
            transcendentals=2 * tok * d,
        ),
        name="attend",
    )(inputs, padding, *weights)


def doc_bounds(doc_ref, idx):
    row = doc_ref[pl.ds(idx[0], 1), :]
    return [
        jnp.sum((row < j).astype(F32), axis=1, keepdims=True).astype(jnp.int32)
        for j in range(1, 9)
    ]


def docs_at(place, bounds, length):
    doc = jnp.zeros(place.shape, jnp.int32)
    for b in bounds:
        doc = doc + (place >= b).astype(jnp.int32)
    return jnp.where((place >= 0) & (place < length), doc, -1)


def tap_lines(taps):
    heads, width = taps.shape
    at = 64 - width // 2
    pad = ((0, 0), (at, 256 - at - width))
    return jnp.stack([jnp.pad(taps, pad), jnp.pad(taps[:, ::-1], pad)])


def fill_bands(line_ref, band_ref):
    for h in range(band_ref.shape[0]):
        wide = jnp.broadcast_to(line_ref[h : h + 1, :], band_ref.shape[1:])
        band_ref[h] = pltpu.roll(wide, 0, 1, stride=1, stride_axis=0).astype(BF)


def banded(band_ref, window, same, col0):
    lane = iota((band_ref.shape[1], 128), 1)
    first = nn(band_ref[col0] * same, window)
    second = nn(band_ref[col0 + 1] * same, window)
    return jnp.where(lane < 64, first, second)


def fill_halo(ext, body, edge_ref, tok):
    ext[0:48, :] = jnp.zeros((48, ext.shape[1]), BF)
    ext[48:64, :] = edge_ref[0:16, :]
    ext[64 : 64 + tok, :] = body[...]
    ext[64 + tok : 80 + tok, :] = edge_ref[16:32, :]
    ext[80 + tok :, :] = jnp.zeros((48, ext.shape[1]), BF)


def erf_parts(u):
    a = jnp.abs(u) * 0.7071067811865476
    e = jnp.exp(-0.5 * u * u)
    t = 1.0 / (1.0 + 0.3275911 * a)
    poly = t * (
        0.254829592
        + t * (-0.284496736 + t * (1.421413741 + t * (-1.453152027 + t * 1.061405429)))
    )
    tail = 0.5 * poly * e
    cdf = jnp.where(u < 0.0, tail, 1.0 - tail)
    return cdf, e * 0.3989422804014327


def norm_stats(h):
    mean = jnp.mean(h, axis=-1, keepdims=True)
    centre = h - mean
    rstd = lax.rsqrt(jnp.mean(centre * centre, axis=-1, keepdims=True) + EPS)
    return centre * rstd, rstd


def norm_back(g, hat, rstd):
    return rstd * (
        g
        - jnp.mean(g, axis=-1, keepdims=True)
        - hat * jnp.mean(g * hat, axis=-1, keepdims=True)
    )


def core_kernel(
    x_any,
    cot_any,
    pad_ref,
    doc_ref,
    v_ref,
    edge_ref,
    k1_ref,
    cm_ref,
    line_ref,
    wo0_any,
    wo1_any,
    wu0_any,
    wu1_any,
    wd0_any,
    wd1_any,
    vec_ref,
    ctx0,
    act0,
    du0,
    gh1_ref,
    gc_ref,
    acc_ref,
    out_own,
    nlt_own,
    gh2t_own,
    gh1t_own,
    out_got,
    nlt_got,
    gh2t_got,
    gh1t_got,
    ctx_got,
    act_got,
    du_got,
    ext,
    band,
    wo,
    wu,
    wd,
    gp,
    x_all,
    cot_all,
    out2,
    nlt2,
    gh2t2,
    gh1t2,
    ctx2,
    act2,
    du2,
    sems,
    send,
    recv,
    local,
    *,
    tok,
    shape,
):
    idx = places()
    step = pl.program_id(0)
    steps = pl.num_programs(0)
    rows, d = gh1_ref.shape
    half = d // 2
    ga, sa, gf, sf = (vec_ref[i : i + 1, :] for i in range(4))
    loads = [
        pltpu.make_async_copy(src, dst, sems.at[n])
        for n, (src, dst) in enumerate(
            [
                (wo0_any, wo.at[0]),
                (wo1_any, wo.at[1]),
                (wu0_any, wu.at[0]),
                (wu1_any, wu.at[1]),
                (wd0_any, wd.at[0]),
                (wd1_any, wd.at[1]),
                (x_any.at[idx[0]], x_all),
                (cot_any.at[idx[0]], cot_all),
            ]
        )
    ]

    def arrived(*which):
        @pl.when(step == 0)
        def _():
            for i in which:
                loads[i].wait()

    own = pl.multiple_of(step * rows, rows)
    slot = lax.rem(step, 2)
    moved = [
        (out2, out_got, out_own, False),
        (nlt2, nlt_got, nlt_own, True),
        (gh2t2, gh2t_got, gh2t_own, True),
        (gh1t2, gh1t_got, gh1t_own, True),
        (ctx2, ctx_got, None, False),
        (act2, act_got, None, False),
        (du2, du_got, None, False),
    ]

    def copies(n, t, both=True):
        src, far, near, turned = moved[n]
        part = pl.ds(pl.multiple_of(t * rows, rows), rows)
        src = src.at[lax.rem(t, 2)]
        at = lambda ref: ref.at[:, part] if turned else ref.at[part]
        out = [remote(src, at(far), send.at[n, t], recv.at[n, t], "mp", 1 - idx[0])]
        if both and near is not None:
            out.append(pltpu.make_async_copy(src, at(near), local.at[n, t]))
        return out

    def give(n):
        for c in copies(n, step):
            c.start()

    def given(t):
        for n in range(len(moved)):
            c = copies(n, t)
            c[0].wait_send()
            if len(c) > 1:
                c[1].wait()

    @pl.when(step == 0)
    def _():
        ready = greet({"mp": 2})
        for i in (0, 1, 6, 2, 3, 4, 5, 7):
            loads[i].start()
        fill_halo(ext, v_ref, edge_ref, tok)
        fill_bands(line_ref.at[0], band)
        acc_ref[...] = jnp.zeros_like(acc_ref)
        ready()

    @pl.when(step >= 2)
    def _():
        given(step - 2)

    out_ref, nlt_ref, gh2t_ref, gh1t_ref, ctx1, act1, du1 = (m[0].at[slot] for m in moved)

    bounds = doc_bounds(doc_ref, idx)
    mask = block_mask()
    start = idx[1] * tok + step * rows
    parts = []
    for sub in range(rows // 128):
        place = start + sub * 128
        same = (
            docs_at(place + iota((128, 1), 0), bounds, LEN)
            == docs_at(place - 64 + iota((1, 256), 1), bounds, LEN)
        ).astype(BF)
        base = pl.multiple_of(step * rows + sub * 128, 128)
        cols = []
        for pair in range(d // 128):
            window = ext[pl.ds(base, 256), pair * 128 : (pair + 1) * 128]
            cols.append(banded(band, window, same, 2 * pair))
        parts.append(jnp.concatenate(cols, axis=1))
    conv = jnp.concatenate(parts, axis=0)
    ctxs = []
    for c in range(d // QUAD):
        cols = slice(c * QUAD, (c + 1) * QUAD)
        att = tn(k1_ref[cols, :], spread_blocks(cm_ref[:, cols], mask))
        ctxs.append((att + conv[:, cols]).astype(BF))
    ctx = jnp.concatenate(ctxs, axis=1)
    ctx0[...] = ctx[:, :half]
    ctx1[...] = ctx[:, half:]
    give(4)
    arrived(0, 1, 6)
    branch = nn(ctx[:, :half], wo[0]) + nn(ctx[:, half:], wo[1])
    xf = x_all[pl.ds(own, rows), :].astype(F32)
    hat1, rstd1 = norm_stats(xf + branch)
    normed = hat1 * ga + sa
    nl = normed.astype(BF)
    store_chunks(nlt_ref, nl.T, idx, shape)
    give(1)
    arrived(2, 3)
    chunk = 512
    hidden = wu.shape[2]
    for i, act in ((0, act0), (1, act1)):
        for at in range(0, hidden, chunk):
            cols = slice(at, at + chunk)
            u = nn(nl, wu[i, :, cols])
            cdf, pdf = erf_parts(u)
            act[:, cols] = (u * cdf).astype(BF)
            gp[i, :, cols] = (cdf + u * pdf).astype(BF)
    give(5)
    arrived(4, 5, 7)
    ffn = nn(act0[...], wd[0]) + nn(act1[...], wd[1])
    hat2, rstd2 = norm_stats(normed + ffn)
    out_ref[...] = (hat2 * gf + sf).astype(BF)
    give(0)
    cot = cot_all[pl.ds(own, rows), :].astype(F32)
    gh2 = norm_back(cot * gf, hat2, rstd2)
    low = gh2.astype(BF)
    store_chunks(gh2t_ref, low.T, idx, shape)
    give(2)
    for i, du in ((0, du0), (1, du1)):
        for at in range(0, hidden, chunk):
            cols = slice(at, at + chunk)
            du[:, cols] = (nt(low, wd[i, cols, :]) * gp[i, :, cols].astype(F32)).astype(BF)
    give(6)
    gn = gh2 + nt(du0[...], wu[0]) + nt(du1[...], wu[1])
    gh1 = norm_back(gn * ga, hat1, rstd1).astype(BF)
    gh1_ref[...] = gh1
    store_chunks(gh1t_ref, gh1.T, idx, shape)
    give(3)
    gc_ref[:, :half] = nt(gh1, wo[0]).astype(BF)
    gc_ref[:, half:] = nt(gh1, wo[1]).astype(BF)
    keep_n = valid_count(pad_ref, idx) - start
    keep = (iota((rows, 1), 0) < keep_n).astype(F32)
    acc_ref[0:1, :] += jnp.sum(gn * hat1, axis=0, keepdims=True)
    acc_ref[1:2, :] += jnp.sum(gn, axis=0, keepdims=True)
    acc_ref[2:3, :] += jnp.sum(cot * hat2, axis=0, keepdims=True)
    acc_ref[3:4, :] += jnp.sum(cot, axis=0, keepdims=True)
    acc_ref[4:5, :] += jnp.sum(xf * xf * keep, axis=0, keepdims=True)
    acc_ref[5:6, :] += jnp.sum(branch * branch * keep, axis=0, keepdims=True)
    acc_ref[6:7, :] += jnp.sum(ffn * ffn * keep, axis=0, keepdims=True)

    @pl.when(step == steps - 1)
    def _():
        given(steps - 2)
        given(steps - 1)
        for n in range(len(moved)):
            for t in range(tok // rows):
                copies(n, t, False)[0].wait_recv()


def core(inputs, cot, padding, documents, v, edge, k1, cm, lines, wo, wu, wd, vecs, shape):
    tok, d = v.shape
    rows = 256
    steps = tok // rows
    f2 = wu[0].shape[1]
    heads = lines.shape[1]
    blk = lambda i: (i, 0)
    flat = pl.BlockSpec((rows, d), blk)
    part = pl.BlockSpec((rows, d // 2), blk)
    turned = pl.BlockSpec((d, rows), lambda i: (0, i))
    wide = pl.BlockSpec((rows, f2), blk)
    full, t = sds((tok, d), BF), sds((d, tok), BF)
    thin, broad = sds((tok, d // 2), BF), sds((tok, f2), BF)
    return pl.pallas_call(
        functools.partial(core_kernel, tok=tok, shape=shape),
        grid=(steps,),
        in_specs=[ANY] * 2
        + [whole(a.shape) for a in (padding, documents, v, edge)]
        + [turned]
        + [whole(a.shape) for a in (cm, lines)]
        + [ANY] * 6
        + [whole(vecs.shape)],
        out_specs=[part, wide, wide, flat, flat, whole((8, d))] + [ANY] * 11,
        out_shape=[thin, broad, broad, full, full, sds((8, d), F32)]
        + [full, t, t, t] * 2
        + [thin, broad, broad],
        scratch_shapes=[
            pltpu.VMEM((tok + 128, d), BF),
            pltpu.VMEM((heads, 128, 256), BF),
            pltpu.VMEM((2, d // 2, d), BF),
            pltpu.VMEM((2, d, f2), BF),
            pltpu.VMEM((2, f2, d), BF),
            pltpu.VMEM((2, rows, f2), BF),
            pltpu.VMEM((tok, d), BF),
            pltpu.VMEM((tok, d), BF),
            pltpu.VMEM((2, rows, d), BF),
            pltpu.VMEM((2, d, rows), BF),
            pltpu.VMEM((2, d, rows), BF),
            pltpu.VMEM((2, d, rows), BF),
            pltpu.VMEM((2, rows, d // 2), BF),
            pltpu.VMEM((2, rows, f2), BF),
            pltpu.VMEM((2, rows, f2), BF),
            pltpu.SemaphoreType.DMA((8,)),
            pltpu.SemaphoreType.DMA((7, steps)),
            pltpu.SemaphoreType.DMA((7, steps)),
            pltpu.SemaphoreType.DMA((4, steps)),
        ],
        compiler_params=params(60, collective_id=2, has_side_effects=True),
        cost_estimate=pl.CostEstimate(
            flops=16 * tok * d * f2, bytes_accessed=60 * tok * d, transcendentals=4 * tok * f2
        ),
        name="core",
    )(inputs, cot, padding, documents, v, edge, k1, cm, lines, *wo, *wu, *wd, vecs)


class Sum:
    def __init__(self, idx, slots, got1, half, got2, parts, got3, send, recv):
        self.idx = idx
        self.slots, self.got1, self.half = slots, got1, half
        self.got2, self.parts, self.got3 = got2, parts, got3
        self.send, self.recv = send, recv
        self.live = []

    @staticmethod
    def shapes(d, n):
        q = d // 4
        ch = q // 4
        return [
            pltpu.VMEM((4, 2 * q, n), BF),
            pltpu.VMEM((2, 2 * q, n), BF),
            pltpu.VMEM((4, q, n), BF),
            pltpu.VMEM((2, q, n), BF),
            pltpu.VMEM((4, ch, 2 * n), BF),
            pltpu.VMEM((3, ch, 2 * n), BF),
            pltpu.SemaphoreType.DMA((7,)),
            pltpu.SemaphoreType.DMA((7,)),
        ]

    def start(self, n, src, dst, axis, to):
        c = remote(src, dst, self.send.at[n], self.recv.at[n], axis, to)
        c.start()
        self.live.append(c)

    def arrived(self):
        for c in self.live:
            c.wait()
        self.live = []

    def store(self, part, cols, acc):
        q = acc.shape[0] // 4
        if part == 0:
            self.slots[1, :, cols] = acc[: 2 * q]
            self.slots[0, :, cols] = acc[2 * q :]
        else:
            self.slots[3, :q, cols] = acc[:q]
            self.slots[2, :q, cols] = acc[q : 2 * q]
            self.slots[3, q:, cols] = acc[2 * q : 3 * q]
            self.slots[2, q:, cols] = acc[3 * q :]

    def step0(self, part):
        bit = 1 + part
        self.start(part, self.slots.at[2 * part], self.got1.at[part], "seq", self.idx[1] ^ bit)

    def step1(self):
        self.arrived()
        q = self.half.shape[1]
        for part in range(2):
            keep = self.slots[2 * part + 1].astype(F32) + self.got1[part].astype(F32)
            self.half[2 * part + 1] = keep[:q].astype(BF)
            self.half[2 * part] = keep[q:].astype(BF)
            bit = 2 - part
            self.start(
                2 + part, self.half.at[2 * part], self.got2.at[part], "seq", self.idx[1] ^ bit
            )

    def step2(self):
        self.arrived()
        n = self.half.shape[2]
        ch = self.parts.shape[1]
        for part in range(2):
            keep = (self.half[2 * part + 1].astype(F32) + self.got2[part].astype(F32)).astype(BF)
            for p in range(4):
                self.parts[p, :, part * n : (part + 1) * n] = keep[p * ch : (p + 1) * ch]
        for p in range(1, 4):
            self.start(3 + p, self.parts.at[p], self.got3.at[p - 1], "dp", self.idx[2] ^ p)

    def finish(self):
        self.arrived()
        out = self.parts[0].astype(F32)
        for p in range(3):
            out = out + self.got3[p].astype(F32)
        return out


def sum_any(full):
    part = lax.psum_scatter(full.astype(F32), "dp", scatter_dimension=0, tiled=True)
    return lax.psum_scatter(part, "seq", scatter_dimension=0, tiled=True)


def joined(send_a, keep_a, send_b, keep_b):
    q = keep_a.shape[0] // 2
    b = jnp.concatenate([keep_b[:q], send_b[:q], keep_b[q:], send_b[q:]], axis=0)
    return jnp.concatenate([jnp.concatenate([keep_a, send_a], axis=0), b], axis=1)


def first_quad(c, q_ref, k1_ref, gc_ref, cm_ref, km, gq_ref, mix_ref, km_ref):
    cols = slice(c * QUAD, (c + 1) * QUAD)
    tok = q_ref.shape[0]
    mask = block_mask()
    kmb = spread_blocks(km[:, cols], mask)
    gc = gc_ref[:, cols]
    k1 = k1_ref[cols, :]
    mix_ref[:, cols] = gather_blocks(nn(k1, gc)).astype(BF)
    g = nt(spread_blocks(cm_ref[:, cols], mask), gc).reshape(QUAD // M, M, tok)
    kf = k1.astype(F32).reshape(QUAD // M, M, tok)
    inner = jnp.sum(g * kf, axis=1, keepdims=True)
    g1 = (kf * (g - inner)).reshape(QUAD, tok).astype(BF)
    gq_ref[:, cols] = (tn(g1, kmb) * 0.125).astype(BF)
    km_ref[:, cols] = gather_blocks(nn(g1, q_ref[:, cols])) * 0.125


def middle(gmix_ref, lv_ref, inv_ref, gst_ref, gm_ref, gt_ref):
    n = gmix_ref.shape[0]
    d = lv_ref.shape[1]
    mask = block_mask()
    lane = iota((M, 128), 1)
    head = iota((M, QUAD), 1) // M
    stat = gst_ref[...]
    gt = jnp.zeros((M, 128), F32)
    for c in range(d // QUAD):
        cols = slice(c * QUAD, (c + 1) * QUAD)
        gmix = jnp.zeros((M, QUAD), F32)
        for i in range(n):
            gmix = gmix + gmix_ref[i, :, cols].astype(F32)
        glv = gather_blocks(
            three(tn, spread_blocks(inv_ref[:, cols], mask), spread_blocks(gmix, mask))
        )
        scale = per_head(stat, 0, c)
        total = per_head(stat, 64, c)
        gm_ref[:, cols] = ((glv / total).astype(BF).astype(F32) * scale).astype(BF)
        prod = glv * lv_ref[:, cols]
        for h in range(QUAD // M):
            at = c * (QUAD // M) + h
            s = jnp.sum(jnp.where(head == h, prod, 0.0), axis=1, keepdims=True)
            gt = jnp.where(lane == at, -s / stat[:, 64 + at : 65 + at] * stat[:, at : at + 1], gt)
    gt_ref[...] = gt


def pinv_back(gmix_ref, lv_ref, k2_ref, save_ref, qm, km, cols, use):
    n = gmix_ref.shape[0]
    mask = block_mask()
    ident = (iota((QUAD, QUAD), 0) == iota((QUAD, QUAD), 1)).astype(F32)
    gmix = jnp.zeros((M, QUAD), F32)
    for i in range(n):
        gmix = gmix + gmix_ref[i, :, cols].astype(F32)
    dz = three(nt, spread_blocks(gmix, mask), spread_blocks(lv_ref[:, cols], mask))
    kernel = spread_blocks(k2_ref[:, cols], mask)
    klow = kernel.astype(BF)
    dk = jnp.zeros((QUAD, QUAD), F32)
    ibf = ident.astype(BF)
    for it in range(ITERS - 1, -1, -1):
        z, p, i2, i3 = (save_ref[it, kind] for kind in range(4))
        i1 = 7.0 * ibf - p
        dlow = dz.astype(BF)
        d3 = (0.25 * tn(z, dlow)).astype(BF)
        dp = nt(d3, i2)
        d2 = (-tn(p, d3)).astype(BF)
        dp = dp + nt(d2, i1)
        d1 = -tn(p, d2)
        dp = (-dp - d1).astype(BF)
        dz = 0.25 * nt(dlow, i3) + tn(klow, dp)
        dk = dk + nt(dp, z)
    sums = jnp.sum(kernel, axis=0, keepdims=True)
    lane = iota((1, QUAD), 1) // M
    dzt = jnp.where(mask, dz, 0.0).T
    dsum = jnp.sum(dzt * kernel, axis=0, keepdims=True)
    scale = jnp.zeros((1, QUAD), F32)
    extra = jnp.zeros((1, QUAD), F32)
    for h in range(QUAD // M):
        mine = lane == h
        best = jnp.max(jnp.where(mine, sums, 0.0), axis=1, keepdims=True)
        dscale = jnp.sum(jnp.where(mine, dsum, 0.0), axis=1, keepdims=True)
        is_best = (mine & (sums == best)).astype(F32)
        share = is_best / jnp.sum(is_best, axis=1, keepdims=True)
        scale = jnp.where(mine, 1.0 / best, scale)
        extra = jnp.where(mine, -dscale / (best * best) * share, extra)
    dk = dk + dzt * scale + extra
    inner = jnp.sum(jnp.where(mask, dk * kernel, 0.0), axis=1, keepdims=True)
    g2 = kernel * (dk - inner)
    g2h, g2l = split(g2)
    kb, qb = spread_blocks(km, mask), spread_blocks(qm, mask)
    use = use * 0.125
    return (
        gather_blocks(nn(g2h, kb) + nn(g2l, kb)) * use,
        gather_blocks(tn(g2h, qb) + tn(g2l, qb)) * use,
    )


def second_quad(
    c, k_ref, v_ref, vedge_ref, gc_ref, gedge_ref, e_ref, gm_ref, gt_ref, marks_ref, bounds,
    start, keep_n, line_ref, gk_ref, gv_ref, qm_ref, gtap_ref, vext, gext, band, pairs,
):
    n, lm = marks_ref.shape[0], marks_ref.shape[1] // 2
    heads = QUAD // M
    tok = k_ref.shape[0]
    at = pl.multiple_of(c * QUAD, QUAD)
    cols = pl.ds(at, QUAD)
    mask = block_mask()
    qm = spread_blocks(
        jnp.concatenate([marks_ref[i, 0:lm, cols] for i in range(n)], axis=0), mask
    )
    gm = spread_blocks(gm_ref[:, cols], mask)
    lane = iota((M, 128), 1)
    gts = []
    for h in range(heads):
        pick = jnp.where(lane == c * heads + h, gt_ref[...], 0.0)
        gts.append(jnp.sum(pick, axis=1, keepdims=True))
    gt = jnp.concatenate(gts, axis=0)
    e = e_ref[cols, :]
    g3 = (e.astype(F32) * (nt(gm, v_ref[:, cols]) + gt)).astype(BF)
    qm_ref[:, cols] = gather_blocks(nn(g3, k_ref[:, cols])) * 0.125
    gk_ref[:, cols] = (tn(g3, qm) * 0.125).astype(BF)
    gv = tn(e, gm)
    fill_halo(vext, v_ref.at[:, cols], vedge_ref.at[:, cols], tok)
    fill_halo(gext, gc_ref.at[:, cols], gedge_ref.at[:, cols], tok)
    fill_bands(line_ref.at[c], band)
    low64 = iota((128, 128), 1) < M
    pairs[...] = jnp.zeros_like(pairs)
    for sub in range(tok // 128):
        place = start + sub * 128
        same = docs_at(place + iota((128, 1), 0), bounds, LEN) == docs_at(
            place - 64 + iota((1, 256), 1), bounds, LEN
        )
        low = same.astype(BF)
        keep = iota((128, 1), 0) < keep_n - sub * 128
        rows = slice(sub * 128, sub * 128 + 128)
        for pair in range(heads // 2):
            lanes = slice(pair * 128, pair * 128 + 128)
            back = banded(band, gext[sub * 128 : sub * 128 + 256, lanes], low, 2 * pair)
            wide = pl.ds(pl.multiple_of(at + pair * 128, 128), 128)
            gv_ref[rows, wide] = jnp.where(keep, gv[rows, lanes] + back, 0.0).astype(BF)
            g = gc_ref[rows, wide]
            win = vext[sub * 128 : sub * 128 + 256, lanes]
            for h in range(2):
                own = jnp.where(low64 == (h == 0), g, jnp.zeros((), BF))
                pairs[2 * pair + h] += jnp.where(same, nt(own, win), 0.0)
    for h in range(heads):
        tall = pairs[h, 0:8]
        for r in range(8, 128, 8):
            tall = tall + pltpu.roll(pairs[h, r : r + 8], 256 - r, 1)
        line = tall[0:1]
        for r in range(1, 8):
            line = line + pltpu.roll(tall[r : r + 1], 256 - r, 1)
        gtap_ref[pl.ds(c * heads + h, 1), :] = line


def back_kernel(*refs, n, dp_n, fast):
    (
        pad_ref, doc_ref, line_ref, marks, cm_ref, lv_ref, inv_ref, gst_ref, k2_ref, vedge, acc_ref,
        k1_any, gc_any, q_any, k_any, v_any, e_any, save_any,
        gh2t_any, gh2t_got, nlt_any, nlt_got, act0, act_got, du0, du_got,
        gv_any, dq_any, dk_any, small_out, *rest,
    ) = refs
    outs, rest = (rest[:2], rest[2:]) if fast else (rest[:8], rest[8:])
    (
        k1, gc, q, k, v, e, save, lhs, rhs, gq, gk, gv, gedge, mix, mixes, gm, gt, gkm, gqm, both,
        got, small, smalls, gtap, vext, gext, band, pairs, loads, stream, ship, send, recv, *rest,
    ) = rest
    idx = places()
    me = idx[1]
    tok, d = q.shape
    lm = tok // M
    quads = d // QUAD
    sizes = {"seq": n, "dp": dp_n} if fast else {"seq": n}
    ready = greet(sizes)
    fetch = [
        pltpu.make_async_copy(src, dst, loads.at[i])
        for i, (src, dst) in enumerate(
            [
                (k1_any, k1), (gc_any, gc), (q_any, q),
                (gh2t_any, lhs.at[0]), (gh2t_got, lhs.at[1]),
                (nlt_any, lhs.at[2]), (nlt_got, lhs.at[3]),
                (save_any, save), (k_any, k), (v_any, v), (e_any, e),
            ]
        )
    ]
    width = rhs.shape[3]
    blocks = act0.shape[1] // width
    work = [(g, j) for g in range(2) for j in range(blocks)]

    def block(i):
        g, j = work[i]
        cols = pl.ds(j * width, width)
        srcs = (act0, act_got) if g == 0 else (du0, du_got)
        return [
            pltpu.make_async_copy(src.at[:, cols], rhs.at[i % 2, t], stream.at[i % 2, t])
            for t, src in enumerate(srcs)
        ]

    for c in fetch[:5]:
        c.start()
    for c in block(0):
        c.start()
    for c in fetch[5:]:
        c.start()
    sent = []

    def tell(src, dst, to):
        c = remote(src, dst, send.at[len(sent)], recv.at[len(sent)], "seq", to)
        c.start()
        sent.append(c)
        return c

    peers = [lax.rem(me + p, n) for p in range(1, n)]
    qm = jnp.concatenate([marks[i, 0:lm, :] for i in range(n)], axis=0)
    km = jnp.concatenate([marks[i, lm : 2 * lm, :] for i in range(n)], axis=0)
    for c in fetch[:3]:
        c.wait()
    for c in range(quads):
        first_quad(c, q, k1, gc, cm_ref, km, gq, mix, gkm)
    ready()
    swaps = [tell(mix, mixes.at[me], to) for to in peers]
    swaps += [
        tell(gc.at[pl.ds(tok - 16, 16)], gedge.at[pl.ds(0, 16)], peers[0]),
        tell(gc.at[pl.ds(0, 16)], gedge.at[pl.ds(16, 16)], peers[n - 2]),
    ]
    mixes[me] = mix[...]

    sums = []
    for g in range(2):
        if fast:
            sums.append(Sum(idx, *rest[8 * g : 8 * g + 8]))
        else:
            sums.append(Sum(idx, rest[g], *([None] * 7)))

    def products(g):
        fetch[3 + 2 * g].wait()
        fetch[4 + 2 * g].wait()
        for j in range(blocks):
            i = g * blocks + j
            if i + 1 < len(work):
                for c in block(i + 1):
                    c.start()
            for c in block(i):
                c.wait()
            acc = nn(lhs[2 * g], rhs[i % 2, 0]) + nn(lhs[2 * g + 1], rhs[i % 2, 1])
            part, at = j // (blocks // 2), (j % (blocks // 2)) * width
            sums[g].store(part, slice(at, at + width), acc.astype(BF))
            if fast and (j + 1) % (blocks // 2) == 0:
                sums[g].step0(part)

    products(0)
    products(1)
    for c in swaps:
        c.wait()
    middle(mixes, lv_ref, inv_ref, gst_ref, gm, gt)
    fetch[7].wait()
    sel = jnp.minimum(me, quads - 1)
    cols = pl.ds(pl.multiple_of(sel * QUAD, QUAD), QUAD)
    use = (me < quads).astype(F32)
    qm_sel = jnp.concatenate([marks[i, 0:lm, cols] for i in range(n)], axis=0)
    km_sel = jnp.concatenate([marks[i, lm : 2 * lm, cols] for i in range(n)], axis=0)
    two_q, two_k = pinv_back(mixes, lv_ref, k2_ref, save, qm_sel, km_sel, cols, use)
    if fast:
        sums[0].step1()
    valid = pad_ref[pl.ds(idx[0], 1), :].astype(F32)
    keep_n = jnp.sum(valid, axis=1, keepdims=True).astype(jnp.int32) - me * tok
    bounds = doc_bounds(doc_ref, idx)
    for c in fetch[8:]:
        c.wait()

    @pl.loop(0, quads)
    def _(c):
        second_quad(
            c, k, v, vedge, gc, gedge, e, gm, gt, marks, bounds, me * tok, keep_n, line_ref,
            gk, gv, gqm, gtap, vext, gext, band, pairs,
        )

    gqm[:, cols] += two_q
    gkm[:, cols] += two_k
    for i in range(n):
        rows = slice(i * lm, (i + 1) * lm)
        both[i, :lm] = gqm[rows].astype(BF)
        both[i, lm:] = gkm[rows].astype(BF)
    for r in range(4):
        for b in range(d // 128):
            small[r * (d // 128) + b : r * (d // 128) + b + 1, :] = acc_ref[
                r : r + 1, b * 128 : (b + 1) * 128
            ]
    at = 4 * (d // 128)
    small[at : at + 2 * gtap.shape[0], :] = jnp.concatenate(
        [gtap[:, :128], gtap[:, 128:]], axis=0
    )
    squares = jnp.sum(acc_ref[...], axis=1, keepdims=True)
    small[at + 2 * gtap.shape[0] :, :] = jnp.broadcast_to(squares, (8, 128))
    swaps = [tell(both.at[to], got.at[me], to) for to in peers]
    swaps += [tell(small, smalls.at[me], to) for to in peers]
    got[me] = both[me]
    smalls[me] = small[...]
    out_gv = pltpu.make_async_copy(gv, gv_any, ship.at[0])
    out_gv.start()
    if fast:
        sums[1].step1()
        sums[0].step2()
    for c in swaps:
        c.wait()
    total = smalls[0]
    for i in range(1, n):
        total = total + smalls[i]
    small_out[...] = total
    spread(gq, gk, got, keep_n)
    moved = [
        pltpu.make_async_copy(gq, dq_any, ship.at[1]),
        pltpu.make_async_copy(gk, dk_any, ship.at[2]),
    ]
    for c in moved:
        c.start()
    if fast:
        sums[1].step2()
        for g in range(2):
            outs[g][...] = sums[g].finish()
    else:
        for g in range(2):
            for i in range(4):
                c = pltpu.make_async_copy(rest[g].at[i], outs[4 * g + i], ship.at[3])
                c.start()
                c.wait()
    out_gv.wait()
    for c in moved:
        c.wait()


def spread(gq_ref, gk_ref, got_ref, keep_n):
    n, lm = got_ref.shape[0], got_ref.shape[1] // 2
    got = got_ref[0].astype(F32)
    for i in range(1, n):
        got = got + got_ref[i].astype(F32)
    for j in range(lm):
        rows = slice(j * M, (j + 1) * M)
        keep = (iota((M, 1), 0) < keep_n - j * M).astype(F32)
        share = keep / jnp.maximum(jnp.sum(keep, axis=0, keepdims=True), 1.0)
        for at, ref in ((0, gq_ref), (lm, gk_ref)):
            ref[rows] = (ref[rows].astype(F32) + got[at + j : at + j + 1] * share).astype(BF)


def back(n, dp_n, fast, near, far):
    pad, doc, lines, marks, cm, lv, inv, gst, k2, vedge, acc = near
    tok, d = far[1].shape
    f2 = far[12].shape[1]
    lm = tok // M
    heads = lines.shape[1]
    lines = lines[1].reshape(d // QUAD, QUAD // M, lines.shape[2])
    near = [pad, doc, lines, marks, cm, lv, inv, gst, k2, vedge, acc]
    flat, turned = (tok, d), (d, tok)
    small = (4 * (d // 128) + 2 * heads + 8, 128)
    vm = pl.BlockSpec(memory_space=pltpu.VMEM)
    ch = d // (n * dp_n)
    out_shape = [sds(flat, BF)] * 3 + [sds(small, F32)]
    out_specs = [ANY] * 3 + [vm]
    sems = pltpu.SemaphoreType.DMA
    if fast:
        out_shape += [sds((ch, f2), F32)] * 2
        out_specs += [vm] * 2
        tail = Sum.shapes(d, f2 // 2) * 2
    else:
        out_shape += [sds((d // 2, f2 // 2), BF)] * 8
        out_specs += [ANY] * 8
        tail = [pltpu.VMEM((4, d // 2, f2 // 2), BF)] * 2
    count = 4 * (n - 1) + 2 + 2
    scratch = [
        pltpu.VMEM(turned, BF),
        *[pltpu.VMEM(flat, BF)] * 4,
        pltpu.VMEM(turned, BF),
        pltpu.VMEM((ITERS, 4, QUAD, QUAD), BF),
        pltpu.VMEM((4,) + turned, BF),
        pltpu.VMEM((2, 2, tok, QUAD), BF),
        *[pltpu.VMEM(flat, BF)] * 3,
        pltpu.VMEM((32, d), BF),
        pltpu.VMEM((M, d), BF),
        pltpu.VMEM((n, M, d), BF),
        pltpu.VMEM((M, d), BF),
        pltpu.VMEM((M, 128), F32),
        pltpu.VMEM((M, d), F32),
        pltpu.VMEM((M, d), F32),
        pltpu.VMEM((n, 2 * lm, d), BF),
        pltpu.VMEM((n, 2 * lm, d), BF),
        pltpu.VMEM(small, F32),
        pltpu.VMEM((n,) + small, F32),
        pltpu.VMEM((heads, 256), F32),
        pltpu.VMEM((tok + 128, QUAD), BF),
        pltpu.VMEM((tok + 128, QUAD), BF),
        pltpu.VMEM((QUAD // M, 128, 256), BF),
        pltpu.VMEM((QUAD // M, 128, 256), F32),
        sems((11,)),
        sems((2, 2)),
        sems((4,)),
        sems((count,)),
        sems((count,)),
        *tail,
    ]
    return pl.pallas_call(
        functools.partial(back_kernel, n=n, dp_n=dp_n, fast=fast),
        in_specs=[vm] * len(near) + [ANY] * len(far),
        out_specs=out_specs,
        out_shape=out_shape,
        scratch_shapes=scratch,
        compiler_params=params(60, collective_id=3, has_side_effects=True),
        cost_estimate=pl.CostEstimate(
            flops=8 * tok * d * f2, bytes_accessed=40 * tok * d, transcendentals=0
        ),
        name="back",
    )(*near, *far)


def last_kernel(*refs, n, dp_n, fast):
    (
        small_ref, gh1t_any, gh1t_got, xt_any, xt_got, ctx0, ctx_got, gv_any, dq_any, dk_any,
        gh1_any, q0, q1, k0, k1, v0, v1, *rest,
    ) = refs
    outs, rest = (rest[:5], rest[5:]) if fast else (rest[:11], rest[11:])
    gin_own, gin_got, small_out = outs[:3]
    (
        gh1t, xt, cx, dv, dq, dk, far, gh1, cat, res, gin, small, small_got, rests,
        loads, ship, send, recv, *rest,
    ) = rest
    idx = places()
    tok, d = dv.shape
    half = d // 2
    mate = 1 - idx[0]
    ready = greet({"seq": n, "dp": dp_n, "mp": 2} if fast else {"mp": 2})
    fetch = [
        pltpu.make_async_copy(src, dst, loads.at[i])
        for i, (src, dst) in enumerate(
            [
                (gv_any, dv), (dq_any, dq), (dk_any, dk),
                (gh1t_any, gh1t.at[0]), (gh1t_got, gh1t.at[1]), (ctx0, cx.at[0]), (ctx_got, cx.at[1]),
                (xt_any, xt.at[0]), (xt_got, xt.at[1]), (gh1_any, gh1),
            ]
        )
    ]
    for c in fetch:
        c.start()
    small[...] = small_ref[...]
    sent = []

    def tell(src, dst, axis, to):
        c = remote(src, dst, send.at[len(sent)], recv.at[len(sent)], axis, to)
        c.start()
        sent.append(c)
        return c

    ready()
    swaps = []
    for i, src in enumerate((dv, dq, dk)):
        fetch[i].wait()
        swaps.append(tell(src.at[:, pl.ds(half, half)], far.at[i], "mp", mate))
    swap_small = tell(small, small_got, "mp", mate)
    sums = []
    for g in range(2):
        if fast:
            sums.append(Sum(idx, *rest[8 * g : 8 * g + 8]))
        else:
            sums.append(Sum(idx, rest[g], *([None] * 7)))
    every = slice(0, half)
    for c in fetch[3:7]:
        c.wait()
    sums[0].store(0, every, (nn(gh1t[0], cx[0]) + nn(gh1t[1], cx[1])).astype(BF))
    if fast:
        sums[0].step0(0)
    fetch[7].wait()
    fetch[8].wait()
    for g, part, i, src in ((0, 1, 0, dv), (1, 0, 1, dq), (1, 1, 2, dk)):
        swaps[i].wait()
        acc = nn(xt[0], src[:, :half]) + nn(xt[1], far[i])
        sums[g].store(part, every, acc.astype(BF))
        if fast:
            sums[g].step0(part)
    for i, w in enumerate((q0, q1, k0, k1, v0, v1)):
        cat[:, i * half : (i + 1) * half] = w[...]
    swap_small.wait()
    fetch[9].wait()
    rows = res.shape[0]
    own = pl.multiple_of(idx[0] * half, half)
    other = pl.multiple_of(mate * half, half)

    @pl.loop(0, tok // rows)
    def _(i):
        r = pl.ds(pl.multiple_of(i * rows, rows), rows)
        lhs = jnp.concatenate([dq[r, :], dk[r, :], dv[r, :]], axis=1)
        res[...] = gh1[r, :].astype(F32) + nt(lhs, cat[...])
        gin[0, r, :] = res[:, pl.ds(own, half)].astype(BF)
        gin[1, r, :] = res[:, pl.ds(other, half)].astype(BF)

    swap_gin = tell(gin.at[1], gin_got, "mp", mate)
    keep_gin = pltpu.make_async_copy(gin.at[0], gin_own, ship.at[0])
    keep_gin.start()
    lines = 4 * (d // 128)
    heads = (small.shape[0] - lines - 8) // 2
    mine = small[...]
    theirs = small_got[...]
    taps_a = mine[lines : lines + 2 * heads]
    taps_b = theirs[lines : lines + 2 * heads]
    per = heads // 2
    rests[0, :lines] = mine[:lines] + theirs[:lines]
    rests[0, lines : lines + per] = taps_a[:per] + taps_b[per:heads]
    rests[0, lines + per : lines + heads] = taps_a[heads : heads + per] + taps_b[heads + per :]
    small_out[...] = jnp.zeros_like(small_out)
    small_out[lines + heads : lines + heads + 8] = mine[lines + 2 * heads :]
    small_out[lines + heads + 8 :] = theirs[lines + 2 * heads :]
    if fast:
        norms = [tell(rests.at[0], rests.at[p], "dp", idx[2] ^ p) for p in range(1, dp_n)]
        sums[0].step1()
        sums[1].step1()
        sums[0].step2()
        sums[1].step2()
        for c in norms:
            c.wait()
        total = rests[0]
        for p in range(1, dp_n):
            total = total + rests[p]
        small_out[: lines + heads] = total
        for g in range(2):
            outs[3 + g][...] = sums[g].finish()
    else:
        small_out[: lines + heads] = rests[0]
        for g in range(2):
            for i in range(4):
                c = pltpu.make_async_copy(rest[g].at[i], outs[3 + 4 * g + i], ship.at[1])
                c.start()
                c.wait()
    swap_gin.wait()
    keep_gin.wait()


def last(n, dp_n, fast, small, far, weights):
    tok, d = far[8].shape
    half = d // 2
    flat, thin, turned = (tok, d), (tok, half), (d, tok)
    lines = 4 * (d // 128)
    heads = (small.shape[0] - lines - 8) // 2
    vm = pl.BlockSpec(memory_space=pltpu.VMEM)
    sems = pltpu.SemaphoreType.DMA
    out_shape = [sds(thin, BF)] * 2 + [sds((lines + heads + 16, 128), F32)]
    out_specs = [ANY] * 2 + [vm]
    if fast:
        ch = d // (n * dp_n)
        out_shape += [sds((ch, d), F32)] * 2
        out_specs += [vm] * 2
        tail = Sum.shapes(d, half) * 2
    else:
        out_shape += [sds((half, half), BF)] * 8
        out_specs += [ANY] * 8
        tail = [pltpu.VMEM((4, half, half), BF)] * 2
    scratch = [
        pltpu.VMEM((2,) + turned, BF),
        pltpu.VMEM((2,) + turned, BF),
        pltpu.VMEM((2,) + thin, BF),
        *[pltpu.VMEM(flat, BF)] * 3,
        pltpu.VMEM((3,) + thin, BF),
        pltpu.VMEM(flat, BF),
        pltpu.VMEM((d, 3 * d), BF),
        pltpu.VMEM((256, d), F32),
        pltpu.VMEM((2,) + thin, BF),
        pltpu.VMEM(small.shape, F32),
        pltpu.VMEM(small.shape, F32),
        pltpu.VMEM((4 if fast else 1, lines + heads, 128), F32),
        sems((10,)),
        sems((2,)),
        sems((8,)),
        sems((8,)),
        *tail,
    ]
    return pl.pallas_call(
        functools.partial(last_kernel, n=n, dp_n=dp_n, fast=fast),
        in_specs=[vm] + [ANY] * len(far) + [vm] * 6,
        out_specs=out_specs,
        out_shape=out_shape,
        scratch_shapes=scratch,
        compiler_params=params(60, collective_id=4, has_side_effects=True),
        cost_estimate=pl.CostEstimate(
            flops=14 * tok * d * d, bytes_accessed=30 * tok * d, transcendentals=0
        ),
        name="last",
    )(small, *far, *weights)


def place_kernel(idx, own_ref, other_ref, out_ref):
    @pl.when(pl.program_id(0) == 0)
    def _():
        out_ref[0] = own_ref[...]

    @pl.when(pl.program_id(0) == 1)
    def _():
        out_ref[0] = other_ref[...]


def place_rows(idx, own, other, name, deps=()):
    tok, d = own.shape
    steps = 2
    rows = tok // steps
    return call(
        place_kernel,
        idx,
        [own, other],
        [
            pl.BlockSpec((rows, d), lambda j, i, s: (jnp.where(j == 0, i, steps - 1), 0)),
            pl.BlockSpec((rows, d), lambda j, i, s: (jnp.where(j == 0, 0, i), 0)),
        ],
        pl.BlockSpec((1, rows, d), lambda j, i, s: (s[0] ^ j, i, 0)),
        sds((2, tok, d), own.dtype),
        (2, steps),
        name,
        moved=8 * tok * d,
        deps=deps,
    )


def shards(
    inputs,
    cotangent,
    padding,
    documents,
    w_query,
    w_key,
    w_value,
    w_out,
    w_up,
    w_down,
    conv_taps,
    gain_attn,
    shift_attn,
    gain_ffn,
    shift_ffn,
):
    row_count, tok, d = inputs.shape
    half = d // 2
    heads = conv_taps.shape[0]
    seq_n, dp_n = lax.axis_size("seq"), lax.axis_size("dp")
    mp, seq, dp = lax.axis_index("mp"), lax.axis_index("seq"), lax.axis_index("dp")
    lm = tok // M
    chunk = d // (seq_n * dp_n)
    fast = seq_n == 4 and dp_n == 4 and chunk % 16 == 0
    shape = (dp_n if fast else 0, seq_n, chunk)
    idx = jnp.stack(
        [mp, seq, dp, jnp.full((), min(d // QUAD, seq_n), jnp.int32)]
    ).astype(jnp.int32)

    def swap(a):
        return lax.ppermute(a, "mp", [(0, 1), (1, 0)])

    def pair(a):
        return (a, swap(a))

    wq, wk, wv = pair(w_query), pair(w_key), pair(w_value)
    wo, wu, wd = pair(w_out), pair(w_up), pair(w_down)
    lines = tap_lines(jnp.concatenate(pair(conv_taps), axis=0))
    vecs = jnp.stack([gain_attn, shift_attn, gain_ffn, shift_ffn])
    q, k, v, xt, k1, e, save, marks, vedge, cm, lv, gst, inv, k2 = attend(
        seq_n, inputs, padding, (*wq, *wk, *wv), shape
    )
    xts = pair(xt)
    (
        ctx0, act0, du0, gh1, gc, acc, out_own, nlt, gh2t, gh1t,
        out_got, nlt_got, gh2t_got, gh1t_got, ctx_got, act_got, du_got,
    ) = core(inputs, cotangent, padding, documents, v, vedge, k1, cm, lines, wo, wu, wd, vecs, shape)
    near = [padding, documents, lines, marks, cm, lv, inv, gst, k2, vedge, acc]
    far = [
        k1, gc, q, k, v, e, save, gh2t, gh2t_got, nlt, nlt_got, act0, act_got, du0, du_got,
    ]
    gv, dq, dk, small, *sums = back(seq_n, dp_n, fast, near, far)
    far = [gh1t, gh1t_got, *xts, ctx0, ctx_got, gv, dq, dk, gh1]
    gin0, gin_got, small, *more = last(seq_n, dp_n, fast, small, far, (*wq, *wk, *wv))
    if fast:
        sum_down, sum_up = sums
        sum_ov, sum_qk = more
    else:
        sum_down, sum_up = sum_any(joined(*sums[:4])), sum_any(joined(*sums[4:]))
        sum_ov, sum_qk = sum_any(joined(*more[:4])), sum_any(joined(*more[4:]))
    n = 4 * (d // 128)
    rest = small[: n + 2 * heads]
    if not fast:
        rest = lax.psum(rest, "dp")
    norms = rest[:n].reshape(4, d)
    width = conv_taps.shape[1]
    tap_total = jnp.concatenate([rest[n : n + heads], rest[n + heads :]], axis=1)
    tap_total = tap_total[:, 64 - width // 2 : 64 - width // 2 + width]
    own_sq, got_sq = small[n + 2 * heads + 4 : n + 2 * heads + 7, 0], small[-4:-1, 0]
    own_squares = jnp.where(mp == 0, jnp.stack([own_sq, got_sq]), jnp.stack([got_sq, own_sq]))
    row_valid = jnp.sum(padding.astype(F32), axis=1)
    row_rms = jnp.sqrt(own_squares / (row_valid[:, None] * d) + 1e-06)
    return (
        place_rows(idx, out_own, out_got, "outputs"),
        place_rows(idx, gin0, gin_got, "grad_inputs"),
        sum_qk[:, :half],
        sum_qk[:, half:],
        sum_ov[:, half:],
        sum_ov[:, :half].T,
        sum_up,
        sum_down.T,
        tap_total,
        norms[0],
        norms[1],
        norms[2],
        norms[3],
        row_rms,
    )


def solution(mesh):
    return jax.shard_map(
        shards,
        mesh=mesh,
        in_specs=(
            P("dp", "seq", None),
            P("dp", "seq", None),
            P("dp", None),
            P("dp", None),
            P(None, "mp"),
            P(None, "mp"),
            P(None, "mp"),
            P("mp", None),
            P(None, "mp"),
            P("mp", None),
            P("mp", None),
            P(),
            P(),
            P(),
            P(),
        ),
        out_specs=(
            P("dp", "seq", None),
            P("dp", "seq", "mp"),
            P(("dp", "seq"), "mp"),
            P(("dp", "seq"), "mp"),
            P(("dp", "seq"), "mp"),
            P("mp", ("dp", "seq")),
            P(("dp", "seq"), "mp"),
            P("mp", ("dp", "seq")),
            P("mp", None),
            P(),
            P(),
            P(),
            P(),
            P("dp", None),
        ),
        check_vma=False,
    )
```

```python
import functools

import jax
import jax.numpy as jnp
from jax import lax
from jax.experimental import pallas as pl
from jax.experimental.pallas import tpu as pltpu
from jax.sharding import PartitionSpec as P

M = 64
ITERS = 6
LEN = 4096
QUAD = 256
MESH = pl.DeviceIdType.MESH
F32 = jnp.float32
BF = jnp.bfloat16
EPS = 1e-05


def nn(a, b):
    return lax.dot_general(a, b, (((1,), (0,)), ((), ())), preferred_element_type=F32)


def nt(a, b):
    return lax.dot_general(a, b, (((1,), (1,)), ((), ())), preferred_element_type=F32)


def tn(a, b):
    return lax.dot_general(a, b, (((0,), (0,)), ((), ())), preferred_element_type=F32)


def split(a):
    high = a.astype(BF)
    return high, (a - high.astype(F32)).astype(BF)


def three(dot, a, b):
    ah, al = split(a)
    bh, bl = split(b)
    return dot(ah, bh) + (dot(ah, bl) + dot(al, bh))


def iota(shape, dim):
    return lax.broadcasted_iota(jnp.int32, shape, dim)


def block_mask():
    return iota((QUAD, QUAD), 0) // M == iota((QUAD, QUAD), 1) // M


def spread_blocks(x, mask):
    return jnp.where(mask, jnp.concatenate([x] * (QUAD // M), axis=0), jnp.zeros((), x.dtype))


def gather_blocks(y):
    lane = iota((M, QUAD), 1) // M
    out = jnp.zeros((M, QUAD), y.dtype)
    for h in range(QUAD // M):
        out = out + jnp.where(lane == h, y[h * M : (h + 1) * M], 0.0)
    return out


def params(limit=56, **kw):
    return pltpu.CompilerParams(vmem_limit_bytes=limit * 1024 * 1024, **kw)


def whole(shape):
    nd = len(shape)
    return pl.BlockSpec(shape, lambda *a: (0,) * nd)


def sds(shape, dtype):
    return jax.ShapeDtypeStruct(shape, dtype)


ANY = pl.BlockSpec(memory_space=pl.ANY)


def call(kernel, idx, args, in_specs, out_specs, out_shape, grid, name, scratch=(), flops=0, moved=0, exps=0, deps=(), limit=56):
    nd = len(deps)

    def body(idx_ref, *refs):
        kernel(idx_ref, *refs[nd:])

    return pl.pallas_call(
        body,
        grid_spec=pltpu.PrefetchScalarGridSpec(
            num_scalar_prefetch=1,
            grid=grid,
            in_specs=[ANY] * nd + list(in_specs),
            out_specs=out_specs,
            scratch_shapes=list(scratch),
        ),
        out_shape=out_shape,
        compiler_params=params(limit),
        cost_estimate=pl.CostEstimate(flops=flops, bytes_accessed=moved, transcendentals=exps),
        name=name,
    )(idx, *deps, *args)


def store_chunks(out_ref, t, idx, shape):
    z, sq, chunk = shape
    if z == 0:
        out_ref[...] = t
        return
    for zr in range(z):
        for sr in range(sq):
            b = idx[1] ^ sr
            place = ((b & 1) * 2 + (b >> 1)) * z + (idx[2] ^ zr)
            src = (zr * sq + sr) * chunk
            out_ref[pl.ds(pl.multiple_of(place * chunk, chunk), chunk), :] = t[src : src + chunk]


def valid_count(pad_ref, idx_ref):
    row = pad_ref[pl.ds(idx_ref[0], 1), :].astype(F32)
    return jnp.sum(row, axis=1, keepdims=True).astype(jnp.int32)


def per_head(stat, base, c):
    lane = iota((M, QUAD), 1) // M
    out = jnp.zeros((M, QUAD), F32)
    for h in range(QUAD // M):
        at = base + c * (QUAD // M) + h
        out = jnp.where(lane == h, stat[:, at : at + 1], out)
    return out


def places():
    return [lax.axis_index(a) for a in ("mp", "seq", "dp")]


def greet(sizes):
    barrier = pltpu.get_barrier_semaphore()
    for axis, size in sizes.items():
        me = lax.axis_index(axis)
        for p in range(1, size):
            pl.semaphore_signal(
                barrier, inc=1, device_id={axis: lax.rem(me + p, size)}, device_id_type=MESH
            )
    return lambda: pl.semaphore_wait(barrier, sum(sizes.values()) - len(sizes))


def remote(src, dst, send, recv, axis, to):
    return pltpu.make_async_remote_copy(
        src_ref=src,
        dst_ref=dst,
        send_sem=send,
        recv_sem=recv,
        device_id={axis: to},
        device_id_type=MESH,
    )


def score_quad(c, q_ref, k_ref, v_ref, qm, km, minus, k1_ref, e_ref, mix_ref, stat):
    cols = slice(c * QUAD, (c + 1) * QUAD)
    tok = q_ref.shape[0]
    mask = block_mask()
    s1 = nt(spread_blocks(km[:, cols], mask), q_ref[:, cols]) * 0.125
    s1 = s1.reshape(QUAD // M, M, tok)
    e1 = jnp.exp(s1 - jnp.max(s1, axis=1, keepdims=True))
    k1 = e1 * (1.0 / jnp.sum(e1, axis=1, keepdims=True))
    k1_ref[cols, :] = k1.reshape(QUAD, tok).astype(BF)
    s3 = nt(spread_blocks(qm[:, cols], mask), k_ref[:, cols]) * 0.125 - minus
    top = jnp.max(s3, axis=1, keepdims=True)
    e3 = jnp.exp(s3 - top)
    total = jnp.sum(e3, axis=1, keepdims=True)
    e3 = e3.astype(BF)
    e_ref[cols, :] = e3
    mix_ref[:, cols] = gather_blocks(nn(e3, v_ref[:, cols])).astype(BF)
    lane = iota((M, 128), 1)
    for h in range(QUAD // M):
        at = c * (QUAD // M) + h
        stat = jnp.where(lane == at, top[h * M : (h + 1) * M], stat)
        stat = jnp.where(lane == 64 + at, total[h * M : (h + 1) * M], stat)
    return stat


def pseudo_inverse(qm, km, k2_ref, inv_ref, save_ref, sel):
    d = qm.shape[1]
    quads = d // QUAD
    mask = block_mask()
    ident = (iota((QUAD, QUAD), 0) == iota((QUAD, QUAD), 1)).astype(F32)
    kernel, z = [], []
    for c in range(quads):
        cols = slice(c * QUAD, (c + 1) * QUAD)
        s2 = nt(spread_blocks(qm[:, cols], mask), spread_blocks(km[:, cols], mask)) * 0.125
        s2 = jnp.where(mask, s2, -1e30)
        e2 = jnp.exp(s2 - jnp.max(s2, axis=1, keepdims=True))
        e2 = e2 / jnp.sum(e2, axis=1, keepdims=True)
        kernel.append(e2)
        sums = jnp.sum(e2, axis=0, keepdims=True)
        lane = iota((1, QUAD), 1) // M
        scale = jnp.zeros((1, QUAD), F32)
        for h in range(QUAD // M):
            best = jnp.max(jnp.where(lane == h, sums, 0.0), axis=1, keepdims=True)
            scale = jnp.where(lane == h, 1.0 / best, scale)
        z.append(e2.T * scale)
        k2_ref[:, cols] = gather_blocks(e2)

    def keep(it, kind, vals):
        for c in range(quads):

            @pl.when(sel == c)
            def _():
                save_ref[it, kind] = gather_blocks(vals[c]).astype(BF)

    ksp = [split(a) for a in kernel]

    def mul(a, b):
        return nn(a[0], b[0]) + (nn(a[0], b[1]) + nn(a[1], b[0]))

    for it in range(ITERS):
        zs = [split(a) for a in z]
        p = [mul(a, b) for a, b in zip(ksp, zs)]
        ps = [split(a) for a in p]
        i2 = [15.0 * ident - mul(a, split(7.0 * ident - b)) for a, b in zip(ps, p)]
        i3 = [13.0 * ident - mul(a, split(b)) for a, b in zip(ps, i2)]
        keep(it, 0, z)
        keep(it, 1, p)
        keep(it, 2, i2)
        keep(it, 3, i3)
        z = [0.25 * mul(a, split(b)) for a, b in zip(zs, i3)]
    for c in range(quads):
        inv_ref[:, c * QUAD : (c + 1) * QUAD] = gather_blocks(z[c])


def combine(mix_ref, stat_ref, inv_ref, me, cm_ref, lv_ref, gst_ref):
    n, _, d = mix_ref.shape
    lane = iota((M, 128), 1)
    top = stat_ref[0]
    for i in range(1, n):
        top = jnp.maximum(top, stat_ref[i])
    top = jnp.where(lane < 64, top, 0.0)
    total = jnp.zeros((M, 128), F32)
    scales = []
    for i in range(n):
        st = stat_ref[i]
        sc = jnp.where(lane < 64, jnp.exp(st - top), 0.0)
        scales.append(sc)
        total = total + sc * pltpu.roll(st, 64, 1)
    own = jnp.where(lane < 64, jnp.exp(stat_ref[me] - top), 0.0)
    gst_ref[...] = jnp.where(lane < 64, own, pltpu.roll(total, 64, 1))
    mask = block_mask()
    for c in range(d // QUAD):
        cols = slice(c * QUAD, (c + 1) * QUAD)
        mixed = jnp.zeros((M, QUAD), F32)
        for i in range(n):
            mixed = mixed + per_head(scales[i], 0, c) * mix_ref[i, :, cols].astype(F32)
        lv = mixed / per_head(total, 0, c)
        lv_ref[:, cols] = lv
        cm = three(nn, spread_blocks(inv_ref[:, cols], mask), spread_blocks(lv, mask))
        cm_ref[:, cols] = gather_blocks(cm).astype(BF)


def fill_lines(taps_ref, far_ref, line_ref, width):
    per = line_ref.shape[1] // 2
    turn = (iota((128, 128), 0) + iota((128, 128), 1) == width - 1).astype(BF)
    at = 64 - width // 2
    for first, ref in ((0, taps_ref), (per, far_ref)):
        taps = ref[...]
        back = nn(taps.astype(BF), turn)
        for i, x in ((0, taps), (1, back)):
            wide = jnp.concatenate([x, jnp.zeros(x.shape, F32)], axis=1)
            line_ref[i, first : first + per, :] = pltpu.roll(wide, at, 1)[:per]


def attend_kernel(
    inputs_any, pad_ref, wq0, wk0, wv0, taps_ref, wo_any, wu_any, wd_any,
    q_any, k_any, v_any, xt_any, k1_any, e_any, save_any, wq_any, wk_any, wv_any,
    xt_got, wo_got, wu_got, wd_got,
    marks, edge, cm_ref, lv_ref, gst_ref, inv_ref, k2_ref, line_ref,
    x, q, k, v, xt, k1, e, save, wq1, wk1, wv1, taps_own, taps_got,
    pack, mix, stat, mixes, stats, ship, send, recv, *, n, shape,
):
    idx = places()
    me, mate = idx[1], 1 - idx[0]
    tok, d = x.shape
    half = d // 2
    lm = tok // M
    ready = greet({"seq": n, "mp": 2})
    load = pltpu.make_async_copy(inputs_any.at[idx[0]], x, ship.at[0])
    load.start()
    moved = []

    def out(src, dst):
        c = pltpu.make_async_copy(src, dst, ship.at[1 + len(moved)])
        c.start()
        moved.append(c)

    peers = [lax.rem(me + p, n) for p in range(1, n)]
    sent = []

    def tell(src, dst, to, axis="seq"):
        c = remote(src, dst, send.at[len(sent)], recv.at[len(sent)], axis, to)
        c.start()
        sent.append(c)
        return c

    per, width = taps_ref.shape
    taps_own[...] = jnp.zeros_like(taps_own)
    taps_own[0:per, 0:width] = taps_ref[...]
    valid = pad_ref[pl.ds(idx[0], 1), :].astype(F32)
    keep_n = jnp.sum(valid, axis=1, keepdims=True).astype(jnp.int32) - me * tok
    keep = (iota((tok, 1), 0) < keep_n).astype(F32)
    count = jnp.maximum(jnp.sum(keep.reshape(lm, M, 1), axis=1), 1.0)
    ready()
    swaps = [tell(a, b, mate, "mp") for a, b in ((wq0, wq1), (wk0, wk1), (wv0, wv1))]
    late = [
        tell(a, b, mate, "mp")
        for a, b in ((taps_own, taps_got), (wo_any, wo_got), (wu_any, wu_got), (wd_any, wd_got))
    ]
    load.wait()

    def project(w, i, at, dst):
        cols = slice(i * half, (i + 1) * half)
        val = nn(x[...], w[...])
        if at is None:
            dst[:, cols] = (val * keep).astype(BF)
            return
        val = val.astype(BF)
        dst[:, cols] = val
        wide = (val.astype(F32) * keep).reshape(lm, M, half)
        pack[at : at + lm, cols] = (jnp.sum(wide, axis=1) / count).astype(BF)

    project(wq0, 0, 0, q)
    project(wk0, 0, lm, k)
    swaps[0].wait()
    project(wq1, 1, 0, q)
    swaps[1].wait()
    project(wk1, 1, lm, k)
    first = [tell(pack, marks.at[me], to) for to in peers]
    marks[me] = pack[...]
    project(wv0, 0, None, v)
    swaps[2].wait()
    project(wv1, 1, None, v)
    edges = [
        tell(v.at[pl.ds(tok - 16, 16)], edge.at[pl.ds(0, 16)], peers[0]),
        tell(v.at[pl.ds(0, 16)], edge.at[pl.ds(16, 16)], peers[n - 2]),
    ]
    store_chunks(xt, x[...].T, idx, shape)
    late.append(tell(xt, xt_got, mate, "mp"))
    for src, dst in (
        (q, q_any), (k, k_any), (v, v_any), (xt, xt_any), (wq1, wq_any), (wk1, wk_any), (wv1, wv_any),
    ):
        out(src, dst)
    for c in first:
        c.wait()
    qm = jnp.concatenate([marks[i, 0:lm, :] for i in range(n)], axis=0)
    km = jnp.concatenate([marks[i, lm : 2 * lm, :] for i in range(n)], axis=0)
    minus = jnp.where(iota((1, tok), 1) < keep_n, 0.0, 1000000000.0)
    st = jnp.zeros((M, 128), F32)
    for c in range(d // QUAD):
        st = score_quad(c, q, k, v, qm, km, minus, k1, e, mix, st)
    stat[...] = st
    second = [tell(a, b.at[me], to) for a, b in ((mix, mixes), (stat, stats)) for to in peers]
    mixes[me] = mix[...]
    stats[me] = stat[...]
    out(k1, k1_any)
    out(e, e_any)
    pseudo_inverse(qm, km, k2_ref, inv_ref, save, jnp.minimum(me, d // QUAD - 1))
    out(save, save_any)
    for c in second:
        c.wait()
    combine(mixes, stats, inv_ref, me, cm_ref, lv_ref, gst_ref)
    late[0].wait()
    fill_lines(taps_own, taps_got, line_ref, width)
    for c in edges + moved + late[1:]:
        c.wait()


def attend(n, inputs, padding, weights, taps, others, shape):
    _, tok, d = inputs.shape
    lm = tok // M
    flat, turned = sds((tok, d), BF), sds((d, tok), BF)
    save = sds((ITERS, 4, M, QUAD), BF)
    thin = sds(weights[0].shape, BF)
    big = [flat, flat, flat, turned, turned, turned, save, thin, thin, thin]
    far = [turned] + [sds(w.shape, BF) for w in others]
    heads = 2 * taps.shape[0]
    small = [
        sds((n, 2 * lm, d), BF),
        sds((32, d), BF),
        sds((M, d), BF),
        sds((M, d), F32),
        sds((M, 128), F32),
        sds((M, d), F32),
        sds((M, d), F32),
        sds((2, heads, 256), F32),
    ]
    vm = pl.BlockSpec(memory_space=pltpu.VMEM)
    count = 3 * (n - 1) + 2 + 8
    return pl.pallas_call(
        functools.partial(attend_kernel, n=n, shape=shape),
        in_specs=[ANY] + [vm] * 5 + [ANY] * 3,
        out_specs=[ANY] * (len(big) + len(far)) + [vm] * len(small),
        out_shape=big + far + small,
        scratch_shapes=[pltpu.VMEM(a.shape, a.dtype) for a in [flat] + big]
        + [
            pltpu.VMEM((8, 128), F32),
            pltpu.VMEM((8, 128), F32),
            pltpu.VMEM((2 * lm, d), BF),
            pltpu.VMEM((M, d), BF),
            pltpu.VMEM((M, 128), F32),
            pltpu.VMEM((n, M, d), BF),
            pltpu.VMEM((n, M, 128), F32),
            pltpu.SemaphoreType.DMA((12,)),
            pltpu.SemaphoreType.DMA((count,)),
            pltpu.SemaphoreType.DMA((count,)),
        ],
        compiler_params=params(56, collective_id=1, has_side_effects=True),
        cost_estimate=pl.CostEstimate(
            flops=6 * tok * d * d + 72 * 3 * 2 * QUAD**3,
            bytes_accessed=30 * tok * d,
            transcendentals=2 * tok * d,
        ),
        name="attend",
    )(inputs, padding, *weights, taps, *others)


def doc_bounds(doc_ref, idx):
    row = doc_ref[pl.ds(idx[0], 1), :]
    return [
        jnp.sum((row < j).astype(F32), axis=1, keepdims=True).astype(jnp.int32)
        for j in range(1, 9)
    ]


def docs_at(place, bounds, length):
    doc = jnp.zeros(place.shape, jnp.int32)
    for b in bounds:
        doc = doc + (place >= b).astype(jnp.int32)
    return jnp.where((place >= 0) & (place < length), doc, -1)


def fill_bands(line_ref, band_ref):
    for h in range(band_ref.shape[0]):
        wide = jnp.broadcast_to(line_ref[h : h + 1, :], band_ref.shape[1:])
        band_ref[h] = pltpu.roll(wide, 0, 1, stride=1, stride_axis=0).astype(BF)


def banded(band_ref, window, same, col0):
    lane = iota((band_ref.shape[1], 128), 1)
    first = nn(band_ref[col0] * same, window)
    second = nn(band_ref[col0 + 1] * same, window)
    return jnp.where(lane < 64, first, second)


def fill_halo(ext, body, edge_ref, tok):
    ext[0:48, :] = jnp.zeros((48, ext.shape[1]), BF)
    ext[48:64, :] = edge_ref[0:16, :]
    ext[64 : 64 + tok, :] = body[...]
    ext[64 + tok : 80 + tok, :] = edge_ref[16:32, :]
    ext[80 + tok :, :] = jnp.zeros((48, ext.shape[1]), BF)


def erf_parts(u):
    a = jnp.abs(u) * 0.7071067811865476
    e = jnp.exp(-0.5 * u * u)
    t = 1.0 / (1.0 + 0.3275911 * a)
    poly = t * (
        0.254829592
        + t * (-0.284496736 + t * (1.421413741 + t * (-1.453152027 + t * 1.061405429)))
    )
    tail = 0.5 * poly * e
    cdf = jnp.where(u < 0.0, tail, 1.0 - tail)
    return cdf, e * 0.3989422804014327


def norm_stats(h):
    mean = jnp.mean(h, axis=-1, keepdims=True)
    centre = h - mean
    rstd = lax.rsqrt(jnp.mean(centre * centre, axis=-1, keepdims=True) + EPS)
    return centre * rstd, rstd


def norm_back(g, hat, rstd):
    return rstd * (
        g
        - jnp.mean(g, axis=-1, keepdims=True)
        - hat * jnp.mean(g * hat, axis=-1, keepdims=True)
    )


def core_kernel(
    x_any,
    cot_any,
    pad_ref,
    doc_ref,
    v_ref,
    edge_ref,
    k1_ref,
    cm_ref,
    line_ref,
    wo0_any,
    wo1_any,
    wu0_any,
    wu1_any,
    wd0_any,
    wd1_any,
    ga_ref,
    sa_ref,
    gf_ref,
    sf_ref,
    ctx0,
    act0,
    du0,
    hat_ref,
    gh2_ref,
    rstd_ref,
    acc_ref,
    out_own,
    nlt_own,
    gh2t_own,
    du_own,
    out_got,
    nlt_got,
    gh2t_got,
    du_got,
    ctx_got,
    act_got,
    ext,
    band,
    wo,
    wu,
    wd,
    gp,
    x_all,
    cot_all,
    out2,
    nlt2,
    gh2t2,
    du2,
    ctx2,
    act2,
    sems,
    send,
    recv,
    local,
    *,
    tok,
    shape,
):
    idx = places()
    step = pl.program_id(0)
    steps = pl.num_programs(0)
    rows, d = hat_ref.shape
    half = d // 2
    ga, sa, gf, sf = (ref[...].reshape(1, d) for ref in (ga_ref, sa_ref, gf_ref, sf_ref))
    loads = [
        pltpu.make_async_copy(src, dst, sems.at[n])
        for n, (src, dst) in enumerate(
            [
                (wo0_any, wo.at[0]),
                (wo1_any, wo.at[1]),
                (wu0_any, wu.at[0]),
                (wu1_any, wu.at[1]),
                (wd0_any, wd.at[0]),
                (wd1_any, wd.at[1]),
                (x_any.at[idx[0]], x_all),
                (cot_any.at[idx[0]], cot_all),
            ]
        )
    ]

    def arrived(*which):
        @pl.when(step == 0)
        def _():
            for i in which:
                loads[i].wait()

    own = pl.multiple_of(step * rows, rows)
    slot = lax.rem(step, 2)
    moved = [
        (out2, out_got, out_own, False),
        (nlt2, nlt_got, nlt_own, True),
        (gh2t2, gh2t_got, gh2t_own, True),
        (du2, du_got, du_own, False),
        (ctx2, ctx_got, None, False),
        (act2, act_got, None, False),
    ]

    def copies(n, t, both=True):
        src, far, near, turned = moved[n]
        part = pl.ds(pl.multiple_of(t * rows, rows), rows)
        src = src.at[lax.rem(t, 2)]
        at = lambda ref: ref.at[:, part] if turned else ref.at[part]
        out = [remote(src, at(far), send.at[n, t], recv.at[n, t], "mp", 1 - idx[0])]
        if both and near is not None:
            out.append(pltpu.make_async_copy(src, at(near), local.at[n, t]))
        return out

    def give(n):
        for c in copies(n, step):
            c.start()

    def given(t):
        for n in range(len(moved)):
            c = copies(n, t)
            c[0].wait_send()
            if len(c) > 1:
                c[1].wait()

    @pl.when(step == 0)
    def _():
        ready = greet({"mp": 2})
        for i in (0, 1, 6, 2, 3, 4, 5, 7):
            loads[i].start()
        fill_halo(ext, v_ref, edge_ref, tok)
        fill_bands(line_ref.at[0], band)
        acc_ref[...] = jnp.zeros_like(acc_ref)
        ready()

    @pl.when(step >= 2)
    def _():
        given(step - 2)

    out_ref, nlt_ref, gh2t_ref, du1, ctx1, act1 = (m[0].at[slot] for m in moved)

    bounds = doc_bounds(doc_ref, idx)
    mask = block_mask()
    start = idx[1] * tok + step * rows
    parts = []
    for sub in range(rows // 128):
        place = start + sub * 128
        same = (
            docs_at(place + iota((128, 1), 0), bounds, LEN)
            == docs_at(place - 64 + iota((1, 256), 1), bounds, LEN)
        ).astype(BF)
        base = pl.multiple_of(step * rows + sub * 128, 128)
        cols = []
        for pair in range(d // 128):
            window = ext[pl.ds(base, 256), pair * 128 : (pair + 1) * 128]
            cols.append(banded(band, window, same, 2 * pair))
        parts.append(jnp.concatenate(cols, axis=1))
    conv = jnp.concatenate(parts, axis=0)
    ctxs = []
    for c in range(d // QUAD):
        cols = slice(c * QUAD, (c + 1) * QUAD)
        att = tn(k1_ref[cols, :], spread_blocks(cm_ref[:, cols], mask))
        ctxs.append((att + conv[:, cols]).astype(BF))
    ctx = jnp.concatenate(ctxs, axis=1)
    ctx0[...] = ctx[:, :half]
    ctx1[...] = ctx[:, half:]
    give(4)
    arrived(0, 1, 6)
    branch = nn(ctx[:, :half], wo[0]) + nn(ctx[:, half:], wo[1])
    xf = x_all[pl.ds(own, rows), :].astype(F32)
    hat1, rstd1 = norm_stats(xf + branch)
    hat_ref[...] = hat1.astype(BF)
    rstd_ref[...] = jnp.broadcast_to(rstd1, rstd_ref.shape)
    normed = hat1 * ga + sa
    nl = normed.astype(BF)
    store_chunks(nlt_ref, nl.T, idx, shape)
    give(1)
    arrived(2, 3)
    chunk = 512
    hidden = wu.shape[2]
    for i, act in ((0, act0), (1, act1)):
        for at in range(0, hidden, chunk):
            cols = slice(at, at + chunk)
            u = nn(nl, wu[i, :, cols])
            cdf, pdf = erf_parts(u)
            act[:, cols] = (u * cdf).astype(BF)
            gp[i, :, cols] = (cdf + u * pdf).astype(BF)
    give(5)
    arrived(4, 5, 7)
    ffn = nn(act0[...], wd[0]) + nn(act1[...], wd[1])
    hat2, rstd2 = norm_stats(normed + ffn)
    out_ref[...] = (hat2 * gf + sf).astype(BF)
    give(0)
    cot = cot_all[pl.ds(own, rows), :].astype(F32)
    gh2 = norm_back(cot * gf, hat2, rstd2)
    low = gh2.astype(BF)
    gh2_ref[...] = low
    store_chunks(gh2t_ref, low.T, idx, shape)
    give(2)
    for i, du in ((0, du0), (1, du1)):
        for at in range(0, hidden, chunk):
            cols = slice(at, at + chunk)
            du[:, cols] = (nt(low, wd[i, cols, :]) * gp[i, :, cols].astype(F32)).astype(BF)
    give(3)
    keep_n = valid_count(pad_ref, idx) - start
    keep = (iota((rows, 1), 0) < keep_n).astype(F32)
    acc_ref[2:3, :] += jnp.sum(cot * hat2, axis=0, keepdims=True)
    acc_ref[3:4, :] += jnp.sum(cot, axis=0, keepdims=True)
    acc_ref[4:5, :] += jnp.sum(xf * xf * keep, axis=0, keepdims=True)
    acc_ref[5:6, :] += jnp.sum(branch * branch * keep, axis=0, keepdims=True)
    acc_ref[6:7, :] += jnp.sum(ffn * ffn * keep, axis=0, keepdims=True)

    @pl.when(step == steps - 1)
    def _():
        given(steps - 2)
        given(steps - 1)
        for n in range(len(moved)):
            for t in range(tok // rows):
                copies(n, t, False)[0].wait_recv()


def core(inputs, cot, padding, documents, v, edge, k1, cm, lines, wo, wu, wd, vecs, shape):
    tok, d = v.shape
    rows = 256
    steps = tok // rows
    f2 = wu[0].shape[1]
    heads = lines.shape[1]
    blk = lambda i: (i, 0)
    flat = pl.BlockSpec((rows, d), blk)
    part = pl.BlockSpec((rows, d // 2), blk)
    turned = pl.BlockSpec((d, rows), lambda i: (0, i))
    wide = pl.BlockSpec((rows, f2), blk)
    full, t = sds((tok, d), BF), sds((d, tok), BF)
    thin, broad = sds((tok, d // 2), BF), sds((tok, f2), BF)
    return pl.pallas_call(
        functools.partial(core_kernel, tok=tok, shape=shape),
        grid=(steps,),
        in_specs=[ANY] * 2
        + [whole(a.shape) for a in (padding, documents, v, edge)]
        + [turned]
        + [whole(a.shape) for a in (cm, lines)]
        + [ANY] * 6
        + [whole((d,))] * 4,
        out_specs=[part, wide, wide, flat, flat, pl.BlockSpec((rows, 128), blk), whole((8, d))]
        + [ANY] * 10,
        out_shape=[thin, broad, broad, full, full, sds((tok, 128), F32), sds((8, d), F32)]
        + [full, t, t, broad] * 2
        + [thin, broad],
        scratch_shapes=[
            pltpu.VMEM((tok + 128, d), BF),
            pltpu.VMEM((heads, 128, 256), BF),
            pltpu.VMEM((2, d // 2, d), BF),
            pltpu.VMEM((2, d, f2), BF),
            pltpu.VMEM((2, f2, d), BF),
            pltpu.VMEM((2, rows, f2), BF),
            pltpu.VMEM((tok, d), BF),
            pltpu.VMEM((tok, d), BF),
            pltpu.VMEM((2, rows, d), BF),
            pltpu.VMEM((2, d, rows), BF),
            pltpu.VMEM((2, d, rows), BF),
            pltpu.VMEM((2, rows, f2), BF),
            pltpu.VMEM((2, rows, d // 2), BF),
            pltpu.VMEM((2, rows, f2), BF),
            pltpu.SemaphoreType.DMA((8,)),
            pltpu.SemaphoreType.DMA((6, steps)),
            pltpu.SemaphoreType.DMA((6, steps)),
            pltpu.SemaphoreType.DMA((4, steps)),
        ],
        compiler_params=params(60, collective_id=2, has_side_effects=True),
        cost_estimate=pl.CostEstimate(
            flops=16 * tok * d * f2, bytes_accessed=60 * tok * d, transcendentals=4 * tok * f2
        ),
        name="core",
    )(inputs, cot, padding, documents, v, edge, k1, cm, lines, *wo, *wu, *wd, *vecs)


class Sum:
    def __init__(self, idx, slots, got1=None, got2=None, parts=None, got3=None, send=None, recv=None):
        self.idx = idx
        self.slots, self.got1, self.fast = slots, got1, got1 is not None
        self.got2, self.parts, self.got3 = got2, parts, got3
        self.send, self.recv = send, recv
        self.live = []

    @staticmethod
    def shapes(d, n):
        q = d // 4
        ch = q // 4
        return [
            pltpu.VMEM((4, 2 * q, n), BF),
            pltpu.VMEM((2, 2 * q, n), BF),
            pltpu.VMEM((2, q, n), BF),
            pltpu.VMEM((4, ch, 2 * n), BF),
            pltpu.VMEM((3, ch, 2 * n), BF),
            pltpu.SemaphoreType.DMA((7,)),
            pltpu.SemaphoreType.DMA((7,)),
        ]

    def start(self, n, src, dst, axis, to):
        c = remote(src, dst, self.send.at[n], self.recv.at[n], axis, to)
        c.start()
        self.live.append(c)

    def arrived(self):
        for c in self.live:
            c.wait()
        self.live = []

    def store(self, part, cols, acc):
        q = acc.shape[0] // 4
        if part == 0:
            self.slots[1, :, cols] = acc[: 2 * q]
            self.slots[0, :, cols] = acc[2 * q :]
        else:
            self.slots[3, :q, cols] = acc[:q]
            self.slots[2, :q, cols] = acc[q : 2 * q]
            self.slots[3, q:, cols] = acc[2 * q : 3 * q]
            self.slots[2, q:, cols] = acc[3 * q :]

    def step0(self, part):
        if self.fast:
            bit = 1 + part
            self.start(part, self.slots.at[2 * part], self.got1.at[part], "seq", self.idx[1] ^ bit)

    def step1(self):
        if not self.fast:
            return
        self.arrived()
        q = self.got2.shape[1]
        for part in range(2):
            at = 2 * part + 1
            self.slots[at] = (self.slots[at].astype(F32) + self.got1[part].astype(F32)).astype(BF)
            bit = 2 - part
            src = self.slots.at[at, pl.ds(q, q)]
            self.start(2 + part, src, self.got2.at[part], "seq", self.idx[1] ^ bit)

    def step2(self):
        if not self.fast:
            return
        self.arrived()
        _, q, n = self.got2.shape
        ch = self.parts.shape[1]
        for part in range(2):
            mine = self.slots[2 * part + 1, :q].astype(F32) + self.got2[part].astype(F32)
            for p in range(4):
                rows = slice(p * ch, (p + 1) * ch)
                self.parts[p, :, part * n : (part + 1) * n] = mine[rows].astype(BF)
        for p in range(1, 4):
            self.start(3 + p, self.parts.at[p], self.got3.at[p - 1], "dp", self.idx[2] ^ p)

    def finish(self):
        self.arrived()
        out = self.parts[0].astype(F32)
        for p in range(3):
            out = out + self.got3[p].astype(F32)
        return out


def sum_any(full):
    part = lax.psum_scatter(full.astype(F32), "dp", scatter_dimension=0, tiled=True)
    return lax.psum_scatter(part, "seq", scatter_dimension=0, tiled=True)


def joined(send_a, keep_a, send_b, keep_b):
    q = keep_a.shape[0] // 2
    b = jnp.concatenate([keep_b[:q], send_b[:q], keep_b[q:], send_b[q:]], axis=0)
    return jnp.concatenate([jnp.concatenate([keep_a, send_a], axis=0), b], axis=1)


def first_quad(c, q_ref, k1_ref, gc_ref, cm_ref, km, gq_ref, mix_ref, km_ref):
    cols = slice(c * QUAD, (c + 1) * QUAD)
    tok = q_ref.shape[0]
    mask = block_mask()
    kmb = spread_blocks(km[:, cols], mask)
    gc = gc_ref[:, cols]
    k1 = k1_ref[cols, :]
    mix_ref[:, cols] = gather_blocks(nn(k1, gc)).astype(BF)
    g = nt(spread_blocks(cm_ref[:, cols], mask), gc).reshape(QUAD // M, M, tok)
    kf = k1.astype(F32).reshape(QUAD // M, M, tok)
    inner = jnp.sum(g * kf, axis=1, keepdims=True)
    g1 = (kf * (g - inner)).reshape(QUAD, tok).astype(BF)
    km_ref[:, cols] = gather_blocks(nn(g1, q_ref[:, cols])) * 0.125
    gq_ref[:, cols] = (tn(g1, kmb) * 0.125).astype(BF)


def middle(gmix_ref, lv_ref, inv_ref, gst_ref, gm_ref, gt_ref):
    n = gmix_ref.shape[0]
    d = lv_ref.shape[1]
    mask = block_mask()
    lane = iota((M, 128), 1)
    head = iota((M, QUAD), 1) // M
    stat = gst_ref[...]
    gt = jnp.zeros((M, 128), F32)
    for c in range(d // QUAD):
        cols = slice(c * QUAD, (c + 1) * QUAD)
        gmix = jnp.zeros((M, QUAD), F32)
        for i in range(n):
            gmix = gmix + gmix_ref[i, :, cols].astype(F32)
        glv = gather_blocks(
            three(tn, spread_blocks(inv_ref[:, cols], mask), spread_blocks(gmix, mask))
        )
        scale = per_head(stat, 0, c)
        total = per_head(stat, 64, c)
        gm_ref[:, cols] = ((glv / total).astype(BF).astype(F32) * scale).astype(BF)
        prod = glv * lv_ref[:, cols]
        for h in range(QUAD // M):
            at = c * (QUAD // M) + h
            s = jnp.sum(jnp.where(head == h, prod, 0.0), axis=1, keepdims=True)
            gt = jnp.where(lane == at, -s / stat[:, 64 + at : 65 + at] * stat[:, at : at + 1], gt)
    gt_ref[...] = gt


def pinv_back(gmix_ref, lv_ref, k2_ref, save_ref, qm, km, cols, use):
    n = gmix_ref.shape[0]
    mask = block_mask()
    ident = (iota((QUAD, QUAD), 0) == iota((QUAD, QUAD), 1)).astype(F32)
    gmix = jnp.zeros((M, QUAD), F32)
    for i in range(n):
        gmix = gmix + gmix_ref[i, :, cols].astype(F32)
    dz = three(nt, spread_blocks(gmix, mask), spread_blocks(lv_ref[:, cols], mask))
    kernel = spread_blocks(k2_ref[:, cols], mask)
    klow = kernel.astype(BF)
    dk = jnp.zeros((QUAD, QUAD), F32)
    ibf = ident.astype(BF)
    for it in range(ITERS - 1, -1, -1):
        z, p, i2, i3 = (spread_blocks(save_ref[it, kind], mask) for kind in range(4))
        i1 = 7.0 * ibf - p
        dlow = dz.astype(BF)
        d3 = (0.25 * tn(z, dlow)).astype(BF)
        dp = nt(d3, i2)
        d2 = (-tn(p, d3)).astype(BF)
        dp = dp + nt(d2, i1)
        d1 = -tn(p, d2)
        dp = (-dp - d1).astype(BF)
        dz = 0.25 * nt(dlow, i3) + tn(klow, dp)
        dk = dk + nt(dp, z)
    sums = jnp.sum(kernel, axis=0, keepdims=True)
    lane = iota((1, QUAD), 1) // M
    dzt = jnp.where(mask, dz, 0.0).T
    dsum = jnp.sum(dzt * kernel, axis=0, keepdims=True)
    scale = jnp.zeros((1, QUAD), F32)
    extra = jnp.zeros((1, QUAD), F32)
    for h in range(QUAD // M):
        mine = lane == h
        best = jnp.max(jnp.where(mine, sums, 0.0), axis=1, keepdims=True)
        dscale = jnp.sum(jnp.where(mine, dsum, 0.0), axis=1, keepdims=True)
        is_best = (mine & (sums == best)).astype(F32)
        share = is_best / jnp.sum(is_best, axis=1, keepdims=True)
        scale = jnp.where(mine, 1.0 / best, scale)
        extra = jnp.where(mine, -dscale / (best * best) * share, extra)
    dk = dk + dzt * scale + extra
    inner = jnp.sum(jnp.where(mask, dk * kernel, 0.0), axis=1, keepdims=True)
    g2 = kernel * (dk - inner)
    g2h, g2l = split(g2)
    kb, qb = spread_blocks(km, mask), spread_blocks(qm, mask)
    use = use * 0.125
    return (
        gather_blocks(nn(g2h, kb) + nn(g2l, kb)) * use,
        gather_blocks(tn(g2h, qb) + tn(g2l, qb)) * use,
    )


def conv_quad(
    c, v_ref, vedge_ref, gc_ref, gedge_ref, bounds, start, line_ref, gv_ref, gtap_ref,
    vext, gext, band, pairs,
):
    heads = QUAD // M
    tok = v_ref.shape[0]
    at = pl.multiple_of(c * QUAD, QUAD)
    cols = pl.ds(at, QUAD)
    fill_halo(vext, v_ref.at[:, cols], vedge_ref.at[:, cols], tok)
    fill_halo(gext, gc_ref.at[:, cols], gedge_ref.at[:, cols], tok)
    fill_bands(line_ref.at[c], band)
    low64 = iota((128, 128), 1) < M
    pairs[...] = jnp.zeros_like(pairs)
    for sub in range(tok // 128):
        place = start + sub * 128
        same = docs_at(place + iota((128, 1), 0), bounds, LEN) == docs_at(
            place - 64 + iota((1, 256), 1), bounds, LEN
        )
        low = same.astype(BF)
        rows = slice(sub * 128, sub * 128 + 128)
        for pair in range(heads // 2):
            lanes = slice(pair * 128, pair * 128 + 128)
            back = banded(band, gext[sub * 128 : sub * 128 + 256, lanes], low, 2 * pair)
            wide = pl.ds(pl.multiple_of(at + pair * 128, 128), 128)
            gv_ref[rows, wide] = back.astype(BF)
            g = gc_ref[rows, wide]
            win = vext[sub * 128 : sub * 128 + 256, lanes]
            for h in range(2):
                own = jnp.where(low64 == (h == 0), g, jnp.zeros((), BF))
                pairs[2 * pair + h] += jnp.where(same, nt(own, win), 0.0)
    for h in range(heads):
        tall = pairs[h, 0:8]
        for r in range(8, 128, 8):
            tall = tall + pltpu.roll(pairs[h, r : r + 8], 256 - r, 1)
        line = tall[0:1]
        for r in range(1, 8):
            line = line + pltpu.roll(tall[r : r + 1], 256 - r, 1)
        gtap_ref[pl.ds(c * heads + h, 1), :] = line


def att_quad(c, k_ref, v_ref, e_ref, gm_ref, gt_ref, qm, keep_n, gv_ref, qm_ref):
    heads = QUAD // M
    tok = k_ref.shape[0]
    cols = slice(c * QUAD, (c + 1) * QUAD)
    mask = block_mask()
    qm = spread_blocks(qm[:, cols], mask)
    gm = spread_blocks(gm_ref[:, cols], mask)
    gt = jnp.concatenate(
        [gt_ref[:, c * heads + h : c * heads + h + 1] for h in range(heads)], axis=0
    )
    e = e_ref[cols, :]
    g3 = (e.astype(F32) * (nt(gm, v_ref[:, cols]) + gt)).astype(BF)
    qm_ref[:, cols] = gather_blocks(nn(g3, k_ref[:, cols])) * 0.125
    k_ref[:, cols] = (tn(g3, qm) * 0.125).astype(BF)
    keep = iota((tok, 1), 0) < keep_n
    gv = gv_ref[:, cols].astype(F32) + tn(e, gm)
    gv_ref[:, cols] = jnp.where(keep, gv, 0.0).astype(BF)


def back_kernel(*refs, n, dp_n, fast):
    (
        pad_ref, doc_ref, line_ref, marks, cm_ref, lv_ref, inv_ref, gst_ref, k2_ref, vedge, acc_ref,
        vec_ref, rstd_ref,
        k1_any, q_any, k_any, v_any, e_any, save_any,
        gh2t_any, gh2t_got, nlt_any, nlt_got, act0, act_got, du0, du_got, du1,
        hat_any, gh2_any, ctx0, ctx_got, xt_any, xt_got,
        wq0, wq1, wk0, wk1, wv0, wv1, wu0, wu1, wo0, wo1, *rest,
    ) = refs
    gin_own, gin_got, gh1t_own, gh1t_got, small_out, *rest = rest
    outs, rest = (rest[:4], rest[4:]) if fast else (rest[:16], rest[16:])
    (
        k1, gc, q, k, v, e, save, lhs, rhs, wu, wo, dus, gh1, gh1t, gv, far, res,
        gedge, mix, mixes, gm, gt, gkm, gqm, both, got, acc, small, smalls, small_got, rests, gtap,
        vext, gext, band, pairs,
        loads, stream, rows_in, turns, ship, send, recv, *rest,
    ) = rest
    idx = places()
    me, mate = idx[1], 1 - idx[0]
    tok, d = q.shape
    half = d // 2
    lm = tok // M
    quads = d // QUAD
    sizes = {"seq": n, "mp": 2}
    if fast:
        sizes["dp"] = dp_n
    ready = greet(sizes)
    sums = []
    for g in range(4):
        sums.append(Sum(idx, *rest[7 * g : 7 * g + 7]) if fast else Sum(idx, rest[g]))
    down, up, ov, qk = sums

    names = {}

    def fetch(name, src, dst):
        names[name] = pltpu.make_async_copy(src, dst, loads.at[len(names)])
        names[name].start()

    def fetched(*which):
        for w in which:
            names[w].wait()

    width = rhs.shape[3]
    blocks = act0.shape[1] // width
    work = [(g, j) for g in range(2) for j in range(blocks)]

    def block(i):
        g, j = work[i]
        cols = pl.ds(j * width, width)
        srcs = (act0, act_got) if g == 0 else (du0, du_got)
        return [
            pltpu.make_async_copy(src.at[:, cols], rhs.at[i % 2, t], stream.at[i % 2, t])
            for t, src in enumerate(srcs)
        ]

    fetch("gh2t", gh2t_any, lhs.at[0])
    for c in block(0):
        c.start()
    fetch("gh2t_got", gh2t_got, lhs.at[1])
    fetch("nlt", nlt_any, lhs.at[2])
    fetch("nlt_got", nlt_got, lhs.at[3])
    fetch("wu0", wu0, wu.at[0])
    fetch("wu1", wu1, wu.at[1])
    fetch("wo0", wo0, wo.at[0])
    fetch("wo1", wo1, wo.at[1])
    fetch("hat", hat_any, k)
    fetch("gh2", gh2_any, v)
    for name, src, dst in (("k1", k1_any, k1), ("q", q_any, q), ("e", e_any, e), ("save", save_any, save)):
        fetch(name, src, dst)
    sent = []

    def tell(src, dst, to, axis="seq"):
        c = remote(src, dst, send.at[len(sent)], recv.at[len(sent)], axis, to)
        c.start()
        sent.append(c)
        return c

    peers = [lax.rem(me + p, n) for p in range(1, n)]

    def products(g, left, right):
        for j in range(blocks):
            i = g * blocks + j
            if i + 1 < len(work):
                for c in block(i + 1):
                    c.start()
            for c in block(i):
                c.wait()
            acc_w = nn(left, rhs[i % 2, 0]) + nn(right, rhs[i % 2, 1])
            part, at = j // (blocks // 2), (j % (blocks // 2)) * width
            sums[g].store(part, slice(at, at + width), acc_w.astype(BF))
            if (j + 1) % (blocks // 2) == 0:
                if g == 0 and part == 0:
                    ready()
                sums[g].step0(part)

    fetched("gh2t", "gh2t_got")
    products(0, lhs[0], lhs[1])
    fetched("nlt", "nlt_got")
    products(1, lhs[2], lhs[3])

    rows = dus.shape[2]
    steps = tok // rows

    def du_rows(i):
        at = pl.ds(i * rows, rows)
        return [
            pltpu.make_async_copy(src.at[at], dus.at[i % 2, t], rows_in.at[i % 2, t])
            for t, src in enumerate((du0, du1))
        ]

    def turn(i):
        at = pl.ds(i * rows, rows)
        src = gh1t.at[i % 2]
        return (
            pltpu.make_async_copy(src, gh1t_own.at[:, at], turns.at[0, i]),
            remote(src, gh1t_got.at[:, at], turns.at[1, i], turns.at[2, i], "mp", mate),
        )

    for c in du_rows(0):
        c.start()
    fetched("wu0", "wu1", "wo0", "wo1", "hat", "gh2")
    acc[...] = acc_ref[...]
    turned = [turn(i) for i in range(steps)]
    shape = (dp_n if fast else 0, n, d // (n * dp_n))
    for i in range(steps):
        if i + 1 < steps:
            for c in du_rows(i + 1):
                c.start()
        for c in du_rows(i):
            c.wait()
        at = slice(i * rows, (i + 1) * rows)
        gn = v[at].astype(F32) + nt(dus[i % 2, 0], wu[0]) + nt(dus[i % 2, 1], wu[1])
        hat = k[at].astype(F32)
        acc[0:1, :] += jnp.sum(gn * hat, axis=0, keepdims=True)
        acc[1:2, :] += jnp.sum(gn, axis=0, keepdims=True)
        low = norm_back(gn * vec_ref[...].reshape(1, d), hat, rstd_ref[at, 0:1]).astype(BF)
        gh1[at] = low
        if i >= 2:
            turned[i - 2][0].wait()
            turned[i - 2][1].wait_send()
        store_chunks(gh1t.at[i % 2], low.T, idx, shape)
        turned[i][0].start()
        turned[i][1].start()
        gc[at, :half] = nt(low, wo[0]).astype(BF)
        gc[at, half:] = nt(low, wo[1]).astype(BF)
    fetch("k", k_any, k)
    fetch("v", v_any, v)
    for i, w in enumerate((wq0, wq1, wk0, wk1)):
        fetch("w%d" % i, w, wu.at[0, :, pl.ds(i * half, half)])
    for i, w in enumerate((wv0, wv1)):
        fetch("w%d" % (4 + i), w, wu.at[1, :, pl.ds(i * half, half)])
    fetch("xt", xt_any, lhs.at[2])
    fetch("xt_got", xt_got, lhs.at[3])

    qm = jnp.concatenate([marks[i, 0:lm, :] for i in range(n)], axis=0)
    km = jnp.concatenate([marks[i, lm : 2 * lm, :] for i in range(n)], axis=0)
    swaps = [
        tell(gc.at[pl.ds(tok - 16, 16)], gedge.at[pl.ds(0, 16)], peers[0]),
        tell(gc.at[pl.ds(0, 16)], gedge.at[pl.ds(16, 16)], peers[n - 2]),
    ]
    fetched("k1", "q")
    for c in range(quads):
        first_quad(c, q, k1, gc, cm_ref, km, q, mix, gkm)
    swaps_mix = [tell(mix, mixes.at[me], to) for to in peers]
    mixes[me] = mix[...]
    down.step1()

    for i in range(max(steps - 2, 0), steps):
        turned[i][0].wait()
        turned[i][1].wait_send()
    for i in range(steps):
        turned[i][1].wait_recv()
    fetch("gh1t", gh1t_own, lhs.at[0])
    fetch("gh1t_got", gh1t_got, lhs.at[1])
    for t, src in enumerate((ctx0, ctx_got)):
        fetch("ctx%d" % t, src.at[:, pl.ds(0, width)], rhs.at[0, t])
        fetch("ctx%d" % (2 + t), src.at[:, pl.ds(width, half - width)], rhs.at[1, t, :, pl.ds(0, half - width)])
    valid = pad_ref[pl.ds(idx[0], 1), :].astype(F32)
    keep_n = jnp.sum(valid, axis=1, keepdims=True).astype(jnp.int32) - me * tok
    bounds = doc_bounds(doc_ref, idx)
    fetched("v")
    for c in swaps:
        c.wait()

    @pl.loop(0, quads)
    def _(c):
        conv_quad(
            c, v, vedge, gc, gedge, bounds, me * tok, line_ref, gv, gtap, vext, gext, band, pairs
        )

    fetched("gh1t", "gh1t_got", "ctx0", "ctx1", "ctx2", "ctx3")
    acc_w = nn(lhs[0], rhs[0, 0]) + nn(lhs[1], rhs[0, 1])
    ov.store(0, slice(0, width), acc_w.astype(BF))
    acc_w = nn(lhs[0], rhs[1, 0, :, : half - width]) + nn(lhs[1], rhs[1, 1, :, : half - width])
    ov.store(0, slice(width, half), acc_w.astype(BF))
    ov.step0(0)

    for c in swaps_mix:
        c.wait()
    middle(mixes, lv_ref, inv_ref, gst_ref, gm, gt)
    fetched("k", "e")
    for c in range(quads):
        att_quad(c, k, v, e, gm, gt, qm, keep_n, gv, gqm)
    swap_v = tell(gv.at[:, pl.ds(half, half)], far.at[0], mate, "mp")
    up.step1()
    down.step2()
    fetched("save")
    sel = jnp.minimum(me, quads - 1)
    cols = pl.ds(pl.multiple_of(sel * QUAD, QUAD), QUAD)
    use = (me < quads).astype(F32)
    qm_sel = jnp.concatenate([marks[i, 0:lm, cols] for i in range(n)], axis=0)
    km_sel = jnp.concatenate([marks[i, lm : 2 * lm, cols] for i in range(n)], axis=0)
    two_q, two_k = pinv_back(mixes, lv_ref, k2_ref, save, qm_sel, km_sel, cols, use)
    gqm[:, cols] += two_q
    gkm[:, cols] += two_k
    for i in range(n):
        part = slice(i * lm, (i + 1) * lm)
        both[i, :lm] = gqm[part].astype(BF)
        both[i, lm:] = gkm[part].astype(BF)
    pieces = d // 128
    for r in range(4):
        for b in range(pieces):
            at = r * pieces + b
            small[at : at + 1, :] = acc[r : r + 1, b * 128 : (b + 1) * 128]
    lines = 4 * pieces
    heads = gtap.shape[0]
    small[lines : lines + 2 * heads, :] = jnp.concatenate([gtap[:, :128], gtap[:, 128:]], axis=0)
    squares = jnp.sum(acc[...], axis=1, keepdims=True)
    small[lines + 2 * heads :, :] = jnp.broadcast_to(squares, (8, 128))
    swaps = [tell(both.at[to], got.at[me], to) for to in peers]
    swaps_small = [tell(small, smalls.at[me], to) for to in peers]
    got[me] = both[me]
    smalls[me] = small[...]

    fetched("xt", "xt_got")
    acc_w = nn(lhs[2], gv[:, :half])
    swap_v.wait()
    ov.store(1, slice(0, half), (acc_w + nn(lhs[3], far[0])).astype(BF))
    ov.step0(1)
    for c in swaps:
        c.wait()
    spread(q, k, got, keep_n)
    swaps = [
        tell(q.at[:, pl.ds(half, half)], far.at[1], mate, "mp"),
        tell(k.at[:, pl.ds(half, half)], far.at[2], mate, "mp"),
    ]
    for c in swaps_small:
        c.wait()
    total = smalls[0]
    for i in range(1, n):
        total = total + smalls[i]
    small[...] = total
    swap_small = tell(small, small_got, mate, "mp")
    up.step2()
    for i, src in ((0, q), (1, k)):
        acc_w = nn(lhs[2], src[:, :half])
        swaps[i].wait()
        qk.store(i, slice(0, half), (acc_w + nn(lhs[3], far[1 + i])).astype(BF))
        qk.step0(i)
    ov.step1()

    fetched(*["w%d" % i for i in range(6)])
    tall = res.shape[0]
    own = pl.multiple_of(idx[0] * half, half)
    other = pl.multiple_of(mate * half, half)
    swap_gin = []
    keep_gin = []
    for i in range(tok // tall):
        at = slice(i * tall, (i + 1) * tall)
        lhs_i = jnp.concatenate([q[at, :], k[at, :]], axis=1)
        res[...] = gh1[at].astype(F32) + nt(lhs_i, wu[0]) + nt(gv[at, :], wu[1, :, :d])
        mine = dus.at[i // 2, i % 2]
        mine[:, :half] = res[:, pl.ds(own, half)].astype(BF)
        mine[:, half:d] = res[:, pl.ds(other, half)].astype(BF)
        part = pl.ds(i * tall, tall)
        swap_gin.append(tell(mine.at[:, pl.ds(half, half)], gin_got.at[part], mate, "mp"))
        c = pltpu.make_async_copy(mine.at[:, pl.ds(0, half)], gin_own.at[part], ship.at[i])
        c.start()
        keep_gin.append(c)
    swap_small.wait()
    mine = small[...]
    theirs = small_got[...]
    per = heads // 2
    taps_a = mine[lines : lines + 2 * heads]
    taps_b = theirs[lines : lines + 2 * heads]
    rests[0, :lines] = mine[:lines] + theirs[:lines]
    rests[0, lines : lines + per] = taps_a[:per] + taps_b[per:heads]
    rests[0, lines + per : lines + heads] = taps_a[heads : heads + per] + taps_b[heads + per :]
    for row, part in ((idx[0], mine), (mate, theirs)):
        real = jnp.sum(pad_ref[pl.ds(row, 1), :].astype(F32), axis=1, keepdims=True)
        at = pl.multiple_of(8 * row, 8)
        small_out[pl.ds(at, 8), :] = jnp.sqrt(part[lines + 2 * heads :] / (real * d) + 1e-06)
    if fast:
        norms = [tell(rests.at[0], rests.at[p], idx[2] ^ p, "dp") for p in range(1, dp_n)]
        ov.step2()
        qk.step1()
        outs[0][...] = down.finish()
        outs[1][...] = up.finish()
        qk.step2()
        for c in norms:
            c.wait()
        total = rests[0]
        for p in range(1, dp_n):
            total = total + rests[p]
        small_out[16:] = total
        outs[2][...] = ov.finish()
        outs[3][...] = qk.finish()
    else:
        small_out[16:] = rests[0]
        for g in range(4):
            for i in range(4):
                c = pltpu.make_async_copy(rest[g].at[i], outs[4 * g + i], ship.at[4])
                c.start()
                c.wait()
    for c in swap_gin + keep_gin:
        c.wait()


def spread(gq_ref, gk_ref, got_ref, keep_n):
    n, lm = got_ref.shape[0], got_ref.shape[1] // 2
    got = got_ref[0].astype(F32)
    for i in range(1, n):
        got = got + got_ref[i].astype(F32)
    for j in range(lm):
        rows = slice(j * M, (j + 1) * M)
        keep = (iota((M, 1), 0) < keep_n - j * M).astype(F32)
        share = keep / jnp.maximum(jnp.sum(keep, axis=0, keepdims=True), 1.0)
        for at, ref in ((0, gq_ref), (lm, gk_ref)):
            ref[rows] = (ref[rows].astype(F32) + got[at + j : at + j + 1] * share).astype(BF)


def back(n, dp_n, fast, near, far):
    lines, marks = near[2], near[3]
    tok, d = far[1].shape
    f2 = far[10].shape[1]
    half = d // 2
    lm = tok // M
    heads = lines.shape[1]
    near = list(near)
    near[2] = lines[1].reshape(d // QUAD, QUAD // M, lines.shape[2])
    flat, turned, thin = (tok, d), (d, tok), (tok, half)
    pieces = 4 * (d // 128)
    small = (pieces + 2 * heads + 8, 128)
    vm = pl.BlockSpec(memory_space=pltpu.VMEM)
    sems = pltpu.SemaphoreType.DMA
    out_shape = [sds(thin, BF)] * 2 + [sds(turned, BF)] * 2 + [sds((pieces + heads + 16, 128), F32)]
    out_specs = [ANY] * 4 + [vm]
    widths = (f2, f2, d, d)
    tail = []
    for w in widths:
        if fast:
            out_shape.append(sds((d // (n * dp_n), w), F32))
            out_specs.append(vm)
            tail += Sum.shapes(d, w // 2)
        else:
            out_shape += [sds((half, w // 2), BF)] * 4
            out_specs += [ANY] * 4
            tail.append(pltpu.VMEM((4, half, w // 2), BF))
    count = 40
    scratch = [
        pltpu.VMEM(turned, BF),
        *[pltpu.VMEM(flat, BF)] * 4,
        pltpu.VMEM(turned, BF),
        pltpu.VMEM((ITERS, 4, M, QUAD), BF),
        pltpu.VMEM((4,) + turned, BF),
        pltpu.VMEM((2, 2, tok, QUAD), BF),
        pltpu.VMEM((2, d, f2), BF),
        pltpu.VMEM((2, half, d), BF),
        pltpu.VMEM((2, 2, 256, f2), BF),
        pltpu.VMEM(flat, BF),
        pltpu.VMEM((2, d, 256), BF),
        pltpu.VMEM(flat, BF),
        pltpu.VMEM((3,) + thin, BF),
        pltpu.VMEM((256, d), F32),
        pltpu.VMEM((32, d), BF),
        pltpu.VMEM((M, d), BF),
        pltpu.VMEM((n, M, d), BF),
        pltpu.VMEM((M, d), BF),
        pltpu.VMEM((M, 128), F32),
        pltpu.VMEM((M, d), F32),
        pltpu.VMEM((M, d), F32),
        pltpu.VMEM((n, 2 * lm, d), BF),
        pltpu.VMEM((n, 2 * lm, d), BF),
        pltpu.VMEM((8, d), F32),
        pltpu.VMEM(small, F32),
        pltpu.VMEM((n,) + small, F32),
        pltpu.VMEM(small, F32),
        pltpu.VMEM((dp_n if fast else 1, pieces + heads, 128), F32),
        pltpu.VMEM((heads, 256), F32),
        pltpu.VMEM((tok + 128, QUAD), BF),
        pltpu.VMEM((tok + 128, QUAD), BF),
        pltpu.VMEM((QUAD // M, 128, 256), BF),
        pltpu.VMEM((QUAD // M, 128, 256), F32),
        sems((32,)),
        sems((2, 2)),
        sems((2, 2)),
        sems((3, tok // 256)),
        sems((5,)),
        sems((count,)),
        sems((count,)),
        *tail,
    ]
    return pl.pallas_call(
        functools.partial(back_kernel, n=n, dp_n=dp_n, fast=fast),
        in_specs=[vm] * len(near) + [ANY] * len(far),
        out_specs=out_specs,
        out_shape=out_shape,
        scratch_shapes=scratch,
        compiler_params=params(62, collective_id=3, has_side_effects=True),
        cost_estimate=pl.CostEstimate(
            flops=14 * tok * d * f2, bytes_accessed=60 * tok * d, transcendentals=0
        ),
        name="back",
    )(*near, *far)


def finish_kernel(
    idx, out_own, out_got, gin_own, gin_got, down, up, ov, qk,
    outs, gins, sq, sk, sv, so, su, sd,
):
    step = pl.program_id(0) * pl.num_programs(1) + pl.program_id(1)
    half = sq.shape[1]

    @pl.when(pl.program_id(0) == 0)
    def _():
        outs[0] = out_own[...]
        gins[0] = gin_own[...]

    @pl.when(pl.program_id(0) == 1)
    def _():
        outs[0] = out_got[...]
        gins[0] = gin_got[...]

    @pl.when(step == 0)
    def _():
        sq[...] = qk[:, :half]
        sk[...] = qk[:, half:]
        sv[...] = ov[:, half:]
        so[...] = ov[:, :half].T
        su[...] = up[...]
        sd[...] = down[...].T


def finish(idx, own, got, gin_own, gin_got, sums):
    tok, d = own.shape
    half = d // 2
    down, up, ov, qk = sums
    ch, f2 = up.shape
    steps = 2
    rows = tok // steps
    mine = lambda j, i, s: (jnp.where(j == 0, i, steps - 1), 0)
    theirs = lambda j, i, s: (jnp.where(j == 0, 0, i), 0)
    there = lambda j, i, s: (s[0] ^ j, i, 0)
    shapes = [(ch, half)] * 3 + [(half, ch), (ch, f2), (f2, ch)]
    return call(
        finish_kernel,
        idx,
        [own, got, gin_own, gin_got, down, up, ov, qk],
        [
            pl.BlockSpec((rows, d), mine),
            pl.BlockSpec((rows, d), theirs),
            pl.BlockSpec((rows, half), mine),
            pl.BlockSpec((rows, half), theirs),
        ]
        + [whole(a.shape) for a in sums],
        [pl.BlockSpec((1, rows, d), there), pl.BlockSpec((1, rows, half), there)]
        + [whole(a) for a in shapes],
        [sds((2, tok, d), BF), sds((2, tok, half), BF)] + [sds(a, F32) for a in shapes],
        (2, steps),
        "finish",
        moved=12 * tok * d,
    )


def shards(
    inputs,
    cotangent,
    padding,
    documents,
    w_query,
    w_key,
    w_value,
    w_out,
    w_up,
    w_down,
    conv_taps,
    gain_attn,
    shift_attn,
    gain_ffn,
    shift_ffn,
):
    row_count, tok, d = inputs.shape
    heads = conv_taps.shape[0]
    seq_n, dp_n = lax.axis_size("seq"), lax.axis_size("dp")
    mp = lax.axis_index("mp")
    chunk = d // (seq_n * dp_n)
    fast = seq_n == 4 and dp_n == 4 and chunk % 16 == 0
    shape = (dp_n if fast else 0, seq_n, chunk)
    own_w = (w_query, w_key, w_value)
    (
        q, k, v, xt, k1, e, save, *got_w, xt_got, wo_got, wu_got, wd_got,
        marks, vedge, cm, lv, gst, inv, k2, lines,
    ) = attend(
        seq_n, inputs, padding, own_w, conv_taps, (w_out, w_up, w_down), shape
    )
    wq, wk, wv = zip(own_w, got_w)
    wo, wu, wd = (w_out, wo_got), (w_up, wu_got), (w_down, wd_got)
    vecs = [gain_attn, shift_attn, gain_ffn, shift_ffn]
    (
        ctx0, act0, du0, hat, gh2, rstd, acc, out_own, nlt, gh2t, du1,
        out_got, nlt_got, gh2t_got, du_got, ctx_got, act_got,
    ) = core(inputs, cotangent, padding, documents, v, vedge, k1, cm, lines, wo, wu, wd, vecs, shape)
    near = [padding, documents, lines, marks, cm, lv, inv, gst, k2, vedge, acc, gain_attn, rstd]
    far = [
        k1, q, k, v, e, save, gh2t, gh2t_got, nlt, nlt_got, act0, act_got, du0, du_got, du1,
        hat, gh2, ctx0, ctx_got, xt, xt_got, *wq, *wk, *wv, *wu, *wo,
    ]
    gin0, gin_got, _, _, small, *sums = back(seq_n, dp_n, fast, near, far)
    if not fast:
        sums = [sum_any(joined(*sums[i : i + 4])) for i in range(0, 16, 4)]
    outputs, grad_inputs, sum_q, sum_k, sum_v, sum_o, sum_up, sum_down = finish(
        mp.astype(jnp.int32).reshape(1), out_own, out_got, gin0, gin_got, sums
    )
    n = 4 * (d // 128)
    rest = small[16:]
    if not fast:
        rest = lax.psum(rest, "dp")
    norms = rest[:n].reshape(4, d)
    width = conv_taps.shape[1]
    tap_total = jnp.concatenate([rest[n : n + heads], rest[n + heads :]], axis=1)
    tap_total = tap_total[:, 64 - width // 2 : 64 - width // 2 + width]
    row_rms = small[:16].reshape(2, 8, 128)[:, 4:7, 0]
    return (
        outputs,
        grad_inputs,
        sum_q,
        sum_k,
        sum_v,
        sum_o,
        sum_up,
        sum_down,
        tap_total,
        norms[0],
        norms[1],
        norms[2],
        norms[3],
        row_rms,
    )


def solution(mesh):
    return jax.shard_map(
        shards,
        mesh=mesh,
        in_specs=(
            P("dp", "seq", None),
            P("dp", "seq", None),
            P("dp", None),
            P("dp", None),
            P(None, "mp"),
            P(None, "mp"),
            P(None, "mp"),
            P("mp", None),
            P(None, "mp"),
            P("mp", None),
            P("mp", None),
            P(),
            P(),
            P(),
            P(),
        ),
        out_specs=(
            P("dp", "seq", None),
            P("dp", "seq", "mp"),
            P(("dp", "seq"), "mp"),
            P(("dp", "seq"), "mp"),
            P(("dp", "seq"), "mp"),
            P("mp", ("dp", "seq")),
            P(("dp", "seq"), "mp"),
            P("mp", ("dp", "seq")),
            P("mp", None),
            P(),
            P(),
            P(),
            P(),
            P("dp", None),
        ),
        check_vma=False,
    )
```

```python
import functools

import jax
import jax.numpy as jnp
from jax import lax
from jax.experimental import pallas as pl
from jax.experimental.pallas import tpu as pltpu
from jax.sharding import PartitionSpec as P

M = 64
ITERS = 6
LEN = 4096
QUAD = 256
MESH = pl.DeviceIdType.MESH
F32 = jnp.float32
BF = jnp.bfloat16
EPS = 1e-05


def nn(a, b):
    return lax.dot_general(a, b, (((1,), (0,)), ((), ())), preferred_element_type=F32)


def nt(a, b):
    return lax.dot_general(a, b, (((1,), (1,)), ((), ())), preferred_element_type=F32)


def tn(a, b):
    return lax.dot_general(a, b, (((0,), (0,)), ((), ())), preferred_element_type=F32)


def split(a):
    high = a.astype(BF)
    return high, (a - high.astype(F32)).astype(BF)


def three(dot, a, b):
    ah, al = split(a)
    bh, bl = split(b)
    return dot(ah, bh) + (dot(ah, bl) + dot(al, bh))


def iota(shape, dim):
    return lax.broadcasted_iota(jnp.int32, shape, dim)


def block_mask():
    return iota((QUAD, QUAD), 0) // M == iota((QUAD, QUAD), 1) // M


def spread_blocks(x, mask):
    return jnp.where(mask, jnp.concatenate([x] * (QUAD // M), axis=0), jnp.zeros((), x.dtype))


def gather_blocks(y):
    lane = iota((M, QUAD), 1) // M
    out = jnp.zeros((M, QUAD), y.dtype)
    for h in range(QUAD // M):
        out = out + jnp.where(lane == h, y[h * M : (h + 1) * M], 0.0)
    return out


def params(limit=56, **kw):
    return pltpu.CompilerParams(vmem_limit_bytes=limit * 1024 * 1024, **kw)


def whole(shape):
    nd = len(shape)
    return pl.BlockSpec(shape, lambda *a: (0,) * nd)


def sds(shape, dtype):
    return jax.ShapeDtypeStruct(shape, dtype)


ANY = pl.BlockSpec(memory_space=pl.ANY)


def call(kernel, idx, args, in_specs, out_specs, out_shape, grid, name, scratch=(), flops=0, moved=0, exps=0, deps=(), limit=56):
    nd = len(deps)

    def body(idx_ref, *refs):
        kernel(idx_ref, *refs[nd:])

    return pl.pallas_call(
        body,
        grid_spec=pltpu.PrefetchScalarGridSpec(
            num_scalar_prefetch=1,
            grid=grid,
            in_specs=[ANY] * nd + list(in_specs),
            out_specs=out_specs,
            scratch_shapes=list(scratch),
        ),
        out_shape=out_shape,
        compiler_params=params(limit),
        cost_estimate=pl.CostEstimate(flops=flops, bytes_accessed=moved, transcendentals=exps),
        name=name,
    )(idx, *deps, *args)


def store_chunks(out_ref, t, idx, shape):
    z, sq, chunk = shape
    if z == 0:
        out_ref[...] = t
        return
    for zr in range(z):
        for sr in range(sq):
            b = idx[1] ^ sr
            place = ((b & 1) * 2 + (b >> 1)) * z + (idx[2] ^ zr)
            src = (zr * sq + sr) * chunk
            out_ref[pl.ds(pl.multiple_of(place * chunk, chunk), chunk), :] = t[src : src + chunk]


def valid_count(pad_ref, idx_ref):
    row = pad_ref[pl.ds(idx_ref[0], 1), :].astype(F32)
    return jnp.sum(row, axis=1, keepdims=True).astype(jnp.int32)


def per_head(stat, base, c):
    lane = iota((M, QUAD), 1) // M
    out = jnp.zeros((M, QUAD), F32)
    for h in range(QUAD // M):
        at = base + c * (QUAD // M) + h
        out = jnp.where(lane == h, stat[:, at : at + 1], out)
    return out


def places():
    return [lax.axis_index(a) for a in ("mp", "seq", "dp")]


def greet(sizes):
    barrier = pltpu.get_barrier_semaphore()
    for axis, size in sizes.items():
        me = lax.axis_index(axis)
        for p in range(1, size):
            pl.semaphore_signal(
                barrier, inc=1, device_id={axis: lax.rem(me + p, size)}, device_id_type=MESH
            )
    return lambda: pl.semaphore_wait(barrier, sum(sizes.values()) - len(sizes))


def remote(src, dst, send, recv, axis, to):
    return pltpu.make_async_remote_copy(
        src_ref=src,
        dst_ref=dst,
        send_sem=send,
        recv_sem=recv,
        device_id={axis: to},
        device_id_type=MESH,
    )


def score_quad(c, q_ref, k_ref, v_ref, marks_ref, minus, k1_ref, e_ref, mix_ref, stat_ref):
    n, lm = marks_ref.shape[0], marks_ref.shape[1] // 2
    cols = slice(c * QUAD, (c + 1) * QUAD)
    tok = q_ref.shape[0]
    mask = block_mask()
    qm = jnp.concatenate([marks_ref[i, 0:lm, cols] for i in range(n)], axis=0)
    km = jnp.concatenate([marks_ref[i, lm : 2 * lm, cols] for i in range(n)], axis=0)
    s1 = nt(spread_blocks(km, mask), q_ref[:, cols]) * 0.125
    s1 = s1.reshape(QUAD // M, M, tok)
    e1 = jnp.exp(s1 - jnp.max(s1, axis=1, keepdims=True))
    k1 = e1 * (1.0 / jnp.sum(e1, axis=1, keepdims=True))
    k1_ref[cols, :] = k1.reshape(QUAD, tok).astype(BF)
    s3 = nt(spread_blocks(qm, mask), k_ref[:, cols]) * 0.125 - minus
    top = jnp.max(s3, axis=1, keepdims=True)
    e3 = jnp.exp(s3 - top)
    total = jnp.sum(e3, axis=1, keepdims=True)
    e3 = e3.astype(BF)
    e_ref[cols, :] = e3
    mix_ref[:, cols] = gather_blocks(nn(e3, v_ref[:, cols])).astype(BF)
    lane = iota((M, 128), 1)
    stat = stat_ref[...]
    for h in range(QUAD // M):
        at = c * (QUAD // M) + h
        stat = jnp.where(lane == at, top[h * M : (h + 1) * M], stat)
        stat = jnp.where(lane == 64 + at, total[h * M : (h + 1) * M], stat)
    stat_ref[...] = stat


def pseudo_inverse(qm, km, k2_ref, inv_ref, save_ref, z_ref, sel):
    d = qm.shape[1]
    quads = d // QUAD
    mask = block_mask()
    ident = (iota((QUAD, QUAD), 0) == iota((QUAD, QUAD), 1)).astype(F32)
    kernel, z = [], []
    for c in range(quads):
        cols = slice(c * QUAD, (c + 1) * QUAD)
        s2 = nt(spread_blocks(qm[:, cols], mask), spread_blocks(km[:, cols], mask)) * 0.125
        s2 = jnp.where(mask, s2, -1e30)
        e2 = jnp.exp(s2 - jnp.max(s2, axis=1, keepdims=True))
        e2 = e2 / jnp.sum(e2, axis=1, keepdims=True)
        kernel.append(e2)
        sums = jnp.sum(e2, axis=0, keepdims=True)
        lane = iota((1, QUAD), 1) // M
        scale = jnp.zeros((1, QUAD), F32)
        for h in range(QUAD // M):
            best = jnp.max(jnp.where(lane == h, sums, 0.0), axis=1, keepdims=True)
            scale = jnp.where(lane == h, 1.0 / best, scale)
        z.append(e2.T * scale)
        k2_ref[:, cols] = gather_blocks(e2)

    def keep(it, kind, vals):
        for c in range(quads):

            @pl.when(sel == c)
            def _():
                save_ref[it, kind] = gather_blocks(vals[c]).astype(BF)

    ksp = [split(a) for a in kernel]
    for c in range(quads):
        z_ref[c] = z[c]

    def mul(a, b):
        return nn(a[0], b[0]) + (nn(a[0], b[1]) + nn(a[1], b[0]))

    for it in range(ITERS):
        z = [z_ref[c] for c in range(quads)]
        zs = [split(a) for a in z]
        p = [mul(a, b) for a, b in zip(ksp, zs)]
        ps = [split(a) for a in p]
        i2 = [15.0 * ident - mul(a, split(7.0 * ident - b)) for a, b in zip(ps, p)]
        i3 = [13.0 * ident - mul(a, split(b)) for a, b in zip(ps, i2)]
        keep(it, 0, z)
        keep(it, 1, p)
        keep(it, 2, i2)
        keep(it, 3, i3)
        for c in range(quads):
            z_ref[c] = 0.25 * mul(zs[c], split(i3[c]))

    for c in range(quads):
        inv_ref[:, c * QUAD : (c + 1) * QUAD] = gather_blocks(z_ref[c])


def combine(mix_ref, stat_ref, inv_ref, me, cm_ref, lv_ref, gst_ref):
    n, _, d = mix_ref.shape
    lane = iota((M, 128), 1)
    top = stat_ref[0]
    for i in range(1, n):
        top = jnp.maximum(top, stat_ref[i])
    top = jnp.where(lane < 64, top, 0.0)
    total = jnp.zeros((M, 128), F32)
    scales = []
    for i in range(n):
        st = stat_ref[i]
        sc = jnp.where(lane < 64, jnp.exp(st - top), 0.0)
        scales.append(sc)
        total = total + sc * pltpu.roll(st, 64, 1)
    own = jnp.where(lane < 64, jnp.exp(stat_ref[me] - top), 0.0)
    gst_ref[...] = jnp.where(lane < 64, own, pltpu.roll(total, 64, 1))
    mask = block_mask()
    for c in range(d // QUAD):
        cols = slice(c * QUAD, (c + 1) * QUAD)
        mixed = jnp.zeros((M, QUAD), F32)
        for i in range(n):
            mixed = mixed + per_head(scales[i], 0, c) * mix_ref[i, :, cols].astype(F32)
        lv = mixed / per_head(total, 0, c)
        lv_ref[:, cols] = lv
        cm = three(nn, spread_blocks(inv_ref[:, cols], mask), spread_blocks(lv, mask))
        cm_ref[:, cols] = gather_blocks(cm).astype(BF)


def fill_lines(taps_ref, far_ref, line_ref, width):
    per = line_ref.shape[1] // 2
    turn = (iota((128, 128), 0) + iota((128, 128), 1) == width - 1).astype(BF)
    at = 64 - width // 2
    for first, ref in ((0, taps_ref), (per, far_ref)):
        taps = ref[...]
        back = nn(taps.astype(BF), turn)
        for i, x in ((0, taps), (1, back)):
            wide = jnp.concatenate([x, jnp.zeros(x.shape, F32)], axis=1)
            line_ref[i, first : first + per, :] = pltpu.roll(wide, at, 1)[:per]


def attend_kernel(
    inputs_any, pad_ref, wq0, wk0, wv0, taps_ref, wo_any, wu_any, wd_any,
    q_any, k_any, v_any, xt_any, k1_any, e_any, save_any, wq_any, wk_any, wv_any,
    xt_got, wo_got, wu_got, wd_got,
    marks, edge, cm_ref, lv_ref, gst_ref, inv_ref, k2_ref, line_ref,
    x, q, k, v, xt, k1, e, save, wq1, wk1, wv1, taps_own, taps_got,
    pack, mix, stat, mixes, stats, zs, ship, send, recv, *, n, shape,
):
    idx = places()
    me, mate = idx[1], 1 - idx[0]
    tok, d = x.shape
    half = d // 2
    lm = tok // M
    ready = greet({"seq": n, "mp": 2})
    load = pltpu.make_async_copy(inputs_any.at[idx[0]], x, ship.at[0])
    load.start()
    moved = []

    def out(src, dst):
        c = pltpu.make_async_copy(src, dst, ship.at[1 + len(moved)])
        c.start()
        moved.append(c)

    peers = [lax.rem(me + p, n) for p in range(1, n)]
    sent = []

    def tell(src, dst, to, axis="seq"):
        c = remote(src, dst, send.at[len(sent)], recv.at[len(sent)], axis, to)
        c.start()
        sent.append(c)
        return c

    per, width = taps_ref.shape
    taps_own[...] = jnp.zeros_like(taps_own)
    taps_own[0:per, 0:width] = taps_ref[...]
    valid = pad_ref[pl.ds(idx[0], 1), :].astype(F32)
    keep_n = jnp.sum(valid, axis=1, keepdims=True).astype(jnp.int32) - me * tok
    keep = (iota((tok, 1), 0) < keep_n).astype(F32)
    count = jnp.maximum(jnp.sum(keep.reshape(lm, M, 1), axis=1), 1.0)
    ready()
    swaps = [tell(a, b, mate, "mp") for a, b in ((wq0, wq1), (wk0, wk1), (wv0, wv1))]
    late = [
        tell(a, b, mate, "mp")
        for a, b in ((taps_own, taps_got), (wo_any, wo_got), (wu_any, wu_got), (wd_any, wd_got))
    ]
    load.wait()

    def project(w, i, at, dst):
        cols = slice(i * half, (i + 1) * half)
        val = nn(x[...], w[...])
        if at is None:
            dst[:, cols] = (val * keep).astype(BF)
            return
        val = val.astype(BF)
        dst[:, cols] = val
        wide = (val.astype(F32) * keep).reshape(lm, M, half)
        pack[at : at + lm, cols] = (jnp.sum(wide, axis=1) / count).astype(BF)

    project(wq0, 0, 0, q)
    project(wk0, 0, lm, k)
    swaps[0].wait()
    project(wq1, 1, 0, q)
    swaps[1].wait()
    project(wk1, 1, lm, k)
    first = [tell(pack, marks.at[me], to) for to in peers]
    marks[me] = pack[...]
    project(wv0, 0, None, v)
    swaps[2].wait()
    project(wv1, 1, None, v)
    edges = [
        tell(v.at[pl.ds(tok - 16, 16)], edge.at[pl.ds(0, 16)], peers[0]),
        tell(v.at[pl.ds(0, 16)], edge.at[pl.ds(16, 16)], peers[n - 2]),
    ]
    store_chunks(xt, x[...].T, idx, shape)
    late.append(tell(xt, xt_got, mate, "mp"))
    for src, dst in (
        (q, q_any), (k, k_any), (v, v_any), (xt, xt_any), (wq1, wq_any), (wk1, wk_any), (wv1, wv_any),
    ):
        out(src, dst)
    for c in first:
        c.wait()
    qm = jnp.concatenate([marks[i, 0:lm, :] for i in range(n)], axis=0)
    km = jnp.concatenate([marks[i, lm : 2 * lm, :] for i in range(n)], axis=0)
    minus = jnp.where(iota((1, tok), 1) < keep_n, 0.0, 1000000000.0)
    stat[...] = jnp.zeros_like(stat)

    for c in range(d // QUAD):
        score_quad(c, q, k, v, marks, minus, k1, e, mix, stat)

    second = [tell(a, b.at[me], to) for a, b in ((mix, mixes), (stat, stats)) for to in peers]
    mixes[me] = mix[...]
    stats[me] = stat[...]
    out(k1, k1_any)
    out(e, e_any)
    pseudo_inverse(qm, km, k2_ref, inv_ref, save, zs, jnp.minimum(me, d // QUAD - 1))
    out(save, save_any)
    for c in second:
        c.wait()
    combine(mixes, stats, inv_ref, me, cm_ref, lv_ref, gst_ref)
    late[0].wait()
    fill_lines(taps_own, taps_got, line_ref, width)
    for c in edges + moved + late[1:]:
        c.wait()


def attend(n, inputs, padding, weights, taps, others, shape):
    _, tok, d = inputs.shape
    lm = tok // M
    flat, turned = sds((tok, d), BF), sds((d, tok), BF)
    save = sds((ITERS, 4, M, QUAD), BF)
    thin = sds(weights[0].shape, BF)
    big = [flat, flat, flat, turned, turned, turned, save, thin, thin, thin]
    far = [turned] + [sds(w.shape, BF) for w in others]
    heads = 2 * taps.shape[0]
    small = [
        sds((n, 2 * lm, d), BF),
        sds((32, d), BF),
        sds((M, d), BF),
        sds((M, d), F32),
        sds((M, 128), F32),
        sds((M, d), F32),
        sds((M, d), F32),
        sds((2, heads, 256), F32),
    ]
    vm = pl.BlockSpec(memory_space=pltpu.VMEM)
    count = 3 * (n - 1) + 2 + 8
    return pl.pallas_call(
        functools.partial(attend_kernel, n=n, shape=shape),
        in_specs=[ANY] + [vm] * 5 + [ANY] * 3,
        out_specs=[ANY] * (len(big) + len(far)) + [vm] * len(small),
        out_shape=big + far + small,
        scratch_shapes=[pltpu.VMEM(a.shape, a.dtype) for a in [flat] + big]
        + [
            pltpu.VMEM((8, 128), F32),
            pltpu.VMEM((8, 128), F32),
            pltpu.VMEM((2 * lm, d), BF),
            pltpu.VMEM((M, d), BF),
            pltpu.VMEM((M, 128), F32),
            pltpu.VMEM((n, M, d), BF),
            pltpu.VMEM((n, M, 128), F32),
            pltpu.VMEM((d // QUAD, QUAD, QUAD), F32),
            pltpu.SemaphoreType.DMA((12,)),
            pltpu.SemaphoreType.DMA((count,)),
            pltpu.SemaphoreType.DMA((count,)),
        ],
        compiler_params=params(56, collective_id=1, has_side_effects=True),
        cost_estimate=pl.CostEstimate(
            flops=6 * tok * d * d + 72 * 3 * 2 * QUAD**3,
            bytes_accessed=30 * tok * d,
            transcendentals=2 * tok * d,
        ),
        name="attend",
    )(inputs, padding, *weights, taps, *others)


def doc_bounds(doc_ref, idx):
    row = doc_ref[pl.ds(idx[0], 1), :]
    return [
        jnp.sum((row < j).astype(F32), axis=1, keepdims=True).astype(jnp.int32)
        for j in range(1, 9)
    ]


def docs_at(place, bounds, length):
    doc = jnp.zeros(place.shape, jnp.int32)
    for b in bounds:
        doc = doc + (place >= b).astype(jnp.int32)
    return jnp.where((place >= 0) & (place < length), doc, -1)


def fill_bands(line_ref, band_ref):
    for h in range(band_ref.shape[0]):
        wide = jnp.broadcast_to(line_ref[h : h + 1, :], band_ref.shape[1:])
        band_ref[h] = pltpu.roll(wide, 0, 1, stride=1, stride_axis=0).astype(BF)


def banded(band_ref, window, same, col0):
    lane = iota((band_ref.shape[1], 128), 1)
    first = nn(band_ref[col0] * same, window)
    second = nn(band_ref[col0 + 1] * same, window)
    return jnp.where(lane < 64, first, second)


def fill_halo(ext, body, edge_ref, tok):
    ext[0:48, :] = jnp.zeros((48, ext.shape[1]), BF)
    ext[48:64, :] = edge_ref[0:16, :]
    ext[64 : 64 + tok, :] = body[...]
    ext[64 + tok : 80 + tok, :] = edge_ref[16:32, :]
    ext[80 + tok :, :] = jnp.zeros((48, ext.shape[1]), BF)


def erf_parts(u):
    a = jnp.abs(u) * 0.7071067811865476
    e = jnp.exp(-0.5 * u * u)
    t = 1.0 / (1.0 + 0.3275911 * a)
    poly = t * (
        0.254829592
        + t * (-0.284496736 + t * (1.421413741 + t * (-1.453152027 + t * 1.061405429)))
    )
    tail = 0.5 * poly * e
    cdf = jnp.where(u < 0.0, tail, 1.0 - tail)
    return cdf, e * 0.3989422804014327


def norm_stats(h):
    mean = jnp.mean(h, axis=-1, keepdims=True)
    centre = h - mean
    rstd = lax.rsqrt(jnp.mean(centre * centre, axis=-1, keepdims=True) + EPS)
    return centre * rstd, rstd


def norm_back(g, hat, rstd):
    return rstd * (
        g
        - jnp.mean(g, axis=-1, keepdims=True)
        - hat * jnp.mean(g * hat, axis=-1, keepdims=True)
    )


def core_kernel(
    x_any,
    cot_any,
    pad_ref,
    doc_ref,
    v_ref,
    edge_ref,
    k1_ref,
    cm_ref,
    line_ref,
    wo0_any,
    wo1_any,
    wu0_any,
    wu1_any,
    wd0_any,
    wd1_any,
    ga_ref,
    sa_ref,
    gf_ref,
    sf_ref,
    ctx0,
    act0,
    du0,
    hat_ref,
    gh2_ref,
    rstd_ref,
    acc_ref,
    out_own,
    nlt_own,
    gh2t_own,
    du_own,
    out_got,
    nlt_got,
    gh2t_got,
    du_got,
    ctx_got,
    act_got,
    ext,
    band,
    wo,
    wu,
    wd,
    gp,
    x_all,
    cot_all,
    out2,
    nlt2,
    gh2t2,
    du2,
    ctx2,
    act2,
    sems,
    send,
    recv,
    local,
    *,
    tok,
    shape,
):
    idx = places()
    step = pl.program_id(0)
    steps = pl.num_programs(0)
    rows, d = hat_ref.shape
    half = d // 2
    ga, sa, gf, sf = (ref[...].reshape(1, d) for ref in (ga_ref, sa_ref, gf_ref, sf_ref))
    loads = [
        pltpu.make_async_copy(src, dst, sems.at[n])
        for n, (src, dst) in enumerate(
            [
                (wo0_any, wo.at[0]),
                (wo1_any, wo.at[1]),
                (wu0_any, wu.at[0]),
                (wu1_any, wu.at[1]),
                (wd0_any, wd.at[0]),
                (wd1_any, wd.at[1]),
                (x_any.at[idx[0]], x_all),
                (cot_any.at[idx[0]], cot_all),
            ]
        )
    ]

    def arrived(*which):
        @pl.when(step == 0)
        def _():
            for i in which:
                loads[i].wait()

    own = pl.multiple_of(step * rows, rows)
    slot = lax.rem(step, 2)
    moved = [
        (out2, out_got, out_own, False),
        (nlt2, nlt_got, nlt_own, True),
        (gh2t2, gh2t_got, gh2t_own, True),
        (du2, du_got, du_own, False),
        (ctx2, ctx_got, None, False),
        (act2, act_got, None, False),
    ]

    def copies(n, t, both=True):
        src, far, near, turned = moved[n]
        part = pl.ds(pl.multiple_of(t * rows, rows), rows)
        src = src.at[lax.rem(t, 2)]
        at = lambda ref: ref.at[:, part] if turned else ref.at[part]
        out = [remote(src, at(far), send.at[n, t], recv.at[n, t], "mp", 1 - idx[0])]
        if both and near is not None:
            out.append(pltpu.make_async_copy(src, at(near), local.at[n, t]))
        return out

    def give(n):
        for c in copies(n, step):
            c.start()

    def given(t):
        for n in range(len(moved)):
            c = copies(n, t)
            c[0].wait_send()
            if len(c) > 1:
                c[1].wait()

    @pl.when(step == 0)
    def _():
        ready = greet({"mp": 2})
        for i in (0, 1, 6, 2, 3, 4, 5, 7):
            loads[i].start()
        fill_halo(ext, v_ref, edge_ref, tok)
        fill_bands(line_ref.at[0], band)
        acc_ref[...] = jnp.zeros_like(acc_ref)
        ready()

    @pl.when(step >= 2)
    def _():
        given(step - 2)

    out_ref, nlt_ref, gh2t_ref, du1, ctx1, act1 = (m[0].at[slot] for m in moved)

    bounds = doc_bounds(doc_ref, idx)
    mask = block_mask()
    start = idx[1] * tok + step * rows
    parts = []
    for sub in range(rows // 128):
        place = start + sub * 128
        same = (
            docs_at(place + iota((128, 1), 0), bounds, LEN)
            == docs_at(place - 64 + iota((1, 256), 1), bounds, LEN)
        ).astype(BF)
        base = pl.multiple_of(step * rows + sub * 128, 128)
        cols = []
        for pair in range(d // 128):
            window = ext[pl.ds(base, 256), pair * 128 : (pair + 1) * 128]
            cols.append(banded(band, window, same, 2 * pair))
        parts.append(jnp.concatenate(cols, axis=1))
    conv = jnp.concatenate(parts, axis=0)
    ctxs = []
    for c in range(d // QUAD):
        cols = slice(c * QUAD, (c + 1) * QUAD)
        att = tn(k1_ref[cols, :], spread_blocks(cm_ref[:, cols], mask))
        ctxs.append((att + conv[:, cols]).astype(BF))
    ctx = jnp.concatenate(ctxs, axis=1)
    ctx0[...] = ctx[:, :half]
    ctx1[...] = ctx[:, half:]
    give(4)
    arrived(0, 1, 6)
    branch = nn(ctx[:, :half], wo[0]) + nn(ctx[:, half:], wo[1])
    xf = x_all[pl.ds(own, rows), :].astype(F32)
    hat1, rstd1 = norm_stats(xf + branch)
    hat_ref[...] = hat1.astype(BF)
    rstd_ref[...] = jnp.broadcast_to(rstd1, rstd_ref.shape)
    normed = hat1 * ga + sa
    nl = normed.astype(BF)
    store_chunks(nlt_ref, nl.T, idx, shape)
    give(1)
    arrived(2, 3, 4, 5, 7)
    chunk = 512
    hidden = wu.shape[2]
    ffn = jnp.zeros((rows, d), F32)
    for i, act in ((0, act0), (1, act1)):
        for at in range(0, hidden, chunk):
            cols = slice(at, at + chunk)
            u = nn(nl, wu[i, :, cols])
            cdf, pdf = erf_parts(u)
            low = (u * cdf).astype(BF)
            act[:, cols] = low
            ffn = ffn + nn(low, wd[i, cols, :])
            gp[i, :, cols] = (cdf + u * pdf).astype(BF)
    give(5)
    hat2, rstd2 = norm_stats(normed + ffn)
    out_ref[...] = (hat2 * gf + sf).astype(BF)
    give(0)
    cot = cot_all[pl.ds(own, rows), :].astype(F32)
    gh2 = norm_back(cot * gf, hat2, rstd2)
    low = gh2.astype(BF)
    gh2_ref[...] = low
    store_chunks(gh2t_ref, low.T, idx, shape)
    give(2)
    for i, du in ((0, du0), (1, du1)):
        for at in range(0, hidden, chunk):
            cols = slice(at, at + chunk)
            du[:, cols] = (nt(low, wd[i, cols, :]) * gp[i, :, cols].astype(F32)).astype(BF)
    give(3)
    keep_n = valid_count(pad_ref, idx) - start
    keep = (iota((rows, 1), 0) < keep_n).astype(F32)
    acc_ref[2:3, :] += jnp.sum(cot * hat2, axis=0, keepdims=True)
    acc_ref[3:4, :] += jnp.sum(cot, axis=0, keepdims=True)
    acc_ref[4:5, :] += jnp.sum(xf * xf * keep, axis=0, keepdims=True)
    acc_ref[5:6, :] += jnp.sum(branch * branch * keep, axis=0, keepdims=True)
    acc_ref[6:7, :] += jnp.sum(ffn * ffn * keep, axis=0, keepdims=True)

    @pl.when(step == steps - 1)
    def _():
        given(steps - 2)
        given(steps - 1)
        for n in range(len(moved)):
            for t in range(tok // rows):
                copies(n, t, False)[0].wait_recv()


def core(inputs, cot, padding, documents, v, edge, k1, cm, lines, wo, wu, wd, vecs, shape):
    tok, d = v.shape
    rows = 256
    steps = tok // rows
    f2 = wu[0].shape[1]
    heads = lines.shape[1]
    blk = lambda i: (i, 0)
    flat = pl.BlockSpec((rows, d), blk)
    part = pl.BlockSpec((rows, d // 2), blk)
    turned = pl.BlockSpec((d, rows), lambda i: (0, i))
    wide = pl.BlockSpec((rows, f2), blk)
    full, t = sds((tok, d), BF), sds((d, tok), BF)
    thin, broad = sds((tok, d // 2), BF), sds((tok, f2), BF)
    return pl.pallas_call(
        functools.partial(core_kernel, tok=tok, shape=shape),
        grid=(steps,),
        in_specs=[ANY] * 2
        + [whole(a.shape) for a in (padding, documents, v, edge)]
        + [turned]
        + [whole(a.shape) for a in (cm, lines)]
        + [ANY] * 6
        + [whole((d,))] * 4,
        out_specs=[part, wide, wide, flat, flat, pl.BlockSpec((rows, 128), blk), whole((8, d))]
        + [ANY] * 10,
        out_shape=[thin, broad, broad, full, full, sds((tok, 128), F32), sds((8, d), F32)]
        + [full, t, t, broad] * 2
        + [thin, broad],
        scratch_shapes=[
            pltpu.VMEM((tok + 128, d), BF),
            pltpu.VMEM((heads, 128, 256), BF),
            pltpu.VMEM((2, d // 2, d), BF),
            pltpu.VMEM((2, d, f2), BF),
            pltpu.VMEM((2, f2, d), BF),
            pltpu.VMEM((2, rows, f2), BF),
            pltpu.VMEM((tok, d), BF),
            pltpu.VMEM((tok, d), BF),
            pltpu.VMEM((2, rows, d), BF),
            pltpu.VMEM((2, d, rows), BF),
            pltpu.VMEM((2, d, rows), BF),
            pltpu.VMEM((2, rows, f2), BF),
            pltpu.VMEM((2, rows, d // 2), BF),
            pltpu.VMEM((2, rows, f2), BF),
            pltpu.SemaphoreType.DMA((8,)),
            pltpu.SemaphoreType.DMA((6, steps)),
            pltpu.SemaphoreType.DMA((6, steps)),
            pltpu.SemaphoreType.DMA((4, steps)),
        ],
        compiler_params=params(60, collective_id=2, has_side_effects=True),
        cost_estimate=pl.CostEstimate(
            flops=16 * tok * d * f2, bytes_accessed=60 * tok * d, transcendentals=4 * tok * f2
        ),
        name="core",
    )(inputs, cot, padding, documents, v, edge, k1, cm, lines, *wo, *wu, *wd, *vecs)


class Sum:
    def __init__(self, idx, slots, got1=None, got2=None, parts=None, got3=None, send=None, recv=None):
        self.idx = idx
        self.slots, self.got1, self.fast = slots, got1, got1 is not None
        self.got2, self.parts, self.got3 = got2, parts, got3
        self.send, self.recv = send, recv
        self.live = []

    @staticmethod
    def shapes(d, n):
        q = d // 4
        ch = q // 4
        return [
            pltpu.VMEM((4, 2 * q, n), BF),
            pltpu.VMEM((2, 2 * q, n), BF),
            pltpu.VMEM((2, q, n), BF),
            pltpu.VMEM((4, ch, 2 * n), BF),
            pltpu.VMEM((3, ch, 2 * n), BF),
            pltpu.SemaphoreType.DMA((7,)),
            pltpu.SemaphoreType.DMA((7,)),
        ]

    def start(self, n, src, dst, axis, to):
        c = remote(src, dst, self.send.at[n], self.recv.at[n], axis, to)
        c.start()
        self.live.append(c)

    def arrived(self):
        for c in self.live:
            c.wait()
        self.live = []

    def store(self, part, cols, acc):
        q = acc.shape[0] // 4
        if part == 0:
            self.slots[1, :, cols] = acc[: 2 * q]
            self.slots[0, :, cols] = acc[2 * q :]
        else:
            self.slots[3, :q, cols] = acc[:q]
            self.slots[2, :q, cols] = acc[q : 2 * q]
            self.slots[3, q:, cols] = acc[2 * q : 3 * q]
            self.slots[2, q:, cols] = acc[3 * q :]

    def step0(self, part):
        if self.fast:
            bit = 1 + part
            self.start(part, self.slots.at[2 * part], self.got1.at[part], "seq", self.idx[1] ^ bit)

    def step1(self):
        if not self.fast:
            return
        self.arrived()
        q = self.got2.shape[1]
        for part in range(2):
            at = 2 * part + 1
            self.slots[at] = (self.slots[at].astype(F32) + self.got1[part].astype(F32)).astype(BF)
            bit = 2 - part
            src = self.slots.at[at, pl.ds(q, q)]
            self.start(2 + part, src, self.got2.at[part], "seq", self.idx[1] ^ bit)

    def step2(self):
        if not self.fast:
            return
        self.arrived()
        _, q, n = self.got2.shape
        ch = self.parts.shape[1]
        for part in range(2):
            mine = self.slots[2 * part + 1, :q].astype(F32) + self.got2[part].astype(F32)
            for at, p in enumerate((0, 2, 1, 3)):
                rows = slice(p * ch, (p + 1) * ch)
                self.parts[at, :, part * n : (part + 1) * n] = mine[rows].astype(BF)
        pair = pl.ds(2, 2)
        self.start(4, self.parts.at[pair], self.got3.at[pl.ds(0, 2)], "dp", self.idx[2] ^ 1)

    def step3(self):
        if not self.fast:
            return
        self.arrived()
        self.parts[1] = (self.parts[1].astype(F32) + self.got3[1].astype(F32)).astype(BF)
        self.start(5, self.parts.at[1], self.got3.at[2], "dp", self.idx[2] ^ 2)

    def finish(self):
        self.arrived()
        return (
            self.parts[0].astype(F32) + self.got3[0].astype(F32) + self.got3[2].astype(F32)
        )


def sum_any(full):
    part = lax.psum_scatter(full.astype(F32), "dp", scatter_dimension=0, tiled=True)
    return lax.psum_scatter(part, "seq", scatter_dimension=0, tiled=True)


def joined(send_a, keep_a, send_b, keep_b):
    q = keep_a.shape[0] // 2
    b = jnp.concatenate([keep_b[:q], send_b[:q], keep_b[q:], send_b[q:]], axis=0)
    return jnp.concatenate([jnp.concatenate([keep_a, send_a], axis=0), b], axis=1)


def first_quad(c, q_ref, k1_ref, gc_ref, cm_ref, marks_ref, gq_ref, mix_ref, km_ref):
    n, lm = marks_ref.shape[0], marks_ref.shape[1] // 2
    cols = slice(c * QUAD, (c + 1) * QUAD)
    tok = q_ref.shape[0]
    mask = block_mask()
    kmb = spread_blocks(
        jnp.concatenate([marks_ref[i, lm : 2 * lm, cols] for i in range(n)], axis=0), mask
    )
    gc = gc_ref[:, cols]
    k1 = k1_ref[cols, :]
    mix_ref[:, cols] = gather_blocks(nn(k1, gc)).astype(BF)
    g = nt(spread_blocks(cm_ref[:, cols], mask), gc).reshape(QUAD // M, M, tok)
    kf = k1.astype(F32).reshape(QUAD // M, M, tok)
    inner = jnp.sum(g * kf, axis=1, keepdims=True)
    g1 = (kf * (g - inner)).reshape(QUAD, tok).astype(BF)
    km_ref[:, cols] = gather_blocks(nn(g1, q_ref[:, cols])) * 0.125
    gq_ref[:, cols] = (tn(g1, kmb) * 0.125).astype(BF)


def middle(gmix_ref, lv_ref, inv_ref, gst_ref, gm_ref, gt_ref):
    n = gmix_ref.shape[0]
    d = lv_ref.shape[1]
    mask = block_mask()
    lane = iota((M, 128), 1)
    head = iota((M, QUAD), 1) // M
    stat = gst_ref[...]
    gt = jnp.zeros((M, 128), F32)
    for c in range(d // QUAD):
        cols = slice(c * QUAD, (c + 1) * QUAD)
        gmix = jnp.zeros((M, QUAD), F32)
        for i in range(n):
            gmix = gmix + gmix_ref[i, :, cols].astype(F32)
        glv = gather_blocks(
            three(tn, spread_blocks(inv_ref[:, cols], mask), spread_blocks(gmix, mask))
        )
        scale = per_head(stat, 0, c)
        total = per_head(stat, 64, c)
        gm_ref[:, cols] = ((glv / total).astype(BF).astype(F32) * scale).astype(BF)
        prod = glv * lv_ref[:, cols]
        for h in range(QUAD // M):
            at = c * (QUAD // M) + h
            s = jnp.sum(jnp.where(head == h, prod, 0.0), axis=1, keepdims=True)
            gt = jnp.where(lane == at, -s / stat[:, 64 + at : 65 + at] * stat[:, at : at + 1], gt)
    gt_ref[...] = gt


def pinv_back(gmix_ref, lv_ref, k2_ref, save_ref, dz_ref, dk_ref, qm, km, cols, use):
    n = gmix_ref.shape[0]
    mask = block_mask()
    ident = (iota((QUAD, QUAD), 0) == iota((QUAD, QUAD), 1)).astype(F32)
    gmix = jnp.zeros((M, QUAD), F32)
    for i in range(n):
        gmix = gmix + gmix_ref[i, :, cols].astype(F32)
    dz = three(nt, spread_blocks(gmix, mask), spread_blocks(lv_ref[:, cols], mask))
    kernel = spread_blocks(k2_ref[:, cols], mask)
    klow = kernel.astype(BF)
    dz_ref[...] = dz
    dk_ref[...] = jnp.zeros((QUAD, QUAD), F32)
    ibf = ident.astype(BF)

    for it in range(ITERS - 1, -1, -1):
        z, p, i2, i3 = (spread_blocks(save_ref[it, kind], mask) for kind in range(4))
        i1 = 7.0 * ibf - p
        dlow = dz_ref[...].astype(BF)
        d3 = (0.25 * tn(z, dlow)).astype(BF)
        dp = nt(d3, i2)
        d2 = (-tn(p, d3)).astype(BF)
        dp = dp + nt(d2, i1)
        d1 = -tn(p, d2)
        dp = (-dp - d1).astype(BF)
        dz_ref[...] = 0.25 * nt(dlow, i3) + tn(klow, dp)
        dk_ref[...] += nt(dp, z)

    dz, dk = dz_ref[...], dk_ref[...]
    sums = jnp.sum(kernel, axis=0, keepdims=True)
    lane = iota((1, QUAD), 1) // M
    dzt = jnp.where(mask, dz, 0.0).T
    dsum = jnp.sum(dzt * kernel, axis=0, keepdims=True)
    scale = jnp.zeros((1, QUAD), F32)
    extra = jnp.zeros((1, QUAD), F32)
    for h in range(QUAD // M):
        mine = lane == h
        best = jnp.max(jnp.where(mine, sums, 0.0), axis=1, keepdims=True)
        dscale = jnp.sum(jnp.where(mine, dsum, 0.0), axis=1, keepdims=True)
        is_best = (mine & (sums == best)).astype(F32)
        share = is_best / jnp.sum(is_best, axis=1, keepdims=True)
        scale = jnp.where(mine, 1.0 / best, scale)
        extra = jnp.where(mine, -dscale / (best * best) * share, extra)
    dk = dk + dzt * scale + extra
    inner = jnp.sum(jnp.where(mask, dk * kernel, 0.0), axis=1, keepdims=True)
    g2 = kernel * (dk - inner)
    g2h, g2l = split(g2)
    kb, qb = spread_blocks(km, mask), spread_blocks(qm, mask)
    use = use * 0.125
    return (
        gather_blocks(nn(g2h, kb) + nn(g2l, kb)) * use,
        gather_blocks(tn(g2h, qb) + tn(g2l, qb)) * use,
    )


def conv_quad(
    c, v_ref, vedge_ref, gc_ref, gedge_ref, bounds, start, keep_n, line_ref, gv_ref, gtap_ref,
    vext, gext, band, pairs,
):
    heads = QUAD // M
    tok = v_ref.shape[0]
    at = pl.multiple_of(c * QUAD, QUAD)
    cols = pl.ds(at, QUAD)
    fill_halo(vext, v_ref.at[:, cols], vedge_ref.at[:, cols], tok)
    fill_halo(gext, gc_ref.at[:, cols], gedge_ref.at[:, cols], tok)
    fill_bands(line_ref.at[c], band)
    low64 = iota((128, 128), 1) < M
    pairs[...] = jnp.zeros_like(pairs)
    for sub in range(tok // 128):
        place = start + sub * 128
        same = docs_at(place + iota((128, 1), 0), bounds, LEN) == docs_at(
            place - 64 + iota((1, 256), 1), bounds, LEN
        )
        low = same.astype(BF)
        keep = iota((128, 1), 0) < keep_n - sub * 128
        rows = slice(sub * 128, sub * 128 + 128)
        for pair in range(heads // 2):
            lanes = slice(pair * 128, pair * 128 + 128)
            back = banded(band, gext[sub * 128 : sub * 128 + 256, lanes], low, 2 * pair)
            wide = pl.ds(pl.multiple_of(at + pair * 128, 128), 128)
            mine = gv_ref[rows, wide].astype(F32) + back
            gv_ref[rows, wide] = jnp.where(keep, mine, 0.0).astype(BF)
            g = gc_ref[rows, wide]
            win = vext[sub * 128 : sub * 128 + 256, lanes]
            for h in range(2):
                own = jnp.where(low64 == (h == 0), g, jnp.zeros((), BF))
                pairs[2 * pair + h] += jnp.where(same, nt(own, win), 0.0)
    for h in range(heads):
        tall = pairs[h, 0:8]
        for r in range(8, 128, 8):
            tall = tall + pltpu.roll(pairs[h, r : r + 8], 256 - r, 1)
        line = tall[0:1]
        for r in range(1, 8):
            line = line + pltpu.roll(tall[r : r + 1], 256 - r, 1)
        gtap_ref[pl.ds(c * heads + h, 1), :] = line


def att_quad(c, k_ref, v_ref, e_ref, gm_ref, gt_ref, marks_ref, gv_ref, qm_ref):
    n, lm = marks_ref.shape[0], marks_ref.shape[1] // 2
    heads = QUAD // M
    cols = slice(c * QUAD, (c + 1) * QUAD)
    mask = block_mask()
    qm = spread_blocks(
        jnp.concatenate([marks_ref[i, 0:lm, cols] for i in range(n)], axis=0), mask
    )
    gm = spread_blocks(gm_ref[:, cols], mask)
    lane = iota((M, 128), 1)
    gts = []
    for h in range(heads):
        pick = jnp.where(lane == c * heads + h, gt_ref[...], 0.0)
        gts.append(jnp.sum(pick, axis=1, keepdims=True))
    gt = jnp.concatenate(gts, axis=0)
    e = e_ref[cols, :]
    g3 = (e.astype(F32) * (nt(gm, v_ref[:, cols]) + gt)).astype(BF)
    qm_ref[:, cols] = gather_blocks(nn(g3, k_ref[:, cols])) * 0.125
    k_ref[:, cols] = (tn(g3, qm) * 0.125).astype(BF)
    gv_ref[:, cols] = tn(e, gm).astype(BF)


def back_kernel(*refs, n, dp_n, fast):
    (
        pad_ref, doc_ref, line_ref, marks, cm_ref, lv_ref, inv_ref, gst_ref, k2_ref, vedge, acc_ref,
        vec_ref, rstd_ref,
        k1_any, q_any, k_any, v_any, e_any, save_any,
        gh2t_any, gh2t_got, nlt_any, nlt_got, act0, act_got, du0, du_got, du1,
        hat_any, gh2_any, ctx0, ctx_got, xt_any, xt_got,
        wq0, wq1, wk0, wk1, wv0, wv1, wu0, wu1, wo0, wo1, *rest,
    ) = refs
    gin_own, gin_got, gh1t_own, gh1t_got, small_out, *rest = rest
    outs, rest = (rest[:4], rest[4:]) if fast else (rest[:16], rest[16:])
    (
        k1, gc, q, k, v, e, save, lhs, rhs, wu, wo, dus, gh1, gh1t, gv, far, res,
        gedge, mix, mixes, gm, gt, gkm, gqm, both, got, acc, small, smalls, small_got, rests, gtap,
        vext, gext, band, pairs, dz_s, dk_s,
        loads, stream, rows_in, turns, ship, send, recv, *rest,
    ) = rest
    idx = places()
    me, mate = idx[1], 1 - idx[0]
    tok, d = q.shape
    half = d // 2
    lm = tok // M
    quads = d // QUAD
    sizes = {"seq": n, "mp": 2}
    if fast:
        sizes["dp"] = dp_n
    ready = greet(sizes)
    sums = []
    for g in range(4):
        sums.append(Sum(idx, *rest[7 * g : 7 * g + 7]) if fast else Sum(idx, rest[g]))
    down, up, ov, qk = sums

    names = {}

    def fetch(name, src, dst):
        names[name] = pltpu.make_async_copy(src, dst, loads.at[len(names)])
        names[name].start()

    def fetched(*which):
        for w in which:
            names[w].wait()

    width = rhs.shape[3]
    blocks = act0.shape[1] // width
    work = [(g, j) for g in range(2) for j in range(blocks)]

    def block(i):
        g, j = work[i]
        cols = pl.ds(j * width, width)
        srcs = (act0, act_got) if g == 0 else (du0, du_got)
        return [
            pltpu.make_async_copy(src.at[:, cols], rhs.at[i % 2, t], stream.at[i % 2, t])
            for t, src in enumerate(srcs)
        ]

    fetch("gh2t", gh2t_any, lhs.at[0])
    for c in block(0):
        c.start()
    fetch("gh2t_got", gh2t_got, lhs.at[1])
    sent = []

    def tell(src, dst, to, axis="seq"):
        c = remote(src, dst, send.at[len(sent)], recv.at[len(sent)], axis, to)
        c.start()
        sent.append(c)
        return c

    peers = [lax.rem(me + p, n) for p in range(1, n)]

    def products(g, left, right, meanwhile):
        for j in range(blocks):
            i = g * blocks + j
            if j + 1 < blocks:
                for c in block(i + 1):
                    c.start()
            if j < len(meanwhile):
                meanwhile[j]()
            for c in block(i):
                c.wait()
            acc_w = nn(left, rhs[i % 2, 0]) + nn(right, rhs[i % 2, 1])
            part, at = j // (blocks // 2), (j % (blocks // 2)) * width
            sums[g].store(part, slice(at, at + width), acc_w.astype(BF))
            if (j + 1) % (blocks // 2) == 0:
                if g == 0 and part == 0:
                    ready()
                sums[g].step0(part)

    def more(*items):
        def go():
            for item in items:
                fetch(*item)

        return go

    fetched("gh2t", "gh2t_got")
    products(
        0,
        lhs[0],
        lhs[1],
        [
            more(("wu0", wu0, wu.at[0])),
            more(("wu1", wu1, wu.at[1])),
            more(("hat", hat_any, k)),
            more(("gh2", gh2_any, v)),
            more(("wo0", wo0, wo.at[0]), ("wo1", wo1, wo.at[1])),
        ],
    )

    rows = dus.shape[2]
    steps = tok // rows

    def du_rows(i):
        at = pl.ds(i * rows, rows)
        return [
            pltpu.make_async_copy(src.at[at], dus.at[i % 2, t], rows_in.at[i % 2, t])
            for t, src in enumerate((du0, du1))
        ]

    def turn(i):
        at = pl.ds(i * rows, rows)
        src = gh1t.at[i % 2]
        return (
            pltpu.make_async_copy(src, gh1t_own.at[:, at], turns.at[0, i]),
            remote(src, gh1t_got.at[:, at], turns.at[1, i], turns.at[2, i], "mp", mate),
        )

    for c in du_rows(0):
        c.start()
    fetched("wu0", "wu1", "wo0", "wo1", "hat", "gh2")
    acc[...] = acc_ref[...]
    turned = [turn(i) for i in range(steps)]
    shape = (dp_n if fast else 0, n, d // (n * dp_n))
    extra = [
        (("k1", k1_any, k1), ("q", q_any, q)),
        (("nlt", nlt_any, lhs.at[2]),),
        (("nlt_got", nlt_got, lhs.at[3]),),
    ]
    for i in range(steps):
        if i + 1 < steps:
            for c in du_rows(i + 1):
                c.start()
        if i < len(extra):
            more(*extra[i])()
        if i == steps - 1:
            for c in block(blocks):
                c.start()
        for c in du_rows(i):
            c.wait()
        at = slice(i * rows, (i + 1) * rows)
        gn = v[at].astype(F32) + nt(dus[i % 2, 0], wu[0]) + nt(dus[i % 2, 1], wu[1])
        hat = k[at].astype(F32)
        acc[0:1, :] += jnp.sum(gn * hat, axis=0, keepdims=True)
        acc[1:2, :] += jnp.sum(gn, axis=0, keepdims=True)
        low = norm_back(gn * vec_ref[...].reshape(1, d), hat, rstd_ref[at, 0:1]).astype(BF)
        gh1[at] = low
        if i >= 2:
            turned[i - 2][0].wait()
            turned[i - 2][1].wait_send()
        store_chunks(gh1t.at[i % 2], low.T, idx, shape)
        turned[i][0].start()
        turned[i][1].start()
        gc[at, :half] = nt(low, wo[0]).astype(BF)
        gc[at, half:] = nt(low, wo[1]).astype(BF)
    fetch("v", v_any, v)
    fetch("k", k_any, k)
    down.step1()

    swaps_edge = [
        tell(gc.at[pl.ds(tok - 16, 16)], gedge.at[pl.ds(0, 16)], peers[0]),
        tell(gc.at[pl.ds(0, 16)], gedge.at[pl.ds(16, 16)], peers[n - 2]),
    ]
    fetched("k1", "q")
    for c in range(quads):
        first_quad(c, q, k1, gc, cm_ref, marks, q, mix, gkm)
    swaps = [tell(mix, mixes.at[me], to) for to in peers]
    mixes[me] = mix[...]
    for i in range(max(steps - 2, 0), steps):
        turned[i][0].wait()
        turned[i][1].wait_send()
    for i in range(steps):
        turned[i][1].wait_recv()

    fetched("nlt", "nlt_got")
    products(
        1,
        lhs[2],
        lhs[3],
        [
            more(("e", e_any, e)),
            more(("save", save_any, save), ("gh1t", gh1t_own, lhs.at[0])),
            more(("gh1t_got", gh1t_got, lhs.at[1])),
            more(*[("w%d" % i, w, wu.at[0, :, pl.ds(i * half, half)]) for i, w in enumerate((wq0, wq1))]),
            more(*[("w%d" % (2 + i), w, wu.at[0, :, pl.ds((2 + i) * half, half)]) for i, w in enumerate((wk0, wk1))]),
            more(*[("w%d" % (4 + i), w, wu.at[1, :, pl.ds(i * half, half)]) for i, w in enumerate((wv0, wv1))]),
        ],
    )
    for t, src in enumerate((ctx0, ctx_got)):
        fetch("ctx%d" % t, src.at[:, pl.ds(0, width)], rhs.at[0, t])
        fetch("ctx%d" % (2 + t), src.at[:, pl.ds(width, half - width)], rhs.at[1, t, :, pl.ds(0, half - width)])
    fetch("xt", xt_any, lhs.at[2])
    fetch("xt_got", xt_got, lhs.at[3])
    down.step2()

    for c in swaps:
        c.wait()
    middle(mixes, lv_ref, inv_ref, gst_ref, gm, gt)
    fetched("k", "v", "e", "save")
    for c in range(quads):
        att_quad(c, k, v, e, gm, gt, marks, gv, gqm)
    down.step3()
    sel = jnp.minimum(me, quads - 1)
    cols = pl.ds(pl.multiple_of(sel * QUAD, QUAD), QUAD)
    use = (me < quads).astype(F32)
    qm_sel = jnp.concatenate([marks[i, 0:lm, cols] for i in range(n)], axis=0)
    km_sel = jnp.concatenate([marks[i, lm : 2 * lm, cols] for i in range(n)], axis=0)
    two_q, two_k = pinv_back(mixes, lv_ref, k2_ref, save, dz_s, dk_s, qm_sel, km_sel, cols, use)
    gqm[:, cols] += two_q
    gkm[:, cols] += two_k
    for i in range(n):
        part = slice(i * lm, (i + 1) * lm)
        both[i, :lm] = gqm[part].astype(BF)
        both[i, lm:] = gkm[part].astype(BF)
    swaps = [tell(both.at[to], got.at[me], to) for to in peers]
    got[me] = both[me]
    up.step1()

    valid = pad_ref[pl.ds(idx[0], 1), :].astype(F32)
    keep_n = jnp.sum(valid, axis=1, keepdims=True).astype(jnp.int32) - me * tok
    bounds = doc_bounds(doc_ref, idx)
    for c in swaps_edge:
        c.wait()

    @pl.loop(0, quads)
    def _(c):
        conv_quad(
            c, v, vedge, gc, gedge, bounds, me * tok, keep_n, line_ref, gv, gtap,
            vext, gext, band, pairs,
        )

    swap_v = tell(gv.at[:, pl.ds(half, half)], far.at[0], mate, "mp")
    pieces = d // 128
    for r in range(4):
        for b in range(pieces):
            at = r * pieces + b
            small[at : at + 1, :] = acc[r : r + 1, b * 128 : (b + 1) * 128]
    lines = 4 * pieces
    heads = gtap.shape[0]
    small[lines : lines + 2 * heads, :] = jnp.concatenate([gtap[:, :128], gtap[:, 128:]], axis=0)
    squares = jnp.sum(acc[...], axis=1, keepdims=True)
    small[lines + 2 * heads :, :] = jnp.broadcast_to(squares, (8, 128))
    swaps_small = [tell(small, smalls.at[me], to) for to in peers]
    smalls[me] = small[...]
    fetched("gh1t", "gh1t_got", "ctx0", "ctx1", "ctx2", "ctx3")
    acc_w = nn(lhs[0], rhs[0, 0]) + nn(lhs[1], rhs[0, 1])
    ov.store(0, slice(0, width), acc_w.astype(BF))
    acc_w = nn(lhs[0], rhs[1, 0, :, : half - width]) + nn(lhs[1], rhs[1, 1, :, : half - width])
    ov.store(0, slice(width, half), acc_w.astype(BF))
    ov.step0(0)

    for c in swaps:
        c.wait()
    spread(q, k, got, keep_n)
    swaps = [
        tell(q.at[:, pl.ds(half, half)], far.at[1], mate, "mp"),
        tell(k.at[:, pl.ds(half, half)], far.at[2], mate, "mp"),
    ]
    up.step2()
    fetched("xt", "xt_got")
    acc_w = nn(lhs[2], gv[:, :half])
    swap_v.wait()
    ov.store(1, slice(0, half), (acc_w + nn(lhs[3], far[0])).astype(BF))
    ov.step0(1)
    for i, src in ((0, q), (1, k)):
        acc_w = nn(lhs[2], src[:, :half])
        swaps[i].wait()
        qk.store(i, slice(0, half), (acc_w + nn(lhs[3], far[1 + i])).astype(BF))
        qk.step0(i)
    up.step3()
    for c in swaps_small:
        c.wait()
    total = smalls[0]
    for i in range(1, n):
        total = total + smalls[i]
    small[...] = total
    swap_small = tell(small, small_got, mate, "mp")

    fetched(*["w%d" % i for i in range(6)])
    tall = res.shape[0]
    own = pl.multiple_of(idx[0] * half, half)
    other = pl.multiple_of(mate * half, half)
    swap_gin = []
    keep_gin = []

    def outs_early():
        if fast:
            outs[0][...] = down.finish()

    for i in range(tok // tall):
        at = slice(i * tall, (i + 1) * tall)
        lhs_i = jnp.concatenate([q[at, :], k[at, :]], axis=1)
        res[...] = gh1[at].astype(F32) + nt(lhs_i, wu[0]) + nt(gv[at, :], wu[1, :, :d])
        mine = dus.at[i // 2, i % 2]
        mine[:, :half] = res[:, pl.ds(own, half)].astype(BF)
        mine[:, half:d] = res[:, pl.ds(other, half)].astype(BF)
        part = pl.ds(i * tall, tall)
        swap_gin.append(tell(mine.at[:, pl.ds(half, half)], gin_got.at[part], mate, "mp"))
        c = pltpu.make_async_copy(mine.at[:, pl.ds(0, half)], gin_own.at[part], ship.at[i])
        c.start()
        keep_gin.append(c)
        if i == 1:
            ov.step1()
            outs_early()
    swap_small.wait()
    mine = small[...]
    theirs = small_got[...]
    per = heads // 2
    taps_a = mine[lines : lines + 2 * heads]
    taps_b = theirs[lines : lines + 2 * heads]
    rests[0, :lines] = mine[:lines] + theirs[:lines]
    rests[0, lines : lines + per] = taps_a[:per] + taps_b[per:heads]
    rests[0, lines + per : lines + heads] = taps_a[heads : heads + per] + taps_b[heads + per :]
    for row, part in ((idx[0], mine), (mate, theirs)):
        real = jnp.sum(pad_ref[pl.ds(row, 1), :].astype(F32), axis=1, keepdims=True)
        at = pl.multiple_of(8 * row, 8)
        small_out[pl.ds(at, 8), :] = jnp.sqrt(part[lines + 2 * heads :] / (real * d) + 1e-06)
    if fast:
        norms = [tell(rests.at[0], rests.at[p], idx[2] ^ p, "dp") for p in range(1, dp_n)]
        qk.step1()
        ov.step2()
        outs[1][...] = up.finish()
        qk.step2()
        ov.step3()
        qk.step3()
        for c in norms:
            c.wait()
        total = rests[0]
        for p in range(1, dp_n):
            total = total + rests[p]
        small_out[16:] = total
        outs[2][...] = ov.finish()
        outs[3][...] = qk.finish()
    else:
        small_out[16:] = rests[0]
        for g in range(4):
            for i in range(4):
                c = pltpu.make_async_copy(rest[g].at[i], outs[4 * g + i], ship.at[4])
                c.start()
                c.wait()
    for c in swap_gin + keep_gin:
        c.wait()


def spread(gq_ref, gk_ref, got_ref, keep_n):
    n, lm = got_ref.shape[0], got_ref.shape[1] // 2
    got = got_ref[0].astype(F32)
    for i in range(1, n):
        got = got + got_ref[i].astype(F32)
    for j in range(lm):
        rows = slice(j * M, (j + 1) * M)
        keep = (iota((M, 1), 0) < keep_n - j * M).astype(F32)
        share = keep / jnp.maximum(jnp.sum(keep, axis=0, keepdims=True), 1.0)
        for at, ref in ((0, gq_ref), (lm, gk_ref)):
            ref[rows] = (ref[rows].astype(F32) + got[at + j : at + j + 1] * share).astype(BF)


def back(n, dp_n, fast, near, far):
    lines, marks = near[2], near[3]
    tok, d = far[1].shape
    f2 = far[10].shape[1]
    half = d // 2
    lm = tok // M
    heads = lines.shape[1]
    near = list(near)
    near[2] = lines[1].reshape(d // QUAD, QUAD // M, lines.shape[2])
    flat, turned, thin = (tok, d), (d, tok), (tok, half)
    pieces = 4 * (d // 128)
    small = (pieces + 2 * heads + 8, 128)
    vm = pl.BlockSpec(memory_space=pltpu.VMEM)
    sems = pltpu.SemaphoreType.DMA
    out_shape = [sds(thin, BF)] * 2 + [sds(turned, BF)] * 2 + [sds((pieces + heads + 16, 128), F32)]
    out_specs = [ANY] * 4 + [vm]
    widths = (f2, f2, d, d)
    tail = []
    for w in widths:
        if fast:
            out_shape.append(sds((d // (n * dp_n), w), F32))
            out_specs.append(vm)
            tail += Sum.shapes(d, w // 2)
        else:
            out_shape += [sds((half, w // 2), BF)] * 4
            out_specs += [ANY] * 4
            tail.append(pltpu.VMEM((4, half, w // 2), BF))
    count = 40
    scratch = [
        pltpu.VMEM(turned, BF),
        *[pltpu.VMEM(flat, BF)] * 4,
        pltpu.VMEM(turned, BF),
        pltpu.VMEM((ITERS, 4, M, QUAD), BF),
        pltpu.VMEM((4,) + turned, BF),
        pltpu.VMEM((2, 2, tok, QUAD), BF),
        pltpu.VMEM((2, d, f2), BF),
        pltpu.VMEM((2, half, d), BF),
        pltpu.VMEM((2, 2, 256, f2), BF),
        pltpu.VMEM(flat, BF),
        pltpu.VMEM((2, d, 256), BF),
        pltpu.VMEM(flat, BF),
        pltpu.VMEM((3,) + thin, BF),
        pltpu.VMEM((256, d), F32),
        pltpu.VMEM((32, d), BF),
        pltpu.VMEM((M, d), BF),
        pltpu.VMEM((n, M, d), BF),
        pltpu.VMEM((M, d), BF),
        pltpu.VMEM((M, 128), F32),
        pltpu.VMEM((M, d), F32),
        pltpu.VMEM((M, d), F32),
        pltpu.VMEM((n, 2 * lm, d), BF),
        pltpu.VMEM((n, 2 * lm, d), BF),
        pltpu.VMEM((8, d), F32),
        pltpu.VMEM(small, F32),
        pltpu.VMEM((n,) + small, F32),
        pltpu.VMEM(small, F32),
        pltpu.VMEM((dp_n if fast else 1, pieces + heads, 128), F32),
        pltpu.VMEM((heads, 256), F32),
        pltpu.VMEM((tok + 128, QUAD), BF),
        pltpu.VMEM((tok + 128, QUAD), BF),
        pltpu.VMEM((QUAD // M, 128, 256), BF),
        pltpu.VMEM((QUAD // M, 128, 256), F32),
        pltpu.VMEM((QUAD, QUAD), F32),
        pltpu.VMEM((QUAD, QUAD), F32),
        sems((32,)),
        sems((2, 2)),
        sems((2, 2)),
        sems((3, tok // 256)),
        sems((5,)),
        sems((count,)),
        sems((count,)),
        *tail,
    ]
    return pl.pallas_call(
        functools.partial(back_kernel, n=n, dp_n=dp_n, fast=fast),
        in_specs=[vm] * len(near) + [ANY] * len(far),
        out_specs=out_specs,
        out_shape=out_shape,
        scratch_shapes=scratch,
        compiler_params=params(62, collective_id=3, has_side_effects=True),
        cost_estimate=pl.CostEstimate(
            flops=14 * tok * d * f2, bytes_accessed=60 * tok * d, transcendentals=0
        ),
        name="back",
    )(*near, *far)


def finish_kernel(
    idx, out_own, out_got, gin_own, gin_got, down, up, ov, qk,
    outs, gins, sq, sk, sv, so, su, sd,
):
    step = pl.program_id(0) * pl.num_programs(1) + pl.program_id(1)
    half = sq.shape[1]

    @pl.when(pl.program_id(0) == 0)
    def _():
        outs[0] = out_own[...]
        gins[0] = gin_own[...]

    @pl.when(pl.program_id(0) == 1)
    def _():
        outs[0] = out_got[...]
        gins[0] = gin_got[...]

    @pl.when(step == 0)
    def _():
        sq[...] = qk[:, :half]
        sk[...] = qk[:, half:]
        sv[...] = ov[:, half:]
        so[...] = ov[:, :half]
        su[...] = up[...]
        sd[...] = down[...]


def finish(idx, own, got, gin_own, gin_got, sums):
    tok, d = own.shape
    half = d // 2
    down, up, ov, qk = sums
    ch, f2 = up.shape
    steps = 2
    rows = tok // steps
    mine = lambda j, i, s: (jnp.where(j == 0, i, steps - 1), 0)
    theirs = lambda j, i, s: (jnp.where(j == 0, 0, i), 0)
    there = lambda j, i, s: (s[0] ^ j, i, 0)
    shapes = [(ch, half)] * 4 + [(ch, f2)] * 2
    return call(
        finish_kernel,
        idx,
        [own, got, gin_own, gin_got, down, up, ov, qk],
        [
            pl.BlockSpec((rows, d), mine),
            pl.BlockSpec((rows, d), theirs),
            pl.BlockSpec((rows, half), mine),
            pl.BlockSpec((rows, half), theirs),
        ]
        + [whole(a.shape) for a in sums],
        [pl.BlockSpec((1, rows, d), there), pl.BlockSpec((1, rows, half), there)]
        + [whole(a) for a in shapes],
        [sds((2, tok, d), BF), sds((2, tok, half), BF)] + [sds(a, F32) for a in shapes],
        (2, steps),
        "finish",
        moved=12 * tok * d,
    )


def shards(
    inputs,
    cotangent,
    padding,
    documents,
    w_query,
    w_key,
    w_value,
    w_out,
    w_up,
    w_down,
    conv_taps,
    gain_attn,
    shift_attn,
    gain_ffn,
    shift_ffn,
):
    row_count, tok, d = inputs.shape
    heads = conv_taps.shape[0]
    seq_n, dp_n = lax.axis_size("seq"), lax.axis_size("dp")
    mp = lax.axis_index("mp")
    chunk = d // (seq_n * dp_n)
    fast = seq_n == 4 and dp_n == 4 and chunk % 16 == 0
    shape = (dp_n if fast else 0, seq_n, chunk)
    own_w = (w_query, w_key, w_value)
    (
        q, k, v, xt, k1, e, save, *got_w, xt_got, wo_got, wu_got, wd_got,
        marks, vedge, cm, lv, gst, inv, k2, lines,
    ) = attend(
        seq_n, inputs, padding, own_w, conv_taps, (w_out, w_up, w_down), shape
    )
    wq, wk, wv = zip(own_w, got_w)
    wo, wu, wd = (w_out, wo_got), (w_up, wu_got), (w_down, wd_got)
    vecs = [gain_attn, shift_attn, gain_ffn, shift_ffn]
    (
        ctx0, act0, du0, hat, gh2, rstd, acc, out_own, nlt, gh2t, du1,
        out_got, nlt_got, gh2t_got, du_got, ctx_got, act_got,
    ) = core(inputs, cotangent, padding, documents, v, vedge, k1, cm, lines, wo, wu, wd, vecs, shape)
    near = [padding, documents, lines, marks, cm, lv, inv, gst, k2, vedge, acc, gain_attn, rstd]
    far = [
        k1, q, k, v, e, save, gh2t, gh2t_got, nlt, nlt_got, act0, act_got, du0, du_got, du1,
        hat, gh2, ctx0, ctx_got, xt, xt_got, *wq, *wk, *wv, *wu, *wo,
    ]
    gin0, gin_got, _, _, small, *sums = back(seq_n, dp_n, fast, near, far)
    if not fast:
        sums = [sum_any(joined(*sums[i : i + 4])) for i in range(0, 16, 4)]
    outputs, grad_inputs, sum_q, sum_k, sum_v, sum_o, sum_up, sum_down = finish(
        mp.astype(jnp.int32).reshape(1), out_own, out_got, gin0, gin_got, sums
    )
    n = 4 * (d // 128)
    rest = small[16:]
    if not fast:
        rest = lax.psum(rest, "dp")
    norms = rest[:n].reshape(4, d)
    width = conv_taps.shape[1]
    tap_total = jnp.concatenate([rest[n : n + heads], rest[n + heads :]], axis=1)
    tap_total = tap_total[:, 64 - width // 2 : 64 - width // 2 + width]
    row_rms = small[:16].reshape(2, 8, 128)[:, 4:7, 0]
    return (
        outputs,
        grad_inputs,
        sum_q,
        sum_k,
        sum_v,
        sum_o.T,
        sum_up,
        sum_down.T,
        tap_total,
        norms[0],
        norms[1],
        norms[2],
        norms[3],
        row_rms,
    )


def solution(mesh):
    return jax.shard_map(
        shards,
        mesh=mesh,
        in_specs=(
            P("dp", "seq", None),
            P("dp", "seq", None),
            P("dp", None),
            P("dp", None),
            P(None, "mp"),
            P(None, "mp"),
            P(None, "mp"),
            P("mp", None),
            P(None, "mp"),
            P("mp", None),
            P("mp", None),
            P(),
            P(),
            P(),
            P(),
        ),
        out_specs=(
            P("dp", "seq", None),
            P("dp", "seq", "mp"),
            P(("dp", "seq"), "mp"),
            P(("dp", "seq"), "mp"),
            P(("dp", "seq"), "mp"),
            P("mp", ("dp", "seq")),
            P(("dp", "seq"), "mp"),
            P("mp", ("dp", "seq")),
            P("mp", None),
            P(),
            P(),
            P(),
            P(),
            P("dp", None),
        ),
        check_vma=False,
    )
```

```python
import functools

import jax
import jax.numpy as jnp
from jax import lax
from jax.experimental import pallas as pl
from jax.experimental.pallas import tpu as pltpu
from jax.sharding import PartitionSpec as P

M = 64
ITERS = 6
LEN = 4096
QUAD = 256
MESH = pl.DeviceIdType.MESH
F32 = jnp.float32
BF = jnp.bfloat16
EPS = 1e-05


def nn(a, b):
    return lax.dot_general(a, b, (((1,), (0,)), ((), ())), preferred_element_type=F32)


def nt(a, b):
    return lax.dot_general(a, b, (((1,), (1,)), ((), ())), preferred_element_type=F32)


def tn(a, b):
    return lax.dot_general(a, b, (((0,), (0,)), ((), ())), preferred_element_type=F32)


def split(a):
    high = a.astype(BF)
    return high, (a - high.astype(F32)).astype(BF)


def three(dot, a, b):
    ah, al = split(a)
    bh, bl = split(b)
    return dot(ah, bh) + (dot(ah, bl) + dot(al, bh))


def iota(shape, dim):
    return lax.broadcasted_iota(jnp.int32, shape, dim)


def block_mask():
    return iota((QUAD, QUAD), 0) // M == iota((QUAD, QUAD), 1) // M


def spread_blocks(x, mask):
    return jnp.where(mask, jnp.concatenate([x] * (QUAD // M), axis=0), jnp.zeros((), x.dtype))


def gather_blocks(y):
    lane = iota((M, QUAD), 1) // M
    out = jnp.zeros((M, QUAD), y.dtype)
    for h in range(QUAD // M):
        out = out + jnp.where(lane == h, y[h * M : (h + 1) * M], 0.0)
    return out


def params(limit=56, **kw):
    return pltpu.CompilerParams(vmem_limit_bytes=limit * 1024 * 1024, **kw)


def whole(shape):
    nd = len(shape)
    return pl.BlockSpec(shape, lambda *a: (0,) * nd)


def sds(shape, dtype):
    return jax.ShapeDtypeStruct(shape, dtype)


ANY = pl.BlockSpec(memory_space=pl.ANY)


def call(kernel, idx, args, in_specs, out_specs, out_shape, grid, name, scratch=(), flops=0, moved=0, exps=0, deps=(), limit=56):
    nd = len(deps)

    def body(idx_ref, *refs):
        kernel(idx_ref, *refs[nd:])

    return pl.pallas_call(
        body,
        grid_spec=pltpu.PrefetchScalarGridSpec(
            num_scalar_prefetch=1,
            grid=grid,
            in_specs=[ANY] * nd + list(in_specs),
            out_specs=out_specs,
            scratch_shapes=list(scratch),
        ),
        out_shape=out_shape,
        compiler_params=params(limit),
        cost_estimate=pl.CostEstimate(flops=flops, bytes_accessed=moved, transcendentals=exps),
        name=name,
    )(idx, *deps, *args)


def store_chunks(out_ref, t, idx, shape):
    z, sq, chunk = shape
    if z == 0:
        out_ref[...] = t
        return
    for zr in range(z):
        for sr in range(sq):
            b = idx[1] ^ sr
            place = ((b & 1) * 2 + (b >> 1)) * z + (idx[2] ^ zr)
            src = (zr * sq + sr) * chunk
            out_ref[pl.ds(pl.multiple_of(place * chunk, chunk), chunk), :] = t[src : src + chunk]


def valid_count(pad_ref, idx_ref):
    row = pad_ref[pl.ds(idx_ref[0], 1), :].astype(F32)
    return jnp.sum(row, axis=1, keepdims=True).astype(jnp.int32)


def per_head(stat, base, c):
    lane = iota((M, QUAD), 1) // M
    out = jnp.zeros((M, QUAD), F32)
    for h in range(QUAD // M):
        at = base + c * (QUAD // M) + h
        out = jnp.where(lane == h, stat[:, at : at + 1], out)
    return out


def places():
    return [lax.axis_index(a) for a in ("mp", "seq", "dp")]


def greet(sizes):
    barrier = pltpu.get_barrier_semaphore()
    for axis, size in sizes.items():
        me = lax.axis_index(axis)
        for p in range(1, size):
            pl.semaphore_signal(
                barrier, inc=1, device_id={axis: lax.rem(me + p, size)}, device_id_type=MESH
            )
    return lambda: pl.semaphore_wait(barrier, sum(sizes.values()) - len(sizes))


def remote(src, dst, send, recv, axis, to):
    return pltpu.make_async_remote_copy(
        src_ref=src,
        dst_ref=dst,
        send_sem=send,
        recv_sem=recv,
        device_id={axis: to},
        device_id_type=MESH,
    )


def score_quad(c, q_ref, k_ref, v_ref, marks_ref, minus, k1_ref, e_ref, mix_ref, stat_ref):
    n, lm = marks_ref.shape[0], marks_ref.shape[1] // 2
    cols = slice(c * QUAD, (c + 1) * QUAD)
    tok = q_ref.shape[0]
    mask = block_mask()
    qm = jnp.concatenate([marks_ref[i, 0:lm, cols] for i in range(n)], axis=0)
    km = jnp.concatenate([marks_ref[i, lm : 2 * lm, cols] for i in range(n)], axis=0)
    s1 = nt(spread_blocks(km, mask), q_ref[:, cols]) * 0.125
    s1 = s1.reshape(QUAD // M, M, tok)
    e1 = jnp.exp(s1 - jnp.max(s1, axis=1, keepdims=True))
    k1 = e1 * (1.0 / jnp.sum(e1, axis=1, keepdims=True))
    k1_ref[cols, :] = k1.reshape(QUAD, tok).astype(BF)
    s3 = nt(spread_blocks(qm, mask), k_ref[:, cols]) * 0.125 - minus
    top = jnp.max(s3, axis=1, keepdims=True)
    e3 = jnp.exp(s3 - top)
    total = jnp.sum(e3, axis=1, keepdims=True)
    e3 = e3.astype(BF)
    e_ref[cols, :] = e3
    mix_ref[:, cols] = gather_blocks(nn(e3, v_ref[:, cols])).astype(BF)
    lane = iota((M, 128), 1)
    stat = stat_ref[...]
    for h in range(QUAD // M):
        at = c * (QUAD // M) + h
        stat = jnp.where(lane == at, top[h * M : (h + 1) * M], stat)
        stat = jnp.where(lane == 64 + at, total[h * M : (h + 1) * M], stat)
    stat_ref[...] = stat


def pseudo_inverse(qm, km, k2_ref, inv_ref, save_ref, z_ref, sel):
    d = qm.shape[1]
    quads = d // QUAD
    mask = block_mask()
    ident = (iota((QUAD, QUAD), 0) == iota((QUAD, QUAD), 1)).astype(F32)
    kernel, z = [], []
    for c in range(quads):
        cols = slice(c * QUAD, (c + 1) * QUAD)
        s2 = nt(spread_blocks(qm[:, cols], mask), spread_blocks(km[:, cols], mask)) * 0.125
        s2 = jnp.where(mask, s2, -1e30)
        e2 = jnp.exp(s2 - jnp.max(s2, axis=1, keepdims=True))
        e2 = e2 / jnp.sum(e2, axis=1, keepdims=True)
        kernel.append(e2)
        sums = jnp.sum(e2, axis=0, keepdims=True)
        lane = iota((1, QUAD), 1) // M
        scale = jnp.zeros((1, QUAD), F32)
        for h in range(QUAD // M):
            best = jnp.max(jnp.where(lane == h, sums, 0.0), axis=1, keepdims=True)
            scale = jnp.where(lane == h, 1.0 / best, scale)
        z.append(e2.T * scale)
        k2_ref[:, cols] = gather_blocks(e2)

    def keep(it, kind, vals):
        for c in range(quads):

            @pl.when(sel == c)
            def _():
                save_ref[it, kind] = gather_blocks(vals[c]).astype(BF)

    ksp = [split(a) for a in kernel]
    for c in range(quads):
        z_ref[c] = z[c]

    def mul(a, b):
        return nn(a[0], b[0]) + (nn(a[0], b[1]) + nn(a[1], b[0]))

    for it in range(ITERS):
        z = [z_ref[c] for c in range(quads)]
        zs = [split(a) for a in z]
        p = [mul(a, b) for a, b in zip(ksp, zs)]
        ps = [split(a) for a in p]
        i2 = [15.0 * ident - mul(a, split(7.0 * ident - b)) for a, b in zip(ps, p)]
        i3 = [13.0 * ident - mul(a, split(b)) for a, b in zip(ps, i2)]
        keep(it, 0, z)
        keep(it, 1, p)
        keep(it, 2, i2)
        keep(it, 3, i3)
        for c in range(quads):
            z_ref[c] = 0.25 * mul(zs[c], split(i3[c]))

    for c in range(quads):
        inv_ref[:, c * QUAD : (c + 1) * QUAD] = gather_blocks(z_ref[c])


def combine(mix_ref, stat_ref, inv_ref, me, cm_ref, lv_ref, gst_ref):
    n, _, d = mix_ref.shape
    lane = iota((M, 128), 1)
    top = stat_ref[0]
    for i in range(1, n):
        top = jnp.maximum(top, stat_ref[i])
    top = jnp.where(lane < 64, top, 0.0)
    total = jnp.zeros((M, 128), F32)
    scales = []
    for i in range(n):
        st = stat_ref[i]
        sc = jnp.where(lane < 64, jnp.exp(st - top), 0.0)
        scales.append(sc)
        total = total + sc * pltpu.roll(st, 64, 1)
    own = jnp.where(lane < 64, jnp.exp(stat_ref[me] - top), 0.0)
    gst_ref[...] = jnp.where(lane < 64, own, pltpu.roll(total, 64, 1))
    mask = block_mask()
    for c in range(d // QUAD):
        cols = slice(c * QUAD, (c + 1) * QUAD)
        mixed = jnp.zeros((M, QUAD), F32)
        for i in range(n):
            mixed = mixed + per_head(scales[i], 0, c) * mix_ref[i, :, cols].astype(F32)
        lv = mixed / per_head(total, 0, c)
        lv_ref[:, cols] = lv
        cm = three(nn, spread_blocks(inv_ref[:, cols], mask), spread_blocks(lv, mask))
        cm_ref[:, cols] = gather_blocks(cm).astype(BF)


def fill_lines(taps_ref, far_ref, line_ref, width):
    per = line_ref.shape[1] // 2
    turn = (iota((128, 128), 0) + iota((128, 128), 1) == width - 1).astype(BF)
    at = 64 - width // 2
    for first, ref in ((0, taps_ref), (per, far_ref)):
        taps = ref[...]
        back = nn(taps.astype(BF), turn)
        for i, x in ((0, taps), (1, back)):
            wide = jnp.concatenate([x, jnp.zeros(x.shape, F32)], axis=1)
            line_ref[i, first : first + per, :] = pltpu.roll(wide, at, 1)[:per]


def attend_kernel(
    inputs_any, pad_ref, wq0, wk0, wv0, taps_ref, wo_any, wu_any, wd_any,
    q_any, k_any, v_any, xt_any, k1_any, e_any, save_any, wq_any, wk_any, wv_any,
    xt_got, wo_got, wu_got, wd_got,
    marks, edge, cm_ref, lv_ref, gst_ref, inv_ref, k2_ref, line_ref,
    x, q, k, v, xt, k1, e, save, wq1, wk1, wv1, taps_own, taps_got,
    pack, mix, stat, mixes, stats, zs, ship, send, recv, *, n, shape,
):
    idx = places()
    me, mate = idx[1], 1 - idx[0]
    tok, d = x.shape
    half = d // 2
    lm = tok // M
    ready = greet({"seq": n, "mp": 2})
    load = pltpu.make_async_copy(inputs_any.at[idx[0]], x, ship.at[0])
    load.start()
    moved = []

    def out(src, dst):
        c = pltpu.make_async_copy(src, dst, ship.at[1 + len(moved)])
        c.start()
        moved.append(c)

    peers = [lax.rem(me + p, n) for p in range(1, n)]
    sent = []

    def tell(src, dst, to, axis="seq"):
        c = remote(src, dst, send.at[len(sent)], recv.at[len(sent)], axis, to)
        c.start()
        sent.append(c)
        return c

    per, width = taps_ref.shape
    taps_own[...] = jnp.zeros_like(taps_own)
    taps_own[0:per, 0:width] = taps_ref[...]
    valid = pad_ref[pl.ds(idx[0], 1), :].astype(F32)
    keep_n = jnp.sum(valid, axis=1, keepdims=True).astype(jnp.int32) - me * tok
    keep = (iota((tok, 1), 0) < keep_n).astype(F32)
    count = jnp.maximum(jnp.sum(keep.reshape(lm, M, 1), axis=1), 1.0)
    ready()
    swaps = [tell(a, b, mate, "mp") for a, b in ((wq0, wq1), (wk0, wk1), (wv0, wv1))]
    late = [tell(taps_own, taps_got, mate, "mp")]
    load.wait()

    def project(w, i, at, dst):
        cols = slice(i * half, (i + 1) * half)
        val = nn(x[...], w[...])
        if at is None:
            dst[:, cols] = (val * keep).astype(BF)
            return
        val = val.astype(BF)
        dst[:, cols] = val
        wide = (val.astype(F32) * keep).reshape(lm, M, half)
        pack[at : at + lm, cols] = (jnp.sum(wide, axis=1) / count).astype(BF)

    project(wq0, 0, 0, q)
    project(wk0, 0, lm, k)
    swaps[0].wait()
    project(wq1, 1, 0, q)
    swaps[1].wait()
    project(wk1, 1, lm, k)
    first = [tell(pack, marks.at[me], to) for to in peers]
    marks[me] = pack[...]
    late += [
        tell(a, b, mate, "mp") for a, b in ((wo_any, wo_got), (wu_any, wu_got), (wd_any, wd_got))
    ]
    project(wv0, 0, None, v)
    swaps[2].wait()
    project(wv1, 1, None, v)
    edges = [
        tell(v.at[pl.ds(tok - 16, 16)], edge.at[pl.ds(0, 16)], peers[0]),
        tell(v.at[pl.ds(0, 16)], edge.at[pl.ds(16, 16)], peers[n - 2]),
    ]
    store_chunks(xt, x[...].T, idx, shape)
    late.append(tell(xt, xt_got, mate, "mp"))
    for src, dst in (
        (q, q_any), (k, k_any), (v, v_any), (xt, xt_any), (wq1, wq_any), (wk1, wk_any), (wv1, wv_any),
    ):
        out(src, dst)
    for c in first:
        c.wait()
    qm = jnp.concatenate([marks[i, 0:lm, :] for i in range(n)], axis=0)
    km = jnp.concatenate([marks[i, lm : 2 * lm, :] for i in range(n)], axis=0)
    minus = jnp.where(iota((1, tok), 1) < keep_n, 0.0, 1000000000.0)
    stat[...] = jnp.zeros_like(stat)

    for c in range(d // QUAD):
        score_quad(c, q, k, v, marks, minus, k1, e, mix, stat)

    second = [tell(a, b.at[me], to) for a, b in ((mix, mixes), (stat, stats)) for to in peers]
    mixes[me] = mix[...]
    stats[me] = stat[...]
    out(k1, k1_any)
    out(e, e_any)
    pseudo_inverse(qm, km, k2_ref, inv_ref, save, zs, jnp.minimum(me, d // QUAD - 1))
    out(save, save_any)
    for c in second:
        c.wait()
    combine(mixes, stats, inv_ref, me, cm_ref, lv_ref, gst_ref)
    late[0].wait()
    fill_lines(taps_own, taps_got, line_ref, width)
    for c in edges + moved + late[1:]:
        c.wait()


def attend(n, inputs, padding, weights, taps, others, shape):
    _, tok, d = inputs.shape
    lm = tok // M
    flat, turned = sds((tok, d), BF), sds((d, tok), BF)
    save = sds((ITERS, 4, M, QUAD), BF)
    thin = sds(weights[0].shape, BF)
    big = [flat, flat, flat, turned, turned, turned, save, thin, thin, thin]
    far = [turned] + [sds(w.shape, BF) for w in others]
    heads = 2 * taps.shape[0]
    small = [
        sds((n, 2 * lm, d), BF),
        sds((32, d), BF),
        sds((M, d), BF),
        sds((M, d), F32),
        sds((M, 128), F32),
        sds((M, d), F32),
        sds((M, d), F32),
        sds((2, heads, 256), F32),
    ]
    vm = pl.BlockSpec(memory_space=pltpu.VMEM)
    count = 3 * (n - 1) + 2 + 8
    return pl.pallas_call(
        functools.partial(attend_kernel, n=n, shape=shape),
        in_specs=[ANY] + [vm] * 5 + [ANY] * 3,
        out_specs=[ANY] * (len(big) + len(far)) + [vm] * len(small),
        out_shape=big + far + small,
        scratch_shapes=[pltpu.VMEM(a.shape, a.dtype) for a in [flat] + big]
        + [
            pltpu.VMEM((8, 128), F32),
            pltpu.VMEM((8, 128), F32),
            pltpu.VMEM((2 * lm, d), BF),
            pltpu.VMEM((M, d), BF),
            pltpu.VMEM((M, 128), F32),
            pltpu.VMEM((n, M, d), BF),
            pltpu.VMEM((n, M, 128), F32),
            pltpu.VMEM((d // QUAD, QUAD, QUAD), F32),
            pltpu.SemaphoreType.DMA((12,)),
            pltpu.SemaphoreType.DMA((count,)),
            pltpu.SemaphoreType.DMA((count,)),
        ],
        compiler_params=params(56, collective_id=1, has_side_effects=True),
        cost_estimate=pl.CostEstimate(
            flops=6 * tok * d * d + 72 * 3 * 2 * QUAD**3,
            bytes_accessed=30 * tok * d,
            transcendentals=2 * tok * d,
        ),
        name="attend",
    )(inputs, padding, *weights, taps, *others)


def doc_bounds(doc_ref, idx):
    row = doc_ref[pl.ds(idx[0], 1), :]
    return [
        jnp.sum((row < j).astype(F32), axis=1, keepdims=True).astype(jnp.int32)
        for j in range(1, 9)
    ]


def docs_at(place, bounds, length):
    doc = jnp.zeros(place.shape, jnp.int32)
    for b in bounds:
        doc = doc + (place >= b).astype(jnp.int32)
    return jnp.where((place >= 0) & (place < length), doc, -1)


def fill_bands(line_ref, band_ref):
    for h in range(band_ref.shape[0]):
        wide = jnp.broadcast_to(line_ref[h : h + 1, :], band_ref.shape[1:])
        band_ref[h] = pltpu.roll(wide, 0, 1, stride=1, stride_axis=0).astype(BF)


def banded(band_ref, window, same, col0):
    lane = iota((band_ref.shape[1], 128), 1)
    first = nn(band_ref[col0] * same, window)
    second = nn(band_ref[col0 + 1] * same, window)
    return jnp.where(lane < 64, first, second)


def fill_halo(ext, body, edge_ref, tok):
    ext[0:48, :] = jnp.zeros((48, ext.shape[1]), BF)
    ext[48:64, :] = edge_ref[0:16, :]
    ext[64 : 64 + tok, :] = body[...]
    ext[64 + tok : 80 + tok, :] = edge_ref[16:32, :]
    ext[80 + tok :, :] = jnp.zeros((48, ext.shape[1]), BF)


def erf_parts(u):
    e = jnp.exp(u * u * -0.5)
    t = 1.0 / (1.0 + 0.2316418882663604 * jnp.abs(u))
    poly = t * (
        0.127414796
        + t * (-0.142248368 + t * (0.7107068705 + t * (-0.7265760135 + t * 0.5307027145)))
    )
    tail = poly * e
    cdf = jnp.where(u < 0.0, tail, 1.0 - tail)
    return cdf, e * 0.3989422804014327


def norm_stats(h):
    mean = jnp.mean(h, axis=-1, keepdims=True)
    centre = h - mean
    rstd = lax.rsqrt(jnp.mean(centre * centre, axis=-1, keepdims=True) + EPS)
    return centre * rstd, rstd


def norm_back(g, hat, rstd):
    return rstd * (
        g
        - jnp.mean(g, axis=-1, keepdims=True)
        - hat * jnp.mean(g * hat, axis=-1, keepdims=True)
    )


def core_kernel(
    x_any,
    cot_any,
    pad_ref,
    doc_ref,
    v_ref,
    edge_ref,
    k1_ref,
    cm_ref,
    line_ref,
    wo0_any,
    wo1_any,
    wu0_any,
    wu1_any,
    wd0_any,
    wd1_any,
    ga_ref,
    sa_ref,
    gf_ref,
    sf_ref,
    ctx0,
    act0,
    du0,
    hat_ref,
    gh2_ref,
    rstd_ref,
    acc_ref,
    out_own,
    nlt_own,
    gh2t_own,
    du_own,
    out_got,
    nlt_got,
    gh2t_got,
    du_got,
    ctx_got,
    act_got,
    ext,
    band,
    wo,
    wu,
    wd,
    gp,
    x_all,
    cot_all,
    out2,
    nlt2,
    gh2t2,
    du2,
    ctx2,
    act2,
    sems,
    send,
    recv,
    local,
    *,
    tok,
    shape,
):
    idx = places()
    step = pl.program_id(0)
    steps = pl.num_programs(0)
    rows, d = hat_ref.shape
    half = d // 2
    ga, sa, gf, sf = (ref[...].reshape(1, d) for ref in (ga_ref, sa_ref, gf_ref, sf_ref))
    loads = [
        pltpu.make_async_copy(src, dst, sems.at[n])
        for n, (src, dst) in enumerate(
            [
                (wo0_any, wo.at[0]),
                (wo1_any, wo.at[1]),
                (wu0_any, wu.at[0]),
                (wu1_any, wu.at[1]),
                (wd0_any, wd.at[0]),
                (wd1_any, wd.at[1]),
                (x_any.at[idx[0]], x_all),
                (cot_any.at[idx[0]], cot_all),
            ]
        )
    ]

    def arrived(*which):
        @pl.when(step == 0)
        def _():
            for i in which:
                loads[i].wait()

    own = pl.multiple_of(step * rows, rows)
    slot = lax.rem(step, 2)
    moved = [
        (out2, out_got, out_own, False),
        (nlt2, nlt_got, nlt_own, True),
        (gh2t2, gh2t_got, gh2t_own, True),
        (du2, du_got, du_own, False),
        (ctx2, ctx_got, None, False),
        (act2, act_got, None, False),
    ]

    def copies(n, t, both=True):
        src, far, near, turned = moved[n]
        part = pl.ds(pl.multiple_of(t * rows, rows), rows)
        src = src.at[lax.rem(t, 2)]
        at = lambda ref: ref.at[:, part] if turned else ref.at[part]
        out = [remote(src, at(far), send.at[n, t], recv.at[n, t], "mp", 1 - idx[0])]
        if both and near is not None:
            out.append(pltpu.make_async_copy(src, at(near), local.at[n, t]))
        return out

    def give(n):
        for c in copies(n, step):
            c.start()

    def given(t):
        for n in range(len(moved)):
            c = copies(n, t)
            c[0].wait_send()
            if len(c) > 1:
                c[1].wait()

    @pl.when(step == 0)
    def _():
        ready = greet({"mp": 2})
        for i in (0, 1, 6, 2, 3, 4, 5, 7):
            loads[i].start()
        fill_halo(ext, v_ref, edge_ref, tok)
        fill_bands(line_ref.at[0], band)
        acc_ref[...] = jnp.zeros_like(acc_ref)
        ready()

    @pl.when(step >= 2)
    def _():
        given(step - 2)

    out_ref, nlt_ref, gh2t_ref, du1, ctx1, act1 = (m[0].at[slot] for m in moved)

    bounds = doc_bounds(doc_ref, idx)
    mask = block_mask()
    start = idx[1] * tok + step * rows
    parts = []
    for sub in range(rows // 128):
        place = start + sub * 128
        same = (
            docs_at(place + iota((128, 1), 0), bounds, LEN)
            == docs_at(place - 64 + iota((1, 256), 1), bounds, LEN)
        ).astype(BF)
        base = pl.multiple_of(step * rows + sub * 128, 128)
        cols = []
        for pair in range(d // 128):
            window = ext[pl.ds(base, 256), pair * 128 : (pair + 1) * 128]
            cols.append(banded(band, window, same, 2 * pair))
        parts.append(jnp.concatenate(cols, axis=1))
    conv = jnp.concatenate(parts, axis=0)
    ctxs = []
    for c in range(d // QUAD):
        cols = slice(c * QUAD, (c + 1) * QUAD)
        att = tn(k1_ref[cols, :], spread_blocks(cm_ref[:, cols], mask))
        ctxs.append((att + conv[:, cols]).astype(BF))
    ctx = jnp.concatenate(ctxs, axis=1)
    ctx0[...] = ctx[:, :half]
    ctx1[...] = ctx[:, half:]
    give(4)
    arrived(0, 1, 6)
    branch = nn(ctx[:, :half], wo[0]) + nn(ctx[:, half:], wo[1])
    xf = x_all[pl.ds(own, rows), :].astype(F32)
    hat1, rstd1 = norm_stats(xf + branch)
    hat_ref[...] = hat1.astype(BF)
    rstd_ref[...] = jnp.broadcast_to(rstd1, rstd_ref.shape)
    normed = hat1 * ga + sa
    nl = normed.astype(BF)
    store_chunks(nlt_ref, nl.T, idx, shape)
    give(1)
    arrived(2, 3, 4, 5, 7)
    chunk = 512
    hidden = wu.shape[2]
    ffn = jnp.zeros((rows, d), F32)
    for i, act in ((0, act0), (1, act1)):
        for at in range(0, hidden, chunk):
            cols = slice(at, at + chunk)
            u = nn(nl, wu[i, :, cols])
            cdf, pdf = erf_parts(u)
            low = (u * cdf).astype(BF)
            act[:, cols] = low
            ffn = ffn + nn(low, wd[i, cols, :])
            gp[i, :, cols] = (cdf + u * pdf).astype(BF)
    give(5)
    hat2, rstd2 = norm_stats(normed + ffn)
    out_ref[...] = (hat2 * gf + sf).astype(BF)
    give(0)
    cot = cot_all[pl.ds(own, rows), :].astype(F32)
    gh2 = norm_back(cot * gf, hat2, rstd2)
    low = gh2.astype(BF)
    gh2_ref[...] = low
    store_chunks(gh2t_ref, low.T, idx, shape)
    give(2)
    for i, du in ((0, du0), (1, du1)):
        for at in range(0, hidden, chunk):
            cols = slice(at, at + chunk)
            du[:, cols] = (nt(low, wd[i, cols, :]) * gp[i, :, cols].astype(F32)).astype(BF)
    give(3)
    keep_n = valid_count(pad_ref, idx) - start
    keep = (iota((rows, 1), 0) < keep_n).astype(F32)
    acc_ref[2:3, :] += jnp.sum(cot * hat2, axis=0, keepdims=True)
    acc_ref[3:4, :] += jnp.sum(cot, axis=0, keepdims=True)
    acc_ref[4:5, :] += jnp.sum(xf * xf * keep, axis=0, keepdims=True)
    acc_ref[5:6, :] += jnp.sum(branch * branch * keep, axis=0, keepdims=True)
    acc_ref[6:7, :] += jnp.sum(ffn * ffn * keep, axis=0, keepdims=True)

    @pl.when(step == steps - 1)
    def _():
        given(steps - 2)
        given(steps - 1)
        for n in range(len(moved)):
            for t in range(tok // rows):
                copies(n, t, False)[0].wait_recv()


def core(inputs, cot, padding, documents, v, edge, k1, cm, lines, wo, wu, wd, vecs, shape):
    tok, d = v.shape
    rows = 256
    steps = tok // rows
    f2 = wu[0].shape[1]
    heads = lines.shape[1]
    blk = lambda i: (i, 0)
    flat = pl.BlockSpec((rows, d), blk)
    part = pl.BlockSpec((rows, d // 2), blk)
    turned = pl.BlockSpec((d, rows), lambda i: (0, i))
    wide = pl.BlockSpec((rows, f2), blk)
    full, t = sds((tok, d), BF), sds((d, tok), BF)
    thin, broad = sds((tok, d // 2), BF), sds((tok, f2), BF)
    return pl.pallas_call(
        functools.partial(core_kernel, tok=tok, shape=shape),
        grid=(steps,),
        in_specs=[ANY] * 2
        + [whole(a.shape) for a in (padding, documents, v, edge)]
        + [turned]
        + [whole(a.shape) for a in (cm, lines)]
        + [ANY] * 6
        + [whole((d,))] * 4,
        out_specs=[part, wide, wide, flat, flat, pl.BlockSpec((rows, 128), blk), whole((8, d))]
        + [ANY] * 10,
        out_shape=[thin, broad, broad, full, full, sds((tok, 128), F32), sds((8, d), F32)]
        + [full, t, t, broad] * 2
        + [thin, broad],
        scratch_shapes=[
            pltpu.VMEM((tok + 128, d), BF),
            pltpu.VMEM((heads, 128, 256), BF),
            pltpu.VMEM((2, d // 2, d), BF),
            pltpu.VMEM((2, d, f2), BF),
            pltpu.VMEM((2, f2, d), BF),
            pltpu.VMEM((2, rows, f2), BF),
            pltpu.VMEM((tok, d), BF),
            pltpu.VMEM((tok, d), BF),
            pltpu.VMEM((2, rows, d), BF),
            pltpu.VMEM((2, d, rows), BF),
            pltpu.VMEM((2, d, rows), BF),
            pltpu.VMEM((2, rows, f2), BF),
            pltpu.VMEM((2, rows, d // 2), BF),
            pltpu.VMEM((2, rows, f2), BF),
            pltpu.SemaphoreType.DMA((8,)),
            pltpu.SemaphoreType.DMA((6, steps)),
            pltpu.SemaphoreType.DMA((6, steps)),
            pltpu.SemaphoreType.DMA((4, steps)),
        ],
        compiler_params=params(60, collective_id=2, has_side_effects=True),
        cost_estimate=pl.CostEstimate(
            flops=16 * tok * d * f2, bytes_accessed=60 * tok * d, transcendentals=4 * tok * f2
        ),
        name="core",
    )(inputs, cot, padding, documents, v, edge, k1, cm, lines, *wo, *wu, *wd, *vecs)


class Sum:
    def __init__(self, idx, turn, refs):
        self.idx, self.turn = idx, turn
        self.slots = refs[:2]
        self.fast = len(refs) > 2
        if self.fast:
            self.got1, self.got2 = refs[2:4], refs[4:6]
            self.parts, self.got3, self.send, self.recv = refs[6:]
        self.live = []

    @staticmethod
    def shapes(d, widths, fast):
        q = d // 4
        ch = q // 4
        out = [pltpu.VMEM((2, 2 * q, n), BF) for n in widths]
        if not fast:
            return out
        n = sum(widths)
        return out + [
            *[pltpu.VMEM((2 * q, w), BF) for w in widths],
            *[pltpu.VMEM((q, w), BF) for w in widths],
            pltpu.VMEM((4, ch, n), BF),
            pltpu.VMEM((3, ch, n), BF),
            pltpu.SemaphoreType.DMA((6,)),
            pltpu.SemaphoreType.DMA((6,)),
        ]

    def start(self, n, src, dst, axis, to):
        c = remote(src, dst, self.send.at[n], self.recv.at[n], axis, to)
        c.start()
        self.live.append(c)

    def arrived(self):
        for c in self.live:
            c.wait()
        self.live = []

    def store(self, part, cols, acc):
        q = acc.shape[0] // 4
        ref = self.slots[part]
        if part == self.turn:
            ref[1, :, cols] = acc[: 2 * q]
            ref[0, :, cols] = acc[2 * q :]
        else:
            ref[1, :q, cols] = acc[:q]
            ref[0, :q, cols] = acc[q : 2 * q]
            ref[1, q:, cols] = acc[2 * q : 3 * q]
            ref[0, q:, cols] = acc[3 * q :]

    def step0(self, part):
        if self.fast:
            bit = 1 if part == self.turn else 2
            self.start(part, self.slots[part].at[0], self.got1[part], "seq", self.idx[1] ^ bit)

    def store_all(self, acc):
        at = self.slots[0].shape[2]
        for part, cols in ((0, slice(0, at)), (1, slice(at, acc.shape[1]))):
            self.store(part, slice(0, cols.stop - cols.start), acc[:, cols])
            self.step0(part)

    def step1(self):
        if not self.fast:
            return
        self.arrived()
        for part in range(2):
            ref = self.slots[part]
            q = ref.shape[1] // 2
            ref[1] = (ref[1].astype(F32) + self.got1[part][...].astype(F32)).astype(BF)
            bit = 2 if part == self.turn else 1
            src = ref.at[1, pl.ds(q, q)]
            self.start(2 + part, src, self.got2[part], "seq", self.idx[1] ^ bit)

    def step2(self):
        if not self.fast:
            return
        self.arrived()
        ch = self.parts.shape[1]
        first = 0
        for part in range(2):
            q, n = self.got2[part].shape
            mine = self.slots[part][1, :q].astype(F32) + self.got2[part][...].astype(F32)
            for at, p in enumerate((0, 2, 1, 3)):
                rows = slice(p * ch, (p + 1) * ch)
                self.parts[at, :, first : first + n] = mine[rows].astype(BF)
            first += n
        pair = pl.ds(2, 2)
        self.start(4, self.parts.at[pair], self.got3.at[pl.ds(0, 2)], "dp", self.idx[2] ^ 1)

    def step3(self):
        if not self.fast:
            return
        self.arrived()
        self.parts[1] = (self.parts[1].astype(F32) + self.got3[1].astype(F32)).astype(BF)
        self.start(5, self.parts.at[1], self.got3.at[2], "dp", self.idx[2] ^ 2)

    def finish(self):
        self.arrived()
        return (
            self.parts[0].astype(F32) + self.got3[0].astype(F32) + self.got3[2].astype(F32)
        )


def sum_any(full):
    part = lax.psum_scatter(full.astype(F32), "dp", scatter_dimension=0, tiled=True)
    return lax.psum_scatter(part, "seq", scatter_dimension=0, tiled=True)


def joined(turn, send_a, keep_a, send_b, keep_b):
    out = []
    for part, (send, keep) in enumerate(((send_a, keep_a), (send_b, keep_b))):
        q = keep.shape[0] // 2
        if part == turn:
            rows = [keep, send]
        else:
            rows = [keep[:q], send[:q], keep[q:], send[q:]]
        out.append(jnp.concatenate(rows, axis=0))
    return jnp.concatenate(out, axis=1)


GROUPS = (0, 0, 0, 1, 0, 1)


def first_quad(c, q_ref, k1_ref, gc_ref, cm_ref, marks_ref, gq_ref, mix_ref, km_ref):
    n, lm = marks_ref.shape[0], marks_ref.shape[1] // 2
    cols = slice(c * QUAD, (c + 1) * QUAD)
    tok = q_ref.shape[0]
    mask = block_mask()
    kmb = spread_blocks(
        jnp.concatenate([marks_ref[i, lm : 2 * lm, cols] for i in range(n)], axis=0), mask
    )
    gc = gc_ref[:, cols]
    k1 = k1_ref[cols, :]
    mix_ref[:, cols] = gather_blocks(nn(k1, gc)).astype(BF)
    g = nt(spread_blocks(cm_ref[:, cols], mask), gc).reshape(QUAD // M, M, tok)
    kf = k1.astype(F32).reshape(QUAD // M, M, tok)
    inner = jnp.sum(g * kf, axis=1, keepdims=True)
    g1 = (kf * (g - inner)).reshape(QUAD, tok).astype(BF)
    km_ref[:, cols] = gather_blocks(nn(g1, q_ref[:, cols])) * 0.125
    gq_ref[:, cols] = (tn(g1, kmb) * 0.125).astype(BF)


def middle(gmix_ref, lv_ref, inv_ref, gst_ref, gm_ref, gt_ref):
    n = gmix_ref.shape[0]
    d = lv_ref.shape[1]
    mask = block_mask()
    lane = iota((M, 128), 1)
    head = iota((M, QUAD), 1) // M
    stat = gst_ref[...]
    gt = jnp.zeros((M, 128), F32)
    for c in range(d // QUAD):
        cols = slice(c * QUAD, (c + 1) * QUAD)
        gmix = jnp.zeros((M, QUAD), F32)
        for i in range(n):
            gmix = gmix + gmix_ref[i, :, cols].astype(F32)
        glv = gather_blocks(
            three(tn, spread_blocks(inv_ref[:, cols], mask), spread_blocks(gmix, mask))
        )
        scale = per_head(stat, 0, c)
        total = per_head(stat, 64, c)
        gm_ref[:, cols] = ((glv / total).astype(BF).astype(F32) * scale).astype(BF)
        prod = glv * lv_ref[:, cols]
        for h in range(QUAD // M):
            at = c * (QUAD // M) + h
            s = jnp.sum(jnp.where(head == h, prod, 0.0), axis=1, keepdims=True)
            gt = jnp.where(lane == at, -s / stat[:, 64 + at : 65 + at] * stat[:, at : at + 1], gt)
    gt_ref[...] = gt


def pinv_back(gmix_ref, lv_ref, k2_ref, save_ref, dz_ref, dk_ref, qm, km, cols, use):
    n = gmix_ref.shape[0]
    mask = block_mask()
    ident = (iota((QUAD, QUAD), 0) == iota((QUAD, QUAD), 1)).astype(F32)
    gmix = jnp.zeros((M, QUAD), F32)
    for i in range(n):
        gmix = gmix + gmix_ref[i, :, cols].astype(F32)
    dz = three(nt, spread_blocks(gmix, mask), spread_blocks(lv_ref[:, cols], mask))
    kernel = spread_blocks(k2_ref[:, cols], mask)
    klow = kernel.astype(BF)
    dz_ref[...] = dz
    dk_ref[...] = jnp.zeros((QUAD, QUAD), F32)
    ibf = ident.astype(BF)

    for it in range(ITERS - 1, -1, -1):
        z, p, i2, i3 = (spread_blocks(save_ref[it, kind], mask) for kind in range(4))
        i1 = 7.0 * ibf - p
        dlow = dz_ref[...].astype(BF)
        d3 = (0.25 * tn(z, dlow)).astype(BF)
        dp = nt(d3, i2)
        d2 = (-tn(p, d3)).astype(BF)
        dp = dp + nt(d2, i1)
        d1 = -tn(p, d2)
        dp = (-dp - d1).astype(BF)
        dz_ref[...] = 0.25 * nt(dlow, i3) + tn(klow, dp)
        dk_ref[...] += nt(dp, z)

    dz, dk = dz_ref[...], dk_ref[...]
    sums = jnp.sum(kernel, axis=0, keepdims=True)
    lane = iota((1, QUAD), 1) // M
    dzt = jnp.where(mask, dz, 0.0).T
    dsum = jnp.sum(dzt * kernel, axis=0, keepdims=True)
    scale = jnp.zeros((1, QUAD), F32)
    extra = jnp.zeros((1, QUAD), F32)
    for h in range(QUAD // M):
        mine = lane == h
        best = jnp.max(jnp.where(mine, sums, 0.0), axis=1, keepdims=True)
        dscale = jnp.sum(jnp.where(mine, dsum, 0.0), axis=1, keepdims=True)
        is_best = (mine & (sums == best)).astype(F32)
        share = is_best / jnp.sum(is_best, axis=1, keepdims=True)
        scale = jnp.where(mine, 1.0 / best, scale)
        extra = jnp.where(mine, -dscale / (best * best) * share, extra)
    dk = dk + dzt * scale + extra
    inner = jnp.sum(jnp.where(mask, dk * kernel, 0.0), axis=1, keepdims=True)
    g2 = kernel * (dk - inner)
    g2h, g2l = split(g2)
    kb, qb = spread_blocks(km, mask), spread_blocks(qm, mask)
    use = use * 0.125
    return (
        gather_blocks(nn(g2h, kb) + nn(g2l, kb)) * use,
        gather_blocks(tn(g2h, qb) + tn(g2l, qb)) * use,
    )


def conv_quad(
    c, v_ref, vedge_ref, gc_ref, gedge_ref, bounds, start, keep_n, line_ref, gv_ref, gtap_ref,
    vext, gext, band, pairs,
):
    heads = QUAD // M
    tok = v_ref.shape[0]
    at = pl.multiple_of(c * QUAD, QUAD)
    cols = pl.ds(at, QUAD)
    fill_halo(vext, v_ref.at[:, cols], vedge_ref.at[:, cols], tok)
    fill_halo(gext, gc_ref.at[:, cols], gedge_ref.at[:, cols], tok)
    fill_bands(line_ref.at[c], band)
    low64 = iota((128, 128), 1) < M
    pairs[...] = jnp.zeros_like(pairs)
    for sub in range(tok // 128):
        place = start + sub * 128
        same = docs_at(place + iota((128, 1), 0), bounds, LEN) == docs_at(
            place - 64 + iota((1, 256), 1), bounds, LEN
        )
        low = same.astype(BF)
        keep = iota((128, 1), 0) < keep_n - sub * 128
        rows = slice(sub * 128, sub * 128 + 128)
        for pair in range(heads // 2):
            lanes = slice(pair * 128, pair * 128 + 128)
            back = banded(band, gext[sub * 128 : sub * 128 + 256, lanes], low, 2 * pair)
            wide = pl.ds(pl.multiple_of(at + pair * 128, 128), 128)
            mine = gv_ref[rows, wide].astype(F32) + back
            gv_ref[rows, wide] = jnp.where(keep, mine, 0.0).astype(BF)
            g = gc_ref[rows, wide]
            win = vext[sub * 128 : sub * 128 + 256, lanes]
            for h in range(2):
                own = jnp.where(low64 == (h == 0), g, jnp.zeros((), BF))
                pairs[2 * pair + h] += jnp.where(same, nt(own, win), 0.0)
    for h in range(heads):
        tall = pairs[h, 0:8]
        for r in range(8, 128, 8):
            tall = tall + pltpu.roll(pairs[h, r : r + 8], 256 - r, 1)
        line = tall[0:1]
        for r in range(1, 8):
            line = line + pltpu.roll(tall[r : r + 1], 256 - r, 1)
        gtap_ref[pl.ds(c * heads + h, 1), :] = line


def att_quad(c, k_ref, v_ref, e_ref, gm_ref, gt_ref, marks_ref, gv_ref, qm_ref):
    n, lm = marks_ref.shape[0], marks_ref.shape[1] // 2
    heads = QUAD // M
    cols = slice(c * QUAD, (c + 1) * QUAD)
    mask = block_mask()
    qm = spread_blocks(
        jnp.concatenate([marks_ref[i, 0:lm, cols] for i in range(n)], axis=0), mask
    )
    gm = spread_blocks(gm_ref[:, cols], mask)
    lane = iota((M, 128), 1)
    gts = []
    for h in range(heads):
        pick = jnp.where(lane == c * heads + h, gt_ref[...], 0.0)
        gts.append(jnp.sum(pick, axis=1, keepdims=True))
    gt = jnp.concatenate(gts, axis=0)
    e = e_ref[cols, :]
    g3 = (e.astype(F32) * (nt(gm, v_ref[:, cols]) + gt)).astype(BF)
    qm_ref[:, cols] = gather_blocks(nn(g3, k_ref[:, cols])) * 0.125
    k_ref[:, cols] = (tn(g3, qm) * 0.125).astype(BF)
    gv_ref[:, cols] = tn(e, gm).astype(BF)


def back_kernel(*refs, n, dp_n, fast):
    (
        pad_ref, doc_ref, line_ref, marks, cm_ref, lv_ref, inv_ref, gst_ref, k2_ref, vedge, acc_ref,
        vec_ref, rstd_ref,
        k1_any, q_any, k_any, v_any, e_any, save_any,
        gh2t_any, gh2t_got, nlt_any, nlt_got, act0, act_got, du0, du_got, du1,
        hat_any, gh2_any, ctx0, ctx_got, xt_any, xt_got,
        wq0, wq1, wk0, wk1, wv0, wv1, wu0, wu1, wo0, wo1, *rest,
    ) = refs
    gin_own, gin_got, gh1t_own, gh1t_got, small_out, *rest = rest
    outs, rest = (rest[:6], rest[6:]) if fast else (rest[:24], rest[24:])
    (
        k1, gc, q, k, v, e, save, lhs, rhs, wu, wo, dus, gh1, gh1t, gv, far, res,
        gedge, mix, mixes, gm, gt, gkm, gqm, both, got, acc, small, smalls, small_got, rests, gtap,
        vext, gext, band, pairs, dz_s, dk_s,
        loads, stream, rows_in, turns, ship, send, recv, *rest,
    ) = rest
    idx = places()
    me, mate = idx[1], 1 - idx[0]
    tok, d = q.shape
    half = d // 2
    lm = tok // M
    quads = d // QUAD
    sizes = {"seq": n, "mp": 2}
    if fast:
        sizes["dp"] = dp_n
    ready = greet(sizes)
    per = 10 if fast else 2
    sums = [Sum(idx, turn, rest[per * g : per * g + per]) for g, turn in enumerate(GROUPS)]
    down, up, out_w, val_w, query_w, key_w = sums

    names = {}

    def fetch(name, src, dst):
        names[name] = pltpu.make_async_copy(src, dst, loads.at[len(names)])
        names[name].start()

    def fetched(*which):
        for w in which:
            names[w].wait()

    width = rhs.shape[3]
    blocks = act0.shape[1] // width
    work = [(g, j) for g in range(2) for j in range(blocks)]

    def block(i):
        g, j = work[i]
        cols = pl.ds(j * width, width)
        srcs = (act0, act_got) if g == 0 else (du0, du_got)
        return [
            pltpu.make_async_copy(src.at[:, cols], rhs.at[i % 2, t], stream.at[i % 2, t])
            for t, src in enumerate(srcs)
        ]

    fetch("gh2t", gh2t_any, lhs.at[0])
    for c in block(0):
        c.start()
    fetch("gh2t_got", gh2t_got, lhs.at[1])
    sent = []

    def tell(src, dst, to, axis="seq"):
        c = remote(src, dst, send.at[len(sent)], recv.at[len(sent)], axis, to)
        c.start()
        sent.append(c)
        return c

    peers = [lax.rem(me + p, n) for p in range(1, n)]

    def products(g, left, right, meanwhile):
        for j in range(blocks):
            i = g * blocks + j
            if j + 1 < blocks:
                for c in block(i + 1):
                    c.start()
            if j < len(meanwhile):
                meanwhile[j]()
            for c in block(i):
                c.wait()
            acc_w = nn(left, rhs[i % 2, 0]) + nn(right, rhs[i % 2, 1])
            part, at = j // (blocks // 2), (j % (blocks // 2)) * width
            sums[g].store(part, slice(at, at + width), acc_w.astype(BF))
            if (j + 1) % (blocks // 2) == 0:
                if g == 0 and part == 0:
                    ready()
                sums[g].step0(part)

    def more(*items):
        def go():
            for item in items:
                fetch(*item)

        return go

    fetched("gh2t", "gh2t_got")
    products(
        0,
        lhs[0],
        lhs[1],
        [
            more(("wu0", wu0, wu.at[0])),
            more(("wu1", wu1, wu.at[1])),
            more(("hat", hat_any, k)),
            more(("gh2", gh2_any, v)),
            more(("wo0", wo0, wo.at[0]), ("wo1", wo1, wo.at[1])),
        ],
    )

    rows = dus.shape[2]
    steps = tok // rows

    def du_rows(i):
        at = pl.ds(i * rows, rows)
        return [
            pltpu.make_async_copy(src.at[at], dus.at[i % 2, t], rows_in.at[i % 2, t])
            for t, src in enumerate((du0, du1))
        ]

    def turn(i):
        at = pl.ds(i * rows, rows)
        src = gh1t.at[i % 2]
        return (
            pltpu.make_async_copy(src, gh1t_own.at[:, at], turns.at[0, i]),
            remote(src, gh1t_got.at[:, at], turns.at[1, i], turns.at[2, i], "mp", mate),
        )

    for c in du_rows(0):
        c.start()
    fetched("wu0", "wu1", "wo0", "wo1", "hat", "gh2")
    acc[...] = acc_ref[...]
    turned = [turn(i) for i in range(steps)]
    shape = (dp_n if fast else 0, n, d // (n * dp_n))
    extra = [
        (("k1", k1_any, k1), ("q", q_any, q)),
        (("nlt", nlt_any, lhs.at[2]),),
        (("nlt_got", nlt_got, lhs.at[3]),),
    ]
    for i in range(steps):
        if i + 1 < steps:
            for c in du_rows(i + 1):
                c.start()
        if i < len(extra):
            more(*extra[i])()
        if i == steps - 1:
            for c in block(blocks):
                c.start()
        for c in du_rows(i):
            c.wait()
        at = slice(i * rows, (i + 1) * rows)
        gn = v[at].astype(F32) + nt(dus[i % 2, 0], wu[0]) + nt(dus[i % 2, 1], wu[1])
        hat = k[at].astype(F32)
        acc[0:1, :] += jnp.sum(gn * hat, axis=0, keepdims=True)
        acc[1:2, :] += jnp.sum(gn, axis=0, keepdims=True)
        low = norm_back(gn * vec_ref[...].reshape(1, d), hat, rstd_ref[at, 0:1]).astype(BF)
        gh1[at] = low
        if i >= 2:
            turned[i - 2][0].wait()
            turned[i - 2][1].wait_send()
        store_chunks(gh1t.at[i % 2], low.T, idx, shape)
        turned[i][0].start()
        turned[i][1].start()
        gc[at, :half] = nt(low, wo[0]).astype(BF)
        gc[at, half:] = nt(low, wo[1]).astype(BF)
    fetch("v", v_any, v)
    fetch("k", k_any, k)

    swaps_edge = [
        tell(gc.at[pl.ds(tok - 16, 16)], gedge.at[pl.ds(0, 16)], peers[0]),
        tell(gc.at[pl.ds(0, 16)], gedge.at[pl.ds(16, 16)], peers[n - 2]),
    ]
    fetched("k1", "q")
    for c in range(quads):
        first_quad(c, q, k1, gc, cm_ref, marks, q, mix, gkm)
    swaps = [tell(mix, mixes.at[me], to) for to in peers]
    mixes[me] = mix[...]
    for i in range(max(steps - 2, 0), steps):
        turned[i][0].wait()
        turned[i][1].wait_send()
    for i in range(steps):
        turned[i][1].wait_recv()

    fetched("nlt", "nlt_got")
    products(
        1,
        lhs[2],
        lhs[3],
        [
            more(("e", e_any, e)),
            more(("save", save_any, save), ("gh1t", gh1t_own, lhs.at[0]), ("gh1t_got", gh1t_got, lhs.at[1])),
            down.step1,
            more(*[("w%d" % i, w, wu.at[0, :, pl.ds(i * half, half)]) for i, w in enumerate((wq0, wq1))]),
            more(*[("w%d" % (2 + i), w, wu.at[0, :, pl.ds((2 + i) * half, half)]) for i, w in enumerate((wk0, wk1))]),
            more(*[("w%d" % (4 + i), w, wu.at[1, :, pl.ds(i * half, half)]) for i, w in enumerate((wv0, wv1))]),
        ],
    )
    for t, src in enumerate((ctx0, ctx_got)):
        fetch("ctx%d" % t, src.at[:, pl.ds(0, width)], rhs.at[0, t])
        fetch("ctx%d" % (2 + t), src.at[:, pl.ds(width, half - width)], rhs.at[1, t, :, pl.ds(0, half - width)])
    fetch("xt", xt_any, lhs.at[2])
    fetch("xt_got", xt_got, lhs.at[3])
    down.step2()

    for c in swaps:
        c.wait()
    middle(mixes, lv_ref, inv_ref, gst_ref, gm, gt)
    fetched("k", "v", "e", "save")
    for c in range(quads):
        att_quad(c, k, v, e, gm, gt, marks, gv, gqm)
    down.step3()
    sel = jnp.minimum(me, quads - 1)
    cols = pl.ds(pl.multiple_of(sel * QUAD, QUAD), QUAD)
    use = (me < quads).astype(F32)
    qm_sel = jnp.concatenate([marks[i, 0:lm, cols] for i in range(n)], axis=0)
    km_sel = jnp.concatenate([marks[i, lm : 2 * lm, cols] for i in range(n)], axis=0)
    two_q, two_k = pinv_back(mixes, lv_ref, k2_ref, save, dz_s, dk_s, qm_sel, km_sel, cols, use)
    gqm[:, cols] += two_q
    gkm[:, cols] += two_k
    for i in range(n):
        part = slice(i * lm, (i + 1) * lm)
        both[i, :lm] = gqm[part].astype(BF)
        both[i, lm:] = gkm[part].astype(BF)
    swaps = [tell(both.at[to], got.at[me], to) for to in peers]
    got[me] = both[me]
    up.step1()

    valid = pad_ref[pl.ds(idx[0], 1), :].astype(F32)
    keep_n = jnp.sum(valid, axis=1, keepdims=True).astype(jnp.int32) - me * tok
    bounds = doc_bounds(doc_ref, idx)
    for c in swaps_edge:
        c.wait()

    @pl.loop(0, quads)
    def _(c):
        conv_quad(
            c, v, vedge, gc, gedge, bounds, me * tok, keep_n, line_ref, gv, gtap,
            vext, gext, band, pairs,
        )

    swap_v = tell(gv.at[:, pl.ds(half, half)], far.at[0], mate, "mp")
    pieces = d // 128
    for r in range(4):
        for b in range(pieces):
            at = r * pieces + b
            small[at : at + 1, :] = acc[r : r + 1, b * 128 : (b + 1) * 128]
    lines = 4 * pieces
    heads = gtap.shape[0]
    small[lines : lines + 2 * heads, :] = jnp.concatenate([gtap[:, :128], gtap[:, 128:]], axis=0)
    squares = jnp.sum(acc[...], axis=1, keepdims=True)
    small[lines + 2 * heads :, :] = jnp.broadcast_to(squares, (8, 128))
    swaps_small = [tell(small, smalls.at[me], to) for to in peers]
    smalls[me] = small[...]
    fetched("gh1t", "gh1t_got", "ctx0", "ctx1", "ctx2", "ctx3")
    acc_w = nn(lhs[0], rhs[0, 0]) + nn(lhs[1], rhs[0, 1])
    out_w.store(0, slice(0, width), acc_w.astype(BF))
    out_w.step0(0)
    acc_w = nn(lhs[0], rhs[1, 0, :, : half - width]) + nn(lhs[1], rhs[1, 1, :, : half - width])
    out_w.store(1, slice(0, half - width), acc_w.astype(BF))
    out_w.step0(1)

    for c in swaps:
        c.wait()
    spread(q, k, got, keep_n)
    swaps = [
        tell(q.at[:, pl.ds(half, half)], far.at[1], mate, "mp"),
        tell(k.at[:, pl.ds(half, half)], far.at[2], mate, "mp"),
    ]
    up.step2()
    fetched("xt", "xt_got")
    acc_w = nn(lhs[2], gv[:, :half])
    swap_v.wait()
    val_w.store_all((acc_w + nn(lhs[3], far[0])).astype(BF))
    for i, src in ((0, q), (1, k)):
        acc_w = nn(lhs[2], src[:, :half])
        swaps[i].wait()
        (query_w, key_w)[i].store_all((acc_w + nn(lhs[3], far[1 + i])).astype(BF))
        if i == 0:
            out_w.step1()
    up.step3()
    for c in swaps_small:
        c.wait()
    total = smalls[0]
    for i in range(1, n):
        total = total + smalls[i]
    small[...] = total
    swap_small = tell(small, small_got, mate, "mp")

    fetched(*["w%d" % i for i in range(6)])
    tall = res.shape[0]
    own = pl.multiple_of(idx[0] * half, half)
    other = pl.multiple_of(mate * half, half)
    swap_gin = []
    keep_gin = []

    def outs_early():
        if fast:
            outs[0][...] = down.finish()

    for i in range(tok // tall):
        at = slice(i * tall, (i + 1) * tall)
        lhs_i = jnp.concatenate([q[at, :], k[at, :]], axis=1)
        res[...] = gh1[at].astype(F32) + nt(lhs_i, wu[0]) + nt(gv[at, :], wu[1, :, :d])
        mine = dus.at[i // 2, i % 2]
        mine[:, :half] = res[:, pl.ds(own, half)].astype(BF)
        mine[:, half:d] = res[:, pl.ds(other, half)].astype(BF)
        part = pl.ds(i * tall, tall)
        swap_gin.append(tell(mine.at[:, pl.ds(half, half)], gin_got.at[part], mate, "mp"))
        c = pltpu.make_async_copy(mine.at[:, pl.ds(0, half)], gin_own.at[part], ship.at[i])
        c.start()
        keep_gin.append(c)
        if i == 0:
            val_w.step1()
        if i == 1:
            out_w.step2()
            query_w.step1()
            outs_early()
        if i == 2:
            val_w.step2()
            key_w.step1()
    swap_small.wait()
    mine = small[...]
    theirs = small_got[...]
    few = heads // 2
    taps_a = mine[lines : lines + 2 * heads]
    taps_b = theirs[lines : lines + 2 * heads]
    rests[0, :lines] = mine[:lines] + theirs[:lines]
    rests[0, lines : lines + few] = taps_a[:few] + taps_b[few:heads]
    rests[0, lines + few : lines + heads] = taps_a[heads : heads + few] + taps_b[heads + few :]
    for row, part in ((idx[0], mine), (mate, theirs)):
        real = jnp.sum(pad_ref[pl.ds(row, 1), :].astype(F32), axis=1, keepdims=True)
        at = pl.multiple_of(8 * row, 8)
        small_out[pl.ds(at, 8), :] = jnp.sqrt(part[lines + 2 * heads :] / (real * d) + 1e-06)
    if fast:
        norms = [tell(rests.at[0], rests.at[p], idx[2] ^ p, "dp") for p in range(1, dp_n)]
        query_w.step2()
        out_w.step3()
        outs[1][...] = up.finish()
        key_w.step2()
        val_w.step3()
        query_w.step3()
        key_w.step3()
        for c in norms:
            c.wait()
        total = rests[0]
        for p in range(1, dp_n):
            total = total + rests[p]
        small_out[16:] = total
        for i in range(2, 6):
            outs[i][...] = sums[i].finish()
    else:
        small_out[16:] = rests[0]
        for g in range(6):
            for i in range(4):
                c = pltpu.make_async_copy(
                    sums[g].slots[i // 2].at[i % 2], outs[4 * g + i], ship.at[4]
                )
                c.start()
                c.wait()
    for c in swap_gin + keep_gin:
        c.wait()


def spread(gq_ref, gk_ref, got_ref, keep_n):
    n, lm = got_ref.shape[0], got_ref.shape[1] // 2
    got = got_ref[0].astype(F32)
    for i in range(1, n):
        got = got + got_ref[i].astype(F32)
    for j in range(lm):
        rows = slice(j * M, (j + 1) * M)
        keep = (iota((M, 1), 0) < keep_n - j * M).astype(F32)
        share = keep / jnp.maximum(jnp.sum(keep, axis=0, keepdims=True), 1.0)
        for at, ref in ((0, gq_ref), (lm, gk_ref)):
            ref[rows] = (ref[rows].astype(F32) + got[at + j : at + j + 1] * share).astype(BF)


def back(n, dp_n, fast, near, far):
    lines, marks = near[2], near[3]
    tok, d = far[1].shape
    f2 = far[10].shape[1]
    half = d // 2
    lm = tok // M
    heads = lines.shape[1]
    near = list(near)
    near[2] = lines[1].reshape(d // QUAD, QUAD // M, lines.shape[2])
    flat, turned, thin = (tok, d), (d, tok), (tok, half)
    pieces = 4 * (d // 128)
    small = (pieces + 2 * heads + 8, 128)
    vm = pl.BlockSpec(memory_space=pltpu.VMEM)
    sems = pltpu.SemaphoreType.DMA
    out_shape = [sds(thin, BF)] * 2 + [sds(turned, BF)] * 2 + [sds((pieces + heads + 16, 128), F32)]
    out_specs = [ANY] * 4 + [vm]
    thirds = (QUAD, half - QUAD)
    tail = []
    for widths in [(f2 // 2, f2 // 2)] * 2 + [thirds] * 4:
        if fast:
            out_shape.append(sds((d // (n * dp_n), sum(widths)), F32))
            out_specs.append(vm)
        else:
            for w in widths:
                out_shape += [sds((half, w), BF)] * 2
            out_specs += [ANY] * 4
        tail += Sum.shapes(d, widths, fast)
    count = 40
    scratch = [
        pltpu.VMEM(turned, BF),
        *[pltpu.VMEM(flat, BF)] * 4,
        pltpu.VMEM(turned, BF),
        pltpu.VMEM((ITERS, 4, M, QUAD), BF),
        pltpu.VMEM((4,) + turned, BF),
        pltpu.VMEM((2, 2, tok, QUAD), BF),
        pltpu.VMEM((2, d, f2), BF),
        pltpu.VMEM((2, half, d), BF),
        pltpu.VMEM((2, 2, 256, f2), BF),
        pltpu.VMEM(flat, BF),
        pltpu.VMEM((2, d, 256), BF),
        pltpu.VMEM(flat, BF),
        pltpu.VMEM((3,) + thin, BF),
        pltpu.VMEM((256, d), F32),
        pltpu.VMEM((32, d), BF),
        pltpu.VMEM((M, d), BF),
        pltpu.VMEM((n, M, d), BF),
        pltpu.VMEM((M, d), BF),
        pltpu.VMEM((M, 128), F32),
        pltpu.VMEM((M, d), F32),
        pltpu.VMEM((M, d), F32),
        pltpu.VMEM((n, 2 * lm, d), BF),
        pltpu.VMEM((n, 2 * lm, d), BF),
        pltpu.VMEM((8, d), F32),
        pltpu.VMEM(small, F32),
        pltpu.VMEM((n,) + small, F32),
        pltpu.VMEM(small, F32),
        pltpu.VMEM((dp_n if fast else 1, pieces + heads, 128), F32),
        pltpu.VMEM((heads, 256), F32),
        pltpu.VMEM((tok + 128, QUAD), BF),
        pltpu.VMEM((tok + 128, QUAD), BF),
        pltpu.VMEM((QUAD // M, 128, 256), BF),
        pltpu.VMEM((QUAD // M, 128, 256), F32),
        pltpu.VMEM((QUAD, QUAD), F32),
        pltpu.VMEM((QUAD, QUAD), F32),
        sems((32,)),
        sems((2, 2)),
        sems((2, 2)),
        sems((3, tok // 256)),
        sems((5,)),
        sems((count,)),
        sems((count,)),
        *tail,
    ]
    return pl.pallas_call(
        functools.partial(back_kernel, n=n, dp_n=dp_n, fast=fast),
        in_specs=[vm] * len(near) + [ANY] * len(far),
        out_specs=out_specs,
        out_shape=out_shape,
        scratch_shapes=scratch,
        compiler_params=params(62, collective_id=3, has_side_effects=True),
        cost_estimate=pl.CostEstimate(
            flops=14 * tok * d * f2, bytes_accessed=60 * tok * d, transcendentals=0
        ),
        name="back",
    )(*near, *far)


def finish_kernel(idx, out_own, out_got, gin_own, gin_got, *refs):
    n = (len(refs) - 2) // 2
    sums, (outs, gins), placed = refs[:n], refs[n : n + 2], refs[n + 2 :]

    @pl.when(pl.program_id(0) == 0)
    def _():
        outs[0] = out_own[...]
        gins[0] = gin_own[...]

    @pl.when(pl.program_id(0) == 1)
    def _():
        outs[0] = out_got[...]
        gins[0] = gin_got[...]

    @pl.when((pl.program_id(0) == 0) & (pl.program_id(1) == 0))
    def _():
        for a, b in zip(sums, placed):
            b[...] = a[...]


def finish(idx, own, got, gin_own, gin_got, sums):
    tok, d = own.shape
    half = d // 2
    steps = 2
    rows = tok // steps
    mine = lambda j, i, s: (jnp.where(j == 0, i, steps - 1), 0)
    theirs = lambda j, i, s: (jnp.where(j == 0, 0, i), 0)
    there = lambda j, i, s: (s[0] ^ j, i, 0)
    specs = [whole(a.shape) for a in sums]
    return call(
        finish_kernel,
        idx,
        [own, got, gin_own, gin_got, *sums],
        [
            pl.BlockSpec((rows, d), mine),
            pl.BlockSpec((rows, d), theirs),
            pl.BlockSpec((rows, half), mine),
            pl.BlockSpec((rows, half), theirs),
        ]
        + specs,
        [pl.BlockSpec((1, rows, d), there), pl.BlockSpec((1, rows, half), there)] + specs,
        [sds((2, tok, d), BF), sds((2, tok, half), BF)] + [sds(a.shape, F32) for a in sums],
        (2, steps),
        "finish",
        moved=12 * tok * d,
    )


def shards(
    inputs,
    cotangent,
    padding,
    documents,
    w_query,
    w_key,
    w_value,
    w_out,
    w_up,
    w_down,
    conv_taps,
    gain_attn,
    shift_attn,
    gain_ffn,
    shift_ffn,
):
    row_count, tok, d = inputs.shape
    heads = conv_taps.shape[0]
    seq_n, dp_n = lax.axis_size("seq"), lax.axis_size("dp")
    mp = lax.axis_index("mp")
    chunk = d // (seq_n * dp_n)
    fast = seq_n == 4 and dp_n == 4 and chunk % 16 == 0
    shape = (dp_n if fast else 0, seq_n, chunk)
    own_w = (w_query, w_key, w_value)
    (
        q, k, v, xt, k1, e, save, *got_w, xt_got, wo_got, wu_got, wd_got,
        marks, vedge, cm, lv, gst, inv, k2, lines,
    ) = attend(
        seq_n, inputs, padding, own_w, conv_taps, (w_out, w_up, w_down), shape
    )
    wq, wk, wv = zip(own_w, got_w)
    wo, wu, wd = (w_out, wo_got), (w_up, wu_got), (w_down, wd_got)
    vecs = [gain_attn, shift_attn, gain_ffn, shift_ffn]
    (
        ctx0, act0, du0, hat, gh2, rstd, acc, out_own, nlt, gh2t, du1,
        out_got, nlt_got, gh2t_got, du_got, ctx_got, act_got,
    ) = core(inputs, cotangent, padding, documents, v, vedge, k1, cm, lines, wo, wu, wd, vecs, shape)
    near = [padding, documents, lines, marks, cm, lv, inv, gst, k2, vedge, acc, gain_attn, rstd]
    far = [
        k1, q, k, v, e, save, gh2t, gh2t_got, nlt, nlt_got, act0, act_got, du0, du_got, du1,
        hat, gh2, ctx0, ctx_got, xt, xt_got, *wq, *wk, *wv, *wu, *wo,
    ]
    gin0, gin_got, _, _, small, *sums = back(seq_n, dp_n, fast, near, far)
    if not fast:
        sums = [sum_any(joined(t, *sums[4 * g : 4 * g + 4])) for g, t in enumerate(GROUPS)]
    outputs, grad_inputs, sum_down, sum_up, sum_o, sum_v, sum_q, sum_k = finish(
        mp.astype(jnp.int32).reshape(1), out_own, out_got, gin0, gin_got, sums
    )
    n = 4 * (d // 128)
    rest = small[16:]
    if not fast:
        rest = lax.psum(rest, "dp")
    norms = rest[:n].reshape(4, d)
    width = conv_taps.shape[1]
    tap_total = jnp.concatenate([rest[n : n + heads], rest[n + heads :]], axis=1)
    tap_total = tap_total[:, 64 - width // 2 : 64 - width // 2 + width]
    row_rms = small[:16].reshape(2, 8, 128)[:, 4:7, 0]
    return (
        outputs,
        grad_inputs,
        sum_q,
        sum_k,
        sum_v,
        sum_o.T,
        sum_up,
        sum_down.T,
        tap_total,
        norms[0],
        norms[1],
        norms[2],
        norms[3],
        row_rms,
    )


def solution(mesh):
    return jax.shard_map(
        shards,
        mesh=mesh,
        in_specs=(
            P("dp", "seq", None),
            P("dp", "seq", None),
            P("dp", None),
            P("dp", None),
            P(None, "mp"),
            P(None, "mp"),
            P(None, "mp"),
            P("mp", None),
            P(None, "mp"),
            P("mp", None),
            P("mp", None),
            P(),
            P(),
            P(),
            P(),
        ),
        out_specs=(
            P("dp", "seq", None),
            P("dp", "seq", "mp"),
            P(("dp", "seq"), "mp"),
            P(("dp", "seq"), "mp"),
            P(("dp", "seq"), "mp"),
            P("mp", ("dp", "seq")),
            P(("dp", "seq"), "mp"),
            P("mp", ("dp", "seq")),
            P("mp", None),
            P(),
            P(),
            P(),
            P(),
            P("dp", None),
        ),
        check_vma=False,
    )
```
